256 devices in a mesh: grp: 16 (over z, core), loc: 16 (over x, y).
Axes of the slice: x: 4, y: 4, z: 8, core: 2. Of those that a mesh axis runs over, the one named last changes fastest.
Arguments:
- right_side: float32 [256, 512, 256], P('grp', 'loc'), may hold values from -6 to 6
- phase: int32 [256, 512, 256], P('grp', 'loc'), may hold values 0 or 1
Outputs:
- fine_residual: float32 [256, 512, 256], P('grp', 'loc')
- coarse_residual: float32 [32, 64, 32], P('grp')
The draws below stay inside these ranges and needn't reach their ends.
All inputs are finite; a program needn't handle non-finite values. No bound on the sum of `phase` on one device may be relied on, other than what follows from the above.
Results may differ from the reference program's by a relative error of at most 0.000027.
Values sent between devices are 32-bit elements; how exact they have to be, the bound alone decides.
A program may use at most 64 MiB of HBM per device.

```python
import jax
import jax.numpy as jnp

NZ = 256
COARSE_SWEEPS = 4
NX = 256
NY = 512


def with_ends(result, rng, low, top_value):
    longest = result.shape.index(max(result.shape))
    spots = []
    for shift in (0, 1):
        where = [jax.random.randint(jax.random.fold_in(rng, axis), (), 0, length) for axis, length in enumerate(result.shape)]
        where[longest] = (where[longest] + shift) % result.shape[longest]
        spots.append(tuple(where))
    return result.at[spots[0]].set(low).at[spots[1]].set(top_value)


def level_of(own_key, shape, pieces, low, largest):
    level = 1.0
    for position, shards_of in pieces:
        draws = jax.random.uniform(jax.random.fold_in(jax.random.fold_in(own_key, 6), position), (shards_of,), jnp.float32, low / len(pieces), largest / len(pieces))
        level = level * jnp.repeat(jnp.exp(draws), shape[position] // shards_of).reshape((-1,) + (1,) * (len(shape) - 1 - position))
    return level


def normal_values(rng, extent, deviation, limit, cuts=(), kind=jnp.bfloat16):
    loudness = level_of(rng, extent, cuts, -0.22, 0.18) if cuts else 1.0
    array = jax.random.normal(rng, extent, jnp.float32) * deviation * loudness
    return jnp.minimum(jnp.maximum(array, -limit), limit).astype(kind)


def setup_inputs(seed: int = 0) -> dict:
    streams_of = jax.random.split(jax.random.key(seed), 3)
    right_side = normal_values(streams_of[0], (NX, NY, NZ), 1.0, 6.0, ((0, 16), (1, 16)), jnp.float32)
    phase = with_ends((jax.random.randint(streams_of[1], (NX, NY, NZ), 0, 3) < 1).astype(jnp.int32), jax.random.fold_in(streams_of[1], 1), 0, 1)
    return {"right_side": right_side, "phase": phase}


RELAXATION = 0.6
LIQUID = 1.0
GASEOUS = 1000.0


def narrow(values, direction, lower_bound, upper_bound):
    selector = [slice(None), slice(None), slice(None)]
    selector[direction] = slice(lower_bound, values.shape[direction] + upper_bound)
    return values[tuple(selector)]


def pair_sum(values, direction):
    return narrow(values, direction, 0, -1) + narrow(values, direction, 1, 0)


def corner_sum(values):
    return pair_sum(pair_sum(pair_sum(values, 0), 1), 2)


def operate(iterate, conduct, weight, spacing):
    cell_values = conduct[:-1, :-1, :-1]
    center = corner_sum(cell_values * corner_sum(iterate))
    edge_terms = jnp.zeros_like(weight)
    for direction in range(3):
        across = [item for item in range(3) if item != direction]
        edge_weight = pair_sum(pair_sum(conduct, across[0]), across[1])
        shifted = narrow(narrow(iterate, across[0], 1, 0), across[1], 1, 0)
        product_term = narrow(edge_weight, direction, 1, -1) * narrow(shifted, direction, 2, 0) + narrow(edge_weight, direction, 0, -2) * narrow(shifted, direction, 0, -2)
        edge_terms = edge_terms + narrow(narrow(product_term, across[0], 0, -1), across[1], 0, -1)
    middle = iterate[1:-1, 1:-1, 1:-1]
    return (spacing / 12.0) * (5.0 * weight * middle + edge_terms - center)


def stride_take(values, direction, lower_bound, length):
    selector = [slice(None), slice(None), slice(None)]
    selector[direction] = slice(lower_bound, lower_bound + 2 * length - 1, 2)
    return values[tuple(selector)]


def restrict_along(values, direction):
    length = (values.shape[direction] - 1) // 2
    return 0.5 * stride_take(values, direction, 0, length) + stride_take(values, direction, 1, length) + 0.5 * stride_take(values, direction, 2, length)


def restrict(residual):
    for direction in (2, 1, 0):
        widths = [(0, 0), (0, 0), (0, 0)]
        widths[direction] = (1, 0)
        residual = restrict_along(jnp.pad(residual, widths), direction)
    return residual


def coarsen(conduct):
    halves = conduct[0::2] + conduct[1::2]
    halves = halves[:, 0::2] + halves[:, 1::2]
    halves = halves[:, :, 0::2] + halves[:, :, 1::2]
    return 0.125 * halves


def level_smooth(source, conduct, spacing, sweeps):
    padded = jnp.pad(conduct, 1)
    weight = corner_sum(padded[:-1, :-1, :-1])
    diagonal = (spacing / 3.0) * weight
    iterate = RELAXATION * source / diagonal
    for repeat in range(sweeps - 1):
        applied = operate(jnp.pad(iterate, 1), padded, weight, spacing)
        iterate = iterate + RELAXATION * (source - applied) / diagonal
    return source - operate(jnp.pad(iterate, 1), padded, weight, spacing)


def reference(right_side, phase):
    conduct = jnp.where(phase == 1, GASEOUS, LIQUID).astype(jnp.float32)
    source = right_side
    spacing = 1.0
    fine_residual = source
    for level_index in range(3):
        residual = level_smooth(source, conduct, spacing, 2)
        if level_index == 0:
            fine_residual = residual
        source = restrict(residual)
        conduct = coarsen(conduct)
        spacing = spacing * 2.0
    coarse_residual = level_smooth(source, conduct, spacing, COARSE_SWEEPS)
    return fine_residual, coarse_residual
```

```python
import functools

import jax
import jax.numpy as jnp
from jax import lax
from jax.experimental import pallas as pl
from jax.experimental.pallas import tpu as pltpu
from jax.sharding import PartitionSpec as P

MESH = pl.DeviceIdType.MESH
NG, NL = 16, 16
COARSE_SWEEPS = 4
F32 = jnp.float32
BF16 = jnp.bfloat16
WHOLE = ((256, 512, 256), (128, 256, 128), (64, 128, 64), (32, 64, 32))
BLOCK = ((16, 32, 256), (8, 16, 128), (4, 8, 64), (2, 64, 32))
LOW = (4, 4, 12, 5)
PLANES = (22, 14, 28, 11)
ROWS = (40, 24, 16, 72)
LANES = (256, 128, 128, 128)

NEAR = [(a, b) for a in (-1, 0, 1) for b in (-1, 0, 1) if (a, b) != (0, 0)]
WIDE = [(a, b) for a in range(-3, 4) for b in (-1, 0, 1) if (a, b) != (0, 0)]
ALONG = [(0, k) for k in range(1, NL)]
GREET = [(a, b % NL) for a, b in WIDE] + [(0, k) for k in range(2, NL - 1)]


def lane_ids(shape):
    return lax.broadcasted_iota(jnp.int32, shape, len(shape) - 1)


def row_ids(shape):
    return lax.broadcasted_iota(jnp.int32, shape, len(shape) - 2)


def split_dot(values, matrix):
    high = values.astype(BF16)
    rest = values - high.astype(F32)
    mid = rest.astype(BF16)
    low = (rest - mid.astype(F32)).astype(BF16)
    dot = functools.partial(jnp.dot, preferred_element_type=F32)
    return dot(high, matrix) + (dot(mid, matrix) + dot(low, matrix))


class Level:
    def __init__(self, index, g, l, refs):
        self.index = index
        self.F, self.C, self.U, self.V, self.Ei, self.Ej, self.El, self.K5, self.W = refs
        self.n = BLOCK[index]
        self.low = LOW[index]
        self.rows, self.lanes = ROWS[index], LANES[index]
        self.g, self.l = g, l

    def up(self, x, axis):
        return pltpu.roll(x, x.shape[axis] - 1, axis)

    def down(self, x, axis):
        return pltpu.roll(x, 1, axis)

    def lane_up(self, x):
        y = self.up(x, x.ndim - 1)
        return jnp.where(lane_ids(y.shape) == self.n[2] - 1, 0.0, y) if self.n[2] == self.lanes else y

    def lane_down(self, x):
        y = self.down(x, x.ndim - 1)
        return jnp.where(lane_ids(y.shape) == 0, 0.0, y) if self.n[2] == self.lanes else y

    def row_up(self, x):
        return self.up(x, x.ndim - 2)

    def row_down(self, x):
        return self.down(x, x.ndim - 2)

    def row_valid(self, shape):
        r = row_ids(shape)
        if self.index == 3:
            ok = r < self.n[1]
        else:
            j = jnp.where(r < self.n[1] + 4, r, r - self.rows) + self.l * self.n[1]
            ok = (j >= 0) & (j < WHOLE[self.index][1])
        if self.n[2] < self.lanes:
            ok = ok & (lane_ids(shape) < self.n[2])
        return jnp.where(ok, 1.0, 0.0).astype(F32)

    def plane_valid(self, i):
        p = self.g * self.n[0] + (i - self.low)
        return jnp.where((p >= 0) & (p < WHOLE[self.index][0]), 1.0, 0.0).astype(F32)

    def plane_valid_many(self, lo, hi):
        shape = (hi - lo, self.rows, self.lanes)
        p = self.g * self.n[0] + (lo - self.low) + lax.broadcasted_iota(jnp.int32, shape, 0)
        return jnp.where((p >= 0) & (p < WHOLE[self.index][0]), 1.0, 0.0).astype(F32)

    def cells(self, c):
        cl = c + self.lane_down(c)
        cj = c + self.row_down(c)
        cjl = cl + self.row_down(cl)
        return cl, cj, cjl

    def coefficients(self, cells, before, valid):
        cl, cj, cjl = cells
        pl_, pj, pjl = before
        k = cjl + pjl
        el = cj + pj
        if self.n[2] == self.lanes:
            el = jnp.where(lane_ids(el.shape) == self.n[2] - 1, 0.0, el)
        return cjl, cl + pl_, el, 5.0 * k, valid * (0.15 / jnp.maximum(k, 1.0))

    def parts(self, u):
        ul = self.lane_up(u)
        uj = self.row_up(u)
        a = u + ul
        return ul, uj, a + self.row_up(a)

    def combine(self, u, un, up, ul, uj, t, ei, eip, ej, el, k5):
        tj = t + self.row_down(t)
        b = k5 * u + ei * un + eip * up + ej * uj + el * ul - tj
        return b + self.lane_down(el * u - tj) + self.row_down(ej * u)

    def setup_all(self, lo, hi):
        cl, cj, cjl = self.cells(self.C[lo - 1:hi])
        valid = self.row_valid((1, self.rows, self.lanes)) * self.plane_valid_many(lo, hi)
        ei, ej, el, k5, w = self.coefficients(
            (cl[1:], cj[1:], cjl[1:]), (cl[:-1], cj[:-1], cjl[:-1]), valid
        )
        self.Ei[lo - 1:hi] = cjl
        self.Ej[lo:hi] = ej
        self.El[lo:hi] = el
        self.K5[lo:hi] = k5
        self.W[lo:hi] = w

    def apply_all(self, u_ref, lo, hi):
        u = u_ref[lo - 1:hi + 1]
        ul, uj, v = self.parts(u)
        t = self.C[lo - 1:hi] * (v[:-1] + v[1:])
        return self.combine(
            u[1:-1], u[2:], u[:-2], ul[1:-1], uj[1:-1], t[1:] + t[:-1],
            self.Ei[lo:hi], self.Ei[lo - 1:hi - 1], self.Ej[lo:hi], self.El[lo:hi], self.K5[lo:hi],
        )

    def first_all(self, lo, hi):
        self.U[lo:hi] = self.W[lo:hi] * self.F[lo:hi]

    def sweep_all(self, source, target, lo, hi):
        b = self.apply_all(source, lo, hi)
        target[lo:hi] = source[lo:hi] + self.W[lo:hi] * (self.F[lo:hi] - b)

    def residual_all(self, source, lo, hi):
        return self.F[lo:hi] - self.apply_all(source, lo, hi)

    def planes_loop(self, lo, hi, step, carry, unroll):
        whole = (hi - lo) // unroll

        def body(k, c):
            for m in range(unroll):
                c = step(lo + k * unroll + m, c)
            return c

        carry = lax.fori_loop(0, whole, body, carry)
        for i in range(lo + whole * unroll, hi):
            carry = step(i, carry)
        return carry

    def apply_loop(self, u_ref, lo, hi, emit, unroll):
        _, _, v0 = self.parts(u_ref[lo - 1])
        ul, uj, v = self.parts(u_ref[lo])
        t = self.C[lo - 1] * (v0 + v)

        def step(i, carry):
            ul, uj, v, t = carry
            u = u_ref[i]
            un = u_ref[i + 1]
            uln, ujn, vn = self.parts(un)
            tn = self.C[i] * (v + vn)
            b = self.combine(
                u, un, u_ref[i - 1], ul, uj, t + tn,
                self.Ei[i], self.Ei[i - 1], self.Ej[i], self.El[i], self.K5[i],
            )
            emit(i, u, b)
            return uln, ujn, vn, tn

        self.planes_loop(lo, hi, step, (ul, uj, v, t), unroll)


def kernel(*refs):
    (rhs, phase, r0_mat, r1_mat, r2_mat, p0_mat, p1_mat, fine_out, coarse_out) = refs[:9]
    refs = refs[9:]
    windows = [refs[9 * k:9 * k + 9] for k in range(4)]
    (
        ph, upk, dpk, rxl0, rxh0, rs, s0, out, ct1, n1, h0,
        rxl1, rxh1, crl1, crh1, c1w, s1, ct2, pf2, pn2, rf2, rn2, n2w, n3s, s2, pf3, pc3, rf3, rc3,
        lsem, ss0, rs0, sf1, qf1, sc1, qc1, sf2, qf2, sc2, qc2, sf3, qf3, sc3, qc3,
    ) = refs[36:]
    g = lax.axis_index("grp")
    l = lax.axis_index("loc")
    lv = [Level(k, g, l, windows[k]) for k in range(4)]
    L0, L1, L2, L3 = lv
    sent = []

    def device(dg, dl):
        return lax.rem(g + dg + NG, NG), lax.rem(l + dl + NL, NL)

    def send(src, dst, s_sem, r_sem, to):
        copy = pltpu.make_async_remote_copy(
            src_ref=src, dst_ref=dst, send_sem=s_sem, recv_sem=r_sem,
            device_id=device(*to), device_id_type=MESH,
        )
        copy.start()
        sent.append(copy)
        return copy

    load_f = pltpu.make_async_copy(rhs, L0.F.at[4:20, 0:32], lsem.at[0])
    load_p = pltpu.make_async_copy(phase, ph, lsem.at[1])
    load_p.start()
    load_f.start()
    barrier = pltpu.get_barrier_semaphore()
    for to in GREET:
        pl.semaphore_signal(barrier, inc=1, device_id=device(*to), device_id_type=MESH)

    load_p.wait()
    gas = ph[...].astype(F32)
    L0.C[4:20, 0:32] = 1.0 + 999.0 * gas
    pairs = jnp.concatenate([gas[2 * i:2 * i + 1] + gas[2 * i + 1:2 * i + 2] for i in range(8)], 0)
    ct1[...] = jnp.dot(
        pairs.reshape(8 * 32, 256).astype(BF16), p0_mat[...], preferred_element_type=F32
    ).reshape(8, 32, 128)
    n1[...] = ct1[:, pl.ds(0, 16, stride=2), :] + ct1[:, pl.ds(1, 16, stride=2), :]
    count1 = n1[...]
    L1.C[4:12, 0:16] = 1.0 + 124.875 * count1
    pairs = jnp.concatenate([count1[2 * i:2 * i + 1] + count1[2 * i + 1:2 * i + 2] for i in range(4)], 0)
    ct2[...] = jnp.dot(
        pairs.reshape(4 * 16, 128).astype(BF16), p1_mat[...], preferred_element_type=F32
    ).reshape(4, 16, 128)
    count2 = ct2[:, pl.ds(0, 8, stride=2), :] + ct2[:, pl.ds(1, 8, stride=2), :]
    pn2[...] = count2[0:2] + pltpu.roll(count2[2:4], 64, 2)
    rn2[3, 1] = pn2[...]

    load_f.wait()
    sub = row_ids((1, 8, 256)) < 4
    upk[...] = jnp.where(sub, pltpu.roll(L0.C[4:20, 24:32], 4, 1), L0.F[4:20, 24:32])
    dpk[...] = jnp.where(sub, L0.F[4:20, 0:8], pltpu.roll(L0.C[4:20, 0:8], 4, 1))
    for ref in (L3.F, L3.C):
        ref[:, 64:72] = jnp.zeros((PLANES[3], 8, 128), F32)

    pl.semaphore_wait(barrier, len(GREET))

    first = []
    k = 0
    for src, dst, to in (
        (upk, rxl0.at[4:20], (0, 1)),
        (dpk, rxh0.at[4:20], (0, -1)),
        (L0.C.at[16:20, 0:32], L0.C.at[0:4, 0:32], (1, 0)),
        (L0.F.at[17:20, 0:32], L0.F.at[1:4, 0:32], (1, 0)),
        (L0.C.at[4:6, 0:32], L0.C.at[20:22, 0:32], (-1, 0)),
        (L0.F.at[4:6, 0:32], L0.F.at[20:22, 0:32], (-1, 0)),
        (upk.at[12:16], rxl0.at[0:4], (1, 1)),
        (dpk.at[12:16], rxh0.at[0:4], (1, -1)),
        (upk.at[0:2], rxl0.at[20:22], (-1, 1)),
        (dpk.at[0:2], rxh0.at[20:22], (-1, -1)),
    ):
        first.append(send(src, dst, ss0.at[k], rs0.at[k], to))
        k += 1

    def near_sends(ref, low, high, ssem, rsem, depth):
        copies = []
        for k, (dg, dl) in enumerate(NEAR):
            lo, hi, at = {1: (12 - depth, 12, 4 - depth), 0: (4, 12, 4), -1: (4, 6, 12)}[dg]
            rows, target = {1: (slice(8, 16), low), 0: (slice(0, 16), ref), -1: (slice(0, 8), high)}[dl]
            where = pl.ds(at, hi - lo)
            dst = target.at[where, 0:16] if dl == 0 else target.at[where]
            copies.append(send(ref.at[lo:hi, rows], dst, ssem.at[k], rsem.at[k], (dg, dl)))
        return copies

    def wide_sends(src, slots, ssem, rsem):
        return [
            send(src, slots.at[3 - dg, 1 - dl], ssem.at[k], rsem.at[k], (dg, dl))
            for k, (dg, dl) in enumerate(WIDE)
        ]

    def along_sends(src, slots, ssem, rsem):
        mine = slots.at[lax.div(l, 2), lax.rem(l, 2)]
        return [send(src, mine, ssem.at[k], rsem.at[k], to) for k, to in enumerate(ALONG)]

    got_c1 = near_sends(L1.C, crl1, crh1, sc1, qc1, 4)
    got_c2 = wide_sends(pn2, rn2, sc2, qc2)

    for copy in first:
        copy.wait_recv()
    rows0 = L0.row_valid((40, 256))
    sub = row_ids((8, 256)) < 4

    def merge(i, _):
        low, high = rxl0[i], rxh0[i]
        L0.F[i, 32:40] = jnp.where(sub, high, low)
        L0.C[i, 32:40] = pltpu.roll(jnp.where(sub, low, high), 4, 0) * rows0[32:40] * L0.plane_valid(i)
        return 0

    lax.fori_loop(0, 22, merge, 0)
    for i in (0, 1, 2, 3, 20, 21):
        L0.C[i, 0:32] = L0.C[i, 0:32] * L0.plane_valid(i)

    def setup(i, before):
        cells = L0.cells(L0.C[i])
        ei, ej, el, k5, w = L0.coefficients(cells, before, rows0 * L0.plane_valid(i))
        L0.Ei[i], L0.Ej[i], L0.El[i], L0.K5[i], L0.W[i] = ei, ej, el, k5, w
        L0.U[i] = w * (12.0 * L0.F[i])
        return cells

    before = L0.cells(L0.C[0])
    L0.Ei[0] = before[2]
    L0.planes_loop(1, 22, setup, before, 3)

    def second(i, u, b):
        L0.V[i] = u + L0.W[i] * (12.0 * L0.F[i] - b)

    L0.apply_loop(L0.U, 2, 21, second, 3)

    def residual(i, u, b):
        r = (12.0 * L0.F[i] - b) * (rows0 * L0.plane_valid(i))
        rs[i - 3, 0:8] = r[32:40]
        rs[i - 3, 8:40] = r[0:32]
        out[jnp.maximum(i - 4, 0)] = r[0:32] * (1.0 / 12.0)

    L0.apply_loop(L0.V, 3, 20, residual, 3)
    store = pltpu.make_async_copy(out, fine_out, lsem.at[2])
    store.start()

    def restrict(scratch, matrix, planes, rows, lanes, kept):
        scratch_r, scratch_s = scratch
        scratch_s[...] = split_dot(scratch_r.reshape(planes * rows, lanes), matrix).reshape(planes, rows, 128)
        h = 0.5 * (
            scratch_s[:, pl.ds(7, kept, stride=2), :] + scratch_s[:, pl.ds(9, kept, stride=2), :]
        ) + scratch_s[:, pl.ds(8, kept, stride=2), :]
        count = (planes - 1) // 2
        return [0.5 * (h[2 * i] + h[2 * i + 2]) + h[2 * i + 1] for i in range(count)]

    f1 = restrict((rs[...], s0), r0_mat[...], 17, 40, 256, 16)
    for i in range(8):
        L1.F[4 + i, 0:16] = f1[i]
    got_f1 = near_sends(L1.F, rxl1, rxh1, sf1, qf1, 3)

    for copy in got_c1:
        copy.wait_recv()
    sub1 = row_ids((1, 8, 128)) < 4
    valid1 = L1.row_valid((1, 24, 128)) * L1.plane_valid_many(0, 14)
    c1w[:, 0:16] = L1.C[:, 0:16] * valid1[:, 0:16]
    c1w[:, 16:24] = jnp.where(sub1, crh1[...], crl1[...]) * valid1[:, 16:24]
    L1.C = c1w
    L1.setup_all(1, 14)

    def unpack_wide(slots, put):
        lane = lane_ids((1, 1, 1, 128)) < 64
        own = slots[:, 1]
        halo = jnp.where(row_ids((1, 1, 8, 128)) < 4, slots[:, 2], slots[:, 0])
        for tile, rows in ((own, slice(0, 8)), (halo, slice(8, 16))):
            first = jnp.where(lane, tile, 0.0)
            later = jnp.where(lane, pltpu.roll(tile, 64, 3), 0.0)
            for d in range(7):
                for half in range(2):
                    put(4 * d + half, rows, first[d, half])
                    put(4 * d + 2 + half, rows, later[d, half])

    for copy in got_c2:
        copy.wait_recv()

    def put_n2(i, rows, value):
        n2w[i, rows] = value

    unpack_wide(rn2, put_n2)
    valid2 = L2.row_valid((1, 16, 128)) * L2.plane_valid_many(0, 28)
    L2.C[...] = (1.0 + (999.0 / 64.0) * n2w[...]) * valid2
    L2.setup_all(1, 26)

    count2 = n2w[2:24, 0:8]
    pairs = jnp.concatenate([count2[2 * i:2 * i + 1] + count2[2 * i + 1:2 * i + 2] for i in range(11)], 0)
    n3s[...] = jnp.dot(
        pairs.reshape(11 * 8, 128).astype(BF16), p1_mat[...], preferred_element_type=F32
    ).reshape(11, 8, 128)
    count3 = n3s[:, pl.ds(0, 4, stride=2), :] + n3s[:, pl.ds(1, 4, stride=2), :]

    odd = lax.rem(l, 2) == 1

    def pack(planes, ref):
        for t in range(2):
            for h in range(2):
                total = jnp.zeros((4, 128), F32)
                for q in range(4):
                    p = 8 * t + 4 * h + q
                    if p < len(planes):
                        total = total + (pltpu.roll(planes[p], 32 * q, 1) if q else planes[p])
                ref[t, 4 * h:4 * h + 4] = total
        tiles = ref[...]
        ref[...] = jnp.where(odd, pltpu.roll(tiles, 4, 1), tiles)

    def unpack_along(slots, count, put):
        sub = row_ids((1, 8, 128)) < 4
        lane = lane_ids((1, 8, 128)) < 32
        for p in range(count):
            t, h, q = p // 8, (p % 8) // 4, p % 4
            even, other = slots[:, 0, t], slots[:, 1, t]
            tile = jnp.where(sub, even, other) if h == 0 else pltpu.roll(jnp.where(sub, other, even), 4, 1)
            if q:
                tile = pltpu.roll(tile, 128 - 32 * q, 2)
            put(p, jnp.where(lane, tile, 0.0).reshape(64, 128))

    pack([count3[i] for i in range(11)], pc3)
    rc3[lax.div(l, 2), lax.rem(l, 2)] = pc3[...]
    got_c3 = along_sends(pc3, rc3, sc3, qc3)

    for copy in got_f1:
        copy.wait_recv()
    L1.F[1:14, 16:24] = jnp.where(sub1, rxh1[1:14], rxl1[1:14])
    L1.first_all(1, 14)
    L1.sweep_all(L1.U, L1.V, 2, 13)
    r1 = L1.residual_all(L1.V, 3, 12) * valid1[3:12]
    r1 = jnp.concatenate([r1[:, 16:24], r1[:, 0:16]], 1)
    f2 = restrict((r1, s1), r1_mat[...], 9, 24, 128, 8)
    pf2[...] = jnp.concatenate([x[None] for x in f2[0:2]], 0) + pltpu.roll(
        jnp.concatenate([x[None] for x in f2[2:4]], 0), 64, 2
    )
    rf2[3, 1] = pf2[...]
    got_f2 = wide_sends(pf2, rf2, sf2, qf2)

    for copy in got_c3:
        copy.wait_recv()

    def put_c3(p, value):
        L3.C[p, 0:64] = (1.0 + (999.0 / 512.0) * value) * (
            L3.row_valid((72, 128))[0:64] * L3.plane_valid(p)
        )

    unpack_along(rc3, 11, put_c3)
    L3.setup_all(1, 11)

    for copy in got_f2:
        copy.wait_recv()

    def put_f2(i, rows, value):
        L2.F[i, rows] = value

    unpack_wide(rf2, put_f2)
    L2.first_all(1, 26)
    L2.sweep_all(L2.U, L2.V, 2, 25)
    r2 = L2.residual_all(L2.V, 3, 24) * valid2[3:24]
    r2 = jnp.concatenate([r2[:, 8:16], r2[:, 0:8]], 1)
    f3 = restrict((r2, s2), r2_mat[...], 21, 16, 128, 4)
    pack(f3, pf3)
    rf3[lax.div(l, 2), lax.rem(l, 2)] = pf3[...]
    got_f3 = along_sends(pf3, rf3, sf3, qf3)
    for copy in got_f3:
        copy.wait_recv()

    def put_f3(p, value):
        L3.F[p + 1, 0:64] = value

    unpack_along(rf3, 10, put_f3)
    L3.first_all(1, 11)
    source, target = L3.U, L3.V
    for sweep in range(COARSE_SWEEPS - 1):
        L3.sweep_all(source, target, 2 + sweep, 10 - sweep)
        source, target = target, source
    coarse_out[...] = ((8.0 / 12.0) * L3.residual_all(source, 5, 7))[:, 0:64, 0:32]

    store.wait()
    for copy in sent:
        copy.wait_send()


def lane_matrices():
    def weights(size, used):
        k = jnp.arange(size)[:, None]
        c = jnp.arange(128)[None, :]
        live = (k < used) & (c < used // 2)
        near = jnp.abs(k - 2 * c)
        full = jnp.where(live, jnp.where(near == 0, 0.5, jnp.where(near == 1, 0.25, 0.0)), 0.0)
        return full.astype(BF16)

    def sums(size):
        k = jnp.arange(size)[:, None]
        c = jnp.arange(128)[None, :]
        return jnp.where(k // 2 == c, 1.0, 0.0).astype(BF16)

    return weights(256, 256), weights(128, 128), weights(128, 64), sums(256), sums(128)


def per_device(right_side, phase):
    scratch = []
    for k in range(4):
        shape = (PLANES[k], ROWS[k], LANES[k])
        scratch += [pltpu.VMEM(shape, F32) for _ in range(9)]
    scratch += [
        pltpu.VMEM(s, d)
        for s, d in (
            ((16, 32, 256), jnp.int32),
            ((16, 8, 256), F32), ((16, 8, 256), F32),
            ((22, 8, 256), F32), ((22, 8, 256), F32),
            ((17, 40, 256), F32), ((17, 40, 128), F32),
            ((16, 32, 256), F32),
            ((8, 32, 128), F32), ((8, 16, 128), F32), ((17, 16, 128), F32),
            ((14, 8, 128), F32), ((14, 8, 128), F32), ((14, 8, 128), F32), ((14, 8, 128), F32),
            ((14, 24, 128), F32),
            ((9, 24, 128), F32),
            ((4, 16, 128), F32),
            ((2, 8, 128), F32), ((2, 8, 128), F32),
            ((7, 3, 2, 8, 128), F32), ((7, 3, 2, 8, 128), F32),
            ((28, 16, 128), F32), ((11, 8, 128), F32), ((21, 16, 128), F32),
            ((2, 8, 128), F32), ((2, 8, 128), F32),
            ((8, 2, 2, 8, 128), F32), ((8, 2, 2, 8, 128), F32),
        )
    ]
    scratch.append(pltpu.SemaphoreType.DMA((3,)))
    for n in (10, len(NEAR), len(NEAR), len(WIDE), len(WIDE), len(ALONG), len(ALONG)):
        scratch += [pltpu.SemaphoreType.DMA((n,)), pltpu.SemaphoreType.DMA((n,))]
    vmem = pl.BlockSpec(memory_space=pltpu.VMEM)
    hbm = pl.BlockSpec(memory_space=pl.ANY)
    return pl.pallas_call(
        kernel,
        out_shape=(
            jax.ShapeDtypeStruct((16, 32, 256), F32),
            jax.ShapeDtypeStruct((2, 64, 32), F32),
        ),
        in_specs=[hbm, hbm] + [vmem] * 5,
        out_specs=(hbm, vmem),
        scratch_shapes=scratch,
        compiler_params=pltpu.CompilerParams(
            collective_id=0, has_side_effects=True, vmem_limit_bytes=56 * 2**20
        ),
    )(right_side, phase, *lane_matrices())


def solution(mesh):
    in_specs = (P("grp", "loc", None), P("grp", "loc", None))
    out_specs = (P("grp", "loc", None), P("grp", None, None))
    return jax.shard_map(
        per_device, mesh=mesh, in_specs=in_specs, out_specs=out_specs, check_vma=False
    )
```

```python
import functools

import jax
import jax.numpy as jnp
from jax import lax
from jax.experimental import pallas as pl
from jax.experimental.pallas import tpu as pltpu
from jax.sharding import PartitionSpec as P

MESH = pl.DeviceIdType.MESH
NG, NL = 16, 16
COARSE_SWEEPS = 4
F32 = jnp.float32
BF16 = jnp.bfloat16
WHOLE = ((256, 512, 256), (128, 256, 128), (64, 128, 64), (32, 64, 32))
BLOCK = ((16, 32, 256), (8, 16, 128), (4, 8, 64), (2, 64, 32))
LOW = (4, 4, 12, 5)
PLANES = (22, 14, 28, 11)
ROWS = (40, 24, 16, 72)
LANES = (256, 128, 128, 128)

NEAR = [(a, b) for a in (-1, 0, 1) for b in (-1, 0, 1) if (a, b) != (0, 0)]
WIDE = [(a, b) for c in (3, 2, 1, 0) for a in (-c, c)[:1 + (c > 0)] for b in (-1, 1, 0) if (a, b) != (0, 0)]
ALONG = [(0, k) for k in (10, 9, 11, 6, 5, 7, 14, 13, 2, 8, 3, 15, 12, 4, 1)]
GREET = [to for to in WIDE if to[0]] + ALONG


def lane_ids(shape):
    return lax.broadcasted_iota(jnp.int32, shape, len(shape) - 1)


def row_ids(shape):
    return lax.broadcasted_iota(jnp.int32, shape, len(shape) - 2)


def split_dot(values, matrix):
    high = values.astype(BF16)
    rest = values - high.astype(F32)
    mid = rest.astype(BF16)
    low = (rest - mid.astype(F32)).astype(BF16)
    dot = functools.partial(jnp.dot, preferred_element_type=F32)
    return dot(high, matrix) + (dot(mid, matrix) + dot(low, matrix))


class Level:
    def __init__(self, index, g, l, refs):
        self.index = index
        self.F, self.C, self.U, self.V, self.Ei, self.Ej, self.El, self.K5, self.W = refs
        self.n = BLOCK[index]
        self.low = LOW[index]
        self.rows, self.lanes = ROWS[index], LANES[index]
        self.g, self.l = g, l

    def up(self, x, axis):
        return pltpu.roll(x, x.shape[axis] - 1, axis)

    def down(self, x, axis):
        return pltpu.roll(x, 1, axis)

    def lane_up(self, x):
        y = self.up(x, x.ndim - 1)
        return jnp.where(lane_ids(y.shape) == self.n[2] - 1, 0.0, y) if self.n[2] == self.lanes else y

    def lane_down(self, x):
        y = self.down(x, x.ndim - 1)
        return jnp.where(lane_ids(y.shape) == 0, 0.0, y) if self.n[2] == self.lanes else y

    def row_up(self, x):
        return self.up(x, x.ndim - 2)

    def row_down(self, x):
        return self.down(x, x.ndim - 2)

    def row_valid(self, shape):
        r = row_ids(shape)
        if self.index == 3:
            ok = r < self.n[1]
        else:
            j = jnp.where(r < self.n[1] + 4, r, r - self.rows) + self.l * self.n[1]
            ok = (j >= 0) & (j < WHOLE[self.index][1])
        if self.n[2] < self.lanes:
            ok = ok & (lane_ids(shape) < self.n[2])
        return jnp.where(ok, 1.0, 0.0).astype(F32)

    def plane_valid(self, i):
        p = self.g * self.n[0] + (i - self.low)
        return jnp.where((p >= 0) & (p < WHOLE[self.index][0]), 1.0, 0.0).astype(F32)

    def plane_valid_many(self, lo, hi):
        shape = (hi - lo, self.rows, self.lanes)
        p = self.g * self.n[0] + (lo - self.low) + lax.broadcasted_iota(jnp.int32, shape, 0)
        return jnp.where((p >= 0) & (p < WHOLE[self.index][0]), 1.0, 0.0).astype(F32)

    def cells(self, c):
        cl = c + self.lane_down(c)
        cj = c + self.row_down(c)
        cjl = cl + self.row_down(cl)
        return cl, cj, cjl

    def coefficients(self, cells, before, valid):
        cl, cj, cjl = cells
        pl_, pj, pjl = before
        k = cjl + pjl
        el = cj + pj
        if self.n[2] == self.lanes:
            el = jnp.where(lane_ids(el.shape) == self.n[2] - 1, 0.0, el)
        return cjl, cl + pl_, el, 5.0 * k, valid * (0.15 / jnp.maximum(k, 1.0))

    def parts(self, u):
        ul = self.lane_up(u)
        uj = self.row_up(u)
        a = u + ul
        return ul, uj, a + self.row_up(a)

    def combine(self, u, un, up, ul, uj, t, ei, eip, ej, el, k5):
        tj = t + self.row_down(t)
        b = k5 * u + ei * un + eip * up + ej * uj + el * ul - tj
        return b + self.lane_down(el * u - tj) + self.row_down(ej * u)

    def setup_all(self, lo, hi):
        cl, cj, cjl = self.cells(self.C[lo - 1:hi])
        valid = self.row_valid((1, self.rows, self.lanes)) * self.plane_valid_many(lo, hi)
        ei, ej, el, k5, w = self.coefficients(
            (cl[1:], cj[1:], cjl[1:]), (cl[:-1], cj[:-1], cjl[:-1]), valid
        )
        self.Ei[lo - 1:hi] = cjl
        self.Ej[lo:hi] = ej
        self.El[lo:hi] = el
        self.K5[lo:hi] = k5
        self.W[lo:hi] = w

    def apply_all(self, u_ref, lo, hi):
        u = u_ref[lo - 1:hi + 1]
        ul, uj, v = self.parts(u)
        t = self.C[lo - 1:hi] * (v[:-1] + v[1:])
        return self.combine(
            u[1:-1], u[2:], u[:-2], ul[1:-1], uj[1:-1], t[1:] + t[:-1],
            self.Ei[lo:hi], self.Ei[lo - 1:hi - 1], self.Ej[lo:hi], self.El[lo:hi], self.K5[lo:hi],
        )

    def first_all(self, lo, hi):
        self.U[lo:hi] = self.W[lo:hi] * self.F[lo:hi]

    def sweep_all(self, source, target, lo, hi):
        b = self.apply_all(source, lo, hi)
        target[lo:hi] = source[lo:hi] + self.W[lo:hi] * (self.F[lo:hi] - b)

    def residual_all(self, source, lo, hi):
        return self.F[lo:hi] - self.apply_all(source, lo, hi)

    def planes_loop(self, lo, hi, step, carry, unroll):
        whole = (hi - lo) // unroll

        def body(k, c):
            for m in range(unroll):
                c = step(lo + k * unroll + m, c)
            return c

        carry = lax.fori_loop(0, whole, body, carry)
        for i in range(lo + whole * unroll, hi):
            carry = step(i, carry)
        return carry

    def apply_loop(self, u_ref, lo, hi, emit, unroll):
        _, _, v0 = self.parts(u_ref[lo - 1])
        ul, uj, v = self.parts(u_ref[lo])
        t = self.C[lo - 1] * (v0 + v)

        def step(i, carry):
            ul, uj, v, t = carry
            u = u_ref[i]
            un = u_ref[i + 1]
            uln, ujn, vn = self.parts(un)
            tn = self.C[i] * (v + vn)
            b = self.combine(
                u, un, u_ref[i - 1], ul, uj, t + tn,
                self.Ei[i], self.Ei[i - 1], self.Ej[i], self.El[i], self.K5[i],
            )
            emit(i, u, b)
            return uln, ujn, vn, tn

        self.planes_loop(lo, hi, step, (ul, uj, v, t), unroll)


def kernel(*refs):
    rhs, phase, fine_out, coarse_out = refs[:4]
    refs = refs[4:]
    windows = [refs[9 * k:9 * k + 9] for k in range(4)]
    (
        ph, upk, dpk, rxl0, rxh0, rs, s0, out, ct1, n1, h0,
        rxl1, rxh1, crl1, crh1, c1w, s1, ct2, pf2, pn2, rf2, rn2, n2w, n3s, s2, pf3, pc3, rf3, rc3,
        r0_mat, r1_mat, r2_mat, p0_mat, p1_mat,
        lsem, ss0, rs0, sf1, qf1, sc1, qc1, sf2, qf2, sc2, qc2, sf3, qf3, sc3, qc3,
    ) = refs[36:]
    g = lax.axis_index("grp")
    l = lax.axis_index("loc")
    lv = [Level(k, g, l, windows[k]) for k in range(4)]
    L0, L1, L2, L3 = lv
    sent = []

    def device(dg, dl):
        return lax.rem(g + dg + NG, NG), lax.rem(l + dl + NL, NL)

    def inside(dg, dl):
        tests = [t for t in (
            g + dg >= 0 if dg < 0 else None, g + dg < NG if dg > 0 else None,
            l + dl >= 0 if dl < 0 else None, l + dl < NL if dl > 0 else None,
        ) if t is not None]
        return functools.reduce(jnp.logical_and, tests)

    def run(test, action):
        action() if test is None else pl.when(test)(action)

    class Sent:
        def __init__(self, src, dst, s_sem, r_sem, to, wrap):
            self.copy = pltpu.make_async_remote_copy(
                src_ref=src, dst_ref=dst, send_sem=s_sem, recv_sem=r_sem,
                device_id=device(*to), device_id_type=MESH,
            )
            self.out = None if wrap else inside(*to)
            self.back = None if wrap else inside(-to[0], -to[1])
            run(self.out, self.copy.start)
            sent.append(self)

        def wait_recv(self):
            run(self.back, self.copy.wait_recv)

        def wait_send(self):
            run(self.out, self.copy.wait_send)

    def send(src, dst, s_sem, r_sem, to, wrap=False):
        return Sent(src, dst, s_sem, r_sem, to, wrap)

    load_f = pltpu.make_async_copy(rhs, L0.F.at[4:20, 0:32], lsem.at[0])
    load_p = pltpu.make_async_copy(phase, ph, lsem.at[1])
    load_p.start()
    load_f.start()
    barrier = pltpu.get_barrier_semaphore()
    expected = jnp.int32(0)
    for to in GREET:
        test = inside(*to) if to[0] or to[1] < 0 else None

        def greet(to=to):
            pl.semaphore_signal(barrier, inc=1, device_id=device(*to), device_id_type=MESH)

        run(test, greet)
        expected = expected + (1 if test is None else jnp.where(test, 1, 0))

    def clear(test, *refs):
        @pl.when(test)
        def _():
            for ref in refs:
                ref[...] = jnp.zeros(ref.shape, F32)

    near_tiles = (rxl1, rxh1, crl1, crh1)
    clear(
        g == 0, L0.F.at[0:4, 0:32], L0.C.at[0:4, 0:32], L1.F.at[0:4, 0:16], L1.C.at[0:4, 0:16],
        *[x.at[0:4] for x in (rxl0, rxh0) + near_tiles],
    )
    clear(
        g == NG - 1, L0.F.at[20:22, 0:32], L0.C.at[20:22, 0:32], L1.F.at[12:14, 0:16], L1.C.at[12:14, 0:16],
        *[x.at[20:22] for x in (rxl0, rxh0)], *[x.at[12:14] for x in near_tiles],
    )
    clear(l == 0, rxl0, rxl1, crl1, rf2.at[:, 0], rn2.at[:, 0])
    clear(l == NL - 1, rxh0, rxh1, crh1, rf2.at[:, 2], rn2.at[:, 2])
    for d in (1, 2, 3):
        clear(g < d, rf2.at[3 - d], rn2.at[3 - d])
        clear(g >= NG - d, rf2.at[3 + d], rn2.at[3 + d])

    load_p.wait()
    gas = ph[...].astype(F32)
    L0.C[4:20, 0:32] = 1.0 + 999.0 * gas
    load_f.wait()
    sub = row_ids((1, 8, 256)) < 4
    upk[...] = jnp.where(sub, pltpu.roll(L0.C[4:20, 24:32], 4, 1), L0.F[4:20, 24:32])
    dpk[...] = jnp.where(sub, L0.F[4:20, 0:8], pltpu.roll(L0.C[4:20, 0:8], 4, 1))
    pl.semaphore_wait(barrier, expected)

    first = []
    k = 0
    for src, dst, to in (
        (upk, rxl0.at[4:20], (0, 1)),
        (dpk, rxh0.at[4:20], (0, -1)),
        (L0.C.at[16:20, 0:32], L0.C.at[0:4, 0:32], (1, 0)),
        (L0.F.at[17:20, 0:32], L0.F.at[1:4, 0:32], (1, 0)),
        (L0.C.at[4:6, 0:32], L0.C.at[20:22, 0:32], (-1, 0)),
        (L0.F.at[4:6, 0:32], L0.F.at[20:22, 0:32], (-1, 0)),
        (upk.at[12:16], rxl0.at[0:4], (1, 1)),
        (dpk.at[12:16], rxh0.at[0:4], (1, -1)),
        (upk.at[0:2], rxl0.at[20:22], (-1, 1)),
        (dpk.at[0:2], rxh0.at[20:22], (-1, -1)),
    ):
        first.append(send(src, dst, ss0.at[k], rs0.at[k], to))
        k += 1

    def near_sends(ref, low, high, ssem, rsem, depth):
        copies = []
        for k, (dg, dl) in enumerate(NEAR):
            lo, hi, at = {1: (12 - depth, 12, 4 - depth), 0: (4, 12, 4), -1: (4, 6, 12)}[dg]
            rows, target = {1: (slice(8, 16), low), 0: (slice(0, 16), ref), -1: (slice(0, 8), high)}[dl]
            where = pl.ds(at, hi - lo)
            dst = target.at[where, 0:16] if dl == 0 else target.at[where]
            copies.append(send(ref.at[lo:hi, rows], dst, ssem.at[k], rsem.at[k], (dg, dl)))
        return copies

    def wide_sends(src, slots, ssem, rsem):
        return [
            send(src, slots.at[3 - dg, 1 - dl], ssem.at[k], rsem.at[k], (dg, dl))
            for k, (dg, dl) in enumerate(WIDE)
        ]

    def along_sends(src, slots, ssem, rsem):
        mine = slots.at[lax.div(l, 2), lax.rem(l, 2)]
        return [send(src, mine, ssem.at[k], rsem.at[k], to, True) for k, to in enumerate(ALONG)]

    weights = ((r0_mat, 256), (r1_mat, 128), (r2_mat, 64))
    for ref, used in weights:
        k, c = row_ids(ref.shape), lane_ids(ref.shape)
        near = jnp.abs(k - 2 * c)
        live = (k < used) & (c < used // 2)
        ref[...] = jnp.where(
            live & (near == 0), 0.5, jnp.where(live & (near == 1), 0.25, 0.0)
        ).astype(BF16)
    for ref in (p0_mat, p1_mat):
        half = row_ids(ref.shape) - 2 * lane_ids(ref.shape)
        ref[...] = jnp.where((half == 0) | (half == 1), 1.0, 0.0).astype(BF16)

    pairs = jnp.concatenate([gas[2 * i:2 * i + 1] + gas[2 * i + 1:2 * i + 2] for i in range(8)], 0)
    ct1[...] = jnp.dot(
        pairs.reshape(8 * 32, 256).astype(BF16), p0_mat[...], preferred_element_type=F32
    ).reshape(8, 32, 128)
    n1[...] = ct1[:, pl.ds(0, 16, stride=2), :] + ct1[:, pl.ds(1, 16, stride=2), :]
    count1 = n1[...]
    L1.C[4:12, 0:16] = 1.0 + 124.875 * count1
    pairs = jnp.concatenate([count1[2 * i:2 * i + 1] + count1[2 * i + 1:2 * i + 2] for i in range(4)], 0)
    ct2[...] = jnp.dot(
        pairs.reshape(4 * 16, 128).astype(BF16), p1_mat[...], preferred_element_type=F32
    ).reshape(4, 16, 128)
    count2 = ct2[:, pl.ds(0, 8, stride=2), :] + ct2[:, pl.ds(1, 8, stride=2), :]
    pn2[...] = count2[0:2] + pltpu.roll(count2[2:4], 64, 2)
    rn2[3, 1] = pn2[...]

    for ref in (L3.F, L3.C):
        ref[:, 64:72] = jnp.zeros((PLANES[3], 8, 128), F32)

    got_c1 = near_sends(L1.C, crl1, crh1, sc1, qc1, 4)
    got_c2 = wide_sends(pn2, rn2, sc2, qc2)

    for copy in first:
        copy.wait_recv()
    rows0 = L0.row_valid((40, 256))
    sub = row_ids((8, 256)) < 4

    def merge(i, _):
        low, high = rxl0[i], rxh0[i]
        L0.F[i, 32:40] = jnp.where(sub, high, low)
        L0.C[i, 32:40] = pltpu.roll(jnp.where(sub, low, high), 4, 0) * rows0[32:40] * L0.plane_valid(i)
        return 0

    lax.fori_loop(0, 22, merge, 0)
    for i in (0, 1, 2, 3, 20, 21):
        L0.C[i, 0:32] = L0.C[i, 0:32] * L0.plane_valid(i)

    def setup(i, before):
        cells = L0.cells(L0.C[i])
        ei, ej, el, k5, w = L0.coefficients(cells, before, rows0 * L0.plane_valid(i))
        L0.Ei[i], L0.Ej[i], L0.El[i], L0.K5[i], L0.W[i] = ei, ej, el, k5, w
        L0.U[i] = w * (12.0 * L0.F[i])
        return cells

    before = L0.cells(L0.C[0])
    L0.Ei[0] = before[2]
    L0.planes_loop(1, 22, setup, before, 3)

    def second(i, u, b):
        L0.V[i] = u + L0.W[i] * (12.0 * L0.F[i] - b)

    L0.apply_loop(L0.U, 2, 21, second, 3)

    def residual(i, u, b):
        r = (12.0 * L0.F[i] - b) * (rows0 * L0.plane_valid(i))
        rs[i - 3, 0:8] = r[32:40]
        rs[i - 3, 8:40] = r[0:32]
        out[jnp.maximum(i - 4, 0)] = r[0:32] * (1.0 / 12.0)

    L0.apply_loop(L0.V, 3, 20, residual, 3)
    store = pltpu.make_async_copy(out, fine_out, lsem.at[2])
    store.start()

    def restrict(scratch, matrix, planes, rows, lanes, kept):
        scratch_r, scratch_s = scratch
        scratch_s[...] = split_dot(scratch_r.reshape(planes * rows, lanes), matrix).reshape(planes, rows, 128)
        h = 0.5 * (
            scratch_s[:, pl.ds(7, kept, stride=2), :] + scratch_s[:, pl.ds(9, kept, stride=2), :]
        ) + scratch_s[:, pl.ds(8, kept, stride=2), :]
        count = (planes - 1) // 2
        return [0.5 * (h[2 * i] + h[2 * i + 2]) + h[2 * i + 1] for i in range(count)]

    f1 = restrict((rs[...], s0), r0_mat[...], 17, 40, 256, 16)
    for i in range(8):
        L1.F[4 + i, 0:16] = f1[i]
    got_f1 = near_sends(L1.F, rxl1, rxh1, sf1, qf1, 3)

    for copy in got_c1:
        copy.wait_recv()
    sub1 = row_ids((1, 8, 128)) < 4
    valid1 = L1.row_valid((1, 24, 128)) * L1.plane_valid_many(0, 14)
    c1w[:, 0:16] = L1.C[:, 0:16] * valid1[:, 0:16]
    c1w[:, 16:24] = jnp.where(sub1, crh1[...], crl1[...]) * valid1[:, 16:24]
    L1.C = c1w
    L1.setup_all(1, 14)

    def unpack_wide(slots, put):
        lane = lane_ids((1, 1, 1, 128)) < 64
        own = slots[:, 1]
        halo = jnp.where(row_ids((1, 1, 8, 128)) < 4, slots[:, 2], slots[:, 0])
        for tile, rows in ((own, slice(0, 8)), (halo, slice(8, 16))):
            first = jnp.where(lane, tile, 0.0)
            later = jnp.where(lane, pltpu.roll(tile, 64, 3), 0.0)
            for d in range(7):
                for half in range(2):
                    put(4 * d + half, rows, first[d, half])
                    put(4 * d + 2 + half, rows, later[d, half])

    for copy in got_c2:
        copy.wait_recv()

    def put_n2(i, rows, value):
        n2w[i, rows] = value

    unpack_wide(rn2, put_n2)
    valid2 = L2.row_valid((1, 16, 128)) * L2.plane_valid_many(0, 28)
    L2.C[...] = (1.0 + (999.0 / 64.0) * n2w[...]) * valid2
    L2.setup_all(1, 26)

    count2 = n2w[2:24, 0:8]
    pairs = jnp.concatenate([count2[2 * i:2 * i + 1] + count2[2 * i + 1:2 * i + 2] for i in range(11)], 0)
    n3s[...] = jnp.dot(
        pairs.reshape(11 * 8, 128).astype(BF16), p1_mat[...], preferred_element_type=F32
    ).reshape(11, 8, 128)
    count3 = n3s[:, pl.ds(0, 4, stride=2), :] + n3s[:, pl.ds(1, 4, stride=2), :]

    odd = lax.rem(l, 2) == 1

    def pack(planes, ref):
        for t in range(2):
            for h in range(2):
                total = jnp.zeros((4, 128), F32)
                for q in range(4):
                    p = 8 * t + 4 * h + q
                    if p < len(planes):
                        total = total + (pltpu.roll(planes[p], 32 * q, 1) if q else planes[p])
                ref[t, 4 * h:4 * h + 4] = total
        tiles = ref[...]
        ref[...] = jnp.where(odd, pltpu.roll(tiles, 4, 1), tiles)

    def unpack_along(slots, count, put):
        sub = row_ids((1, 8, 128)) < 4
        lane = lane_ids((1, 8, 128)) < 32
        for p in range(count):
            t, h, q = p // 8, (p % 8) // 4, p % 4
            even, other = slots[:, 0, t], slots[:, 1, t]
            tile = jnp.where(sub, even, other) if h == 0 else pltpu.roll(jnp.where(sub, other, even), 4, 1)
            if q:
                tile = pltpu.roll(tile, 128 - 32 * q, 2)
            put(p, jnp.where(lane, tile, 0.0).reshape(64, 128))

    pack([count3[i] for i in range(11)], pc3)
    rc3[lax.div(l, 2), lax.rem(l, 2)] = pc3[...]
    got_c3 = along_sends(pc3, rc3, sc3, qc3)

    for copy in got_f1:
        copy.wait_recv()
    L1.F[1:14, 16:24] = jnp.where(sub1, rxh1[1:14], rxl1[1:14])
    L1.first_all(1, 14)
    L1.sweep_all(L1.U, L1.V, 2, 13)
    r1 = L1.residual_all(L1.V, 3, 12) * valid1[3:12]
    r1 = jnp.concatenate([r1[:, 16:24], r1[:, 0:16]], 1)
    f2 = restrict((r1, s1), r1_mat[...], 9, 24, 128, 8)
    pf2[...] = jnp.concatenate([x[None] for x in f2[0:2]], 0) + pltpu.roll(
        jnp.concatenate([x[None] for x in f2[2:4]], 0), 64, 2
    )
    rf2[3, 1] = pf2[...]
    got_f2 = wide_sends(pf2, rf2, sf2, qf2)

    for copy in got_c3:
        copy.wait_recv()

    def put_c3(p, value):
        L3.C[p, 0:64] = (1.0 + (999.0 / 512.0) * value) * (
            L3.row_valid((72, 128))[0:64] * L3.plane_valid(p)
        )

    unpack_along(rc3, 11, put_c3)
    L3.setup_all(1, 11)

    for copy in got_f2:
        copy.wait_recv()

    def put_f2(i, rows, value):
        L2.F[i, rows] = value

    unpack_wide(rf2, put_f2)
    L2.first_all(1, 26)
    L2.sweep_all(L2.U, L2.V, 2, 25)
    r2 = L2.residual_all(L2.V, 3, 24) * valid2[3:24]
    r2 = jnp.concatenate([r2[:, 8:16], r2[:, 0:8]], 1)
    f3 = restrict((r2, s2), r2_mat[...], 21, 16, 128, 4)
    pack(f3, pf3)
    rf3[lax.div(l, 2), lax.rem(l, 2)] = pf3[...]
    got_f3 = along_sends(pf3, rf3, sf3, qf3)
    for copy in got_f3:
        copy.wait_recv()

    def put_f3(p, value):
        L3.F[p + 1, 0:64] = value

    unpack_along(rf3, 10, put_f3)
    L3.first_all(1, 11)
    source, target = L3.U, L3.V
    for sweep in range(COARSE_SWEEPS - 1):
        L3.sweep_all(source, target, 2 + sweep, 10 - sweep)
        source, target = target, source
    last = (8.0 / 12.0) * L3.residual_all(source, 5, 7)
    for i in range(2):
        coarse_out[i] = jnp.transpose(last[i, 0:64], (1, 0))[0:32]

    store.wait()
    for copy in sent:
        copy.wait_send()


def per_device(right_side, phase):
    scratch = []
    for k in range(4):
        shape = (PLANES[k], ROWS[k], LANES[k])
        scratch += [pltpu.VMEM(shape, F32) for _ in range(9)]
    scratch += [
        pltpu.VMEM(s, d)
        for s, d in (
            ((16, 32, 256), jnp.int32),
            ((16, 8, 256), F32), ((16, 8, 256), F32),
            ((22, 8, 256), F32), ((22, 8, 256), F32),
            ((17, 40, 256), F32), ((17, 40, 128), F32),
            ((16, 32, 256), F32),
            ((8, 32, 128), F32), ((8, 16, 128), F32), ((17, 16, 128), F32),
            ((14, 8, 128), F32), ((14, 8, 128), F32), ((14, 8, 128), F32), ((14, 8, 128), F32),
            ((14, 24, 128), F32),
            ((9, 24, 128), F32),
            ((4, 16, 128), F32),
            ((2, 8, 128), F32), ((2, 8, 128), F32),
            ((7, 3, 2, 8, 128), F32), ((7, 3, 2, 8, 128), F32),
            ((28, 16, 128), F32), ((11, 8, 128), F32), ((21, 16, 128), F32),
            ((2, 8, 128), F32), ((2, 8, 128), F32),
            ((8, 2, 2, 8, 128), F32), ((8, 2, 2, 8, 128), F32),
            ((256, 128), BF16), ((128, 128), BF16), ((128, 128), BF16),
            ((256, 128), BF16), ((128, 128), BF16),
        )
    ]
    scratch.append(pltpu.SemaphoreType.DMA((3,)))
    for n in (10, len(NEAR), len(NEAR), len(WIDE), len(WIDE), len(ALONG), len(ALONG)):
        scratch += [pltpu.SemaphoreType.DMA((n,)), pltpu.SemaphoreType.DMA((n,))]
    vmem = pl.BlockSpec(memory_space=pltpu.VMEM)
    hbm = pl.BlockSpec(memory_space=pl.ANY)
    fine, coarse = pl.pallas_call(
        kernel,
        out_shape=(
            jax.ShapeDtypeStruct((16, 32, 256), F32),
            jax.ShapeDtypeStruct((2, 32, 64), F32),
        ),
        in_specs=[hbm, hbm],
        out_specs=(hbm, vmem),
        scratch_shapes=scratch,
        compiler_params=pltpu.CompilerParams(
            collective_id=0, has_side_effects=True, vmem_limit_bytes=56 * 2**20
        ),
    )(right_side, phase)
    return fine, jnp.transpose(coarse, (0, 2, 1))


def solution(mesh):
    in_specs = (P("grp", "loc", None), P("grp", "loc", None))
    out_specs = (P("grp", "loc", None), P("grp", None, None))
    return jax.shard_map(
        per_device, mesh=mesh, in_specs=in_specs, out_specs=out_specs, check_vma=False
    )
```

```python
import functools

import jax
import jax.numpy as jnp
from jax import lax
from jax.experimental import pallas as pl
from jax.experimental.pallas import tpu as pltpu
from jax.sharding import PartitionSpec as P

MESH = pl.DeviceIdType.MESH
NG, NL = 16, 16
COARSE_SWEEPS = 4
F32 = jnp.float32
BF16 = jnp.bfloat16
WHOLE = ((256, 512, 256), (128, 256, 128), (64, 128, 64), (32, 64, 32))
BLOCK = ((16, 32, 256), (8, 16, 128), (4, 8, 64), (2, 64, 32))
LOW = (4, 4, 12, 5)
PLANES = (22, 14, 28, 11)
ROWS = (40, 24, 16, 72)
LANES = (256, 128, 128, 128)

NEAR = [(a, b) for a in (-1, 0, 1) for b in (-1, 0, 1) if (a, b) != (0, 0)]
WIDE = [(a, b) for c in (3, 2, 1, 0) for a in (-c, c)[:1 + (c > 0)] for b in (-1, 1, 0) if (a, b) != (0, 0)]
ALONG = [(0, k) for k in (10, 9, 11, 6, 5, 7, 14, 13, 2, 8, 3, 15, 12, 4, 1)]
GREET = [to for to in WIDE if to[0]] + ALONG


def lane_ids(shape):
    return lax.broadcasted_iota(jnp.int32, shape, len(shape) - 1)


def row_ids(shape):
    return lax.broadcasted_iota(jnp.int32, shape, len(shape) - 2)


def split_dot(values, matrix):
    high = values.astype(BF16)
    rest = values - high.astype(F32)
    mid = rest.astype(BF16)
    low = (rest - mid.astype(F32)).astype(BF16)
    dot = functools.partial(jnp.dot, preferred_element_type=F32)
    return dot(high, matrix) + (dot(mid, matrix) + dot(low, matrix))


class Level:
    def __init__(self, index, g, l, refs):
        self.index = index
        self.F, self.C, self.U, self.V, self.Ei, self.Ej, self.El, self.K5, self.W = refs
        self.n = BLOCK[index]
        self.low = LOW[index]
        self.rows, self.lanes = ROWS[index], LANES[index]
        self.g, self.l = g, l

    def up(self, x, axis):
        return pltpu.roll(x, x.shape[axis] - 1, axis)

    def down(self, x, axis):
        return pltpu.roll(x, 1, axis)

    def lane_up(self, x):
        y = self.up(x, x.ndim - 1)
        return jnp.where(lane_ids(y.shape) == self.n[2] - 1, 0.0, y) if self.n[2] == self.lanes else y

    def lane_down(self, x):
        y = self.down(x, x.ndim - 1)
        return jnp.where(lane_ids(y.shape) == 0, 0.0, y) if self.n[2] == self.lanes else y

    def row_up(self, x):
        return self.up(x, x.ndim - 2)

    def row_down(self, x):
        return self.down(x, x.ndim - 2)

    def row_valid(self, shape):
        r = row_ids(shape)
        if self.index == 3:
            ok = r < self.n[1]
        else:
            j = jnp.where(r < self.n[1] + 4, r, r - self.rows) + self.l * self.n[1]
            ok = (j >= 0) & (j < WHOLE[self.index][1])
        if self.n[2] < self.lanes:
            ok = ok & (lane_ids(shape) < self.n[2])
        return jnp.where(ok, 1.0, 0.0).astype(F32)

    def plane_valid(self, i):
        p = self.g * self.n[0] + (i - self.low)
        return jnp.where((p >= 0) & (p < WHOLE[self.index][0]), 1.0, 0.0).astype(F32)

    def plane_valid_many(self, lo, hi):
        shape = (hi - lo, self.rows, self.lanes)
        p = self.g * self.n[0] + (lo - self.low) + lax.broadcasted_iota(jnp.int32, shape, 0)
        return jnp.where((p >= 0) & (p < WHOLE[self.index][0]), 1.0, 0.0).astype(F32)

    def cells(self, c):
        cl = c + self.lane_down(c)
        cj = c + self.row_down(c)
        cjl = cl + self.row_down(cl)
        return cl, cj, cjl

    def coefficients(self, cells, before, valid):
        cl, cj, cjl = cells
        pl_, pj, pjl = before
        k = cjl + pjl
        el = cj + pj
        if self.n[2] == self.lanes:
            el = jnp.where(lane_ids(el.shape) == self.n[2] - 1, 0.0, el)
        return cjl, cl + pl_, el, 5.0 * k, valid * (0.15 / jnp.maximum(k, 1.0))

    def parts(self, u):
        ul = self.lane_up(u)
        uj = self.row_up(u)
        a = u + ul
        return ul, uj, a + self.row_up(a)

    def combine(self, u, un, up, ul, uj, t, ei, eip, ej, el, k5):
        tj = t + self.row_down(t)
        b = k5 * u + ei * un + eip * up + ej * uj + el * ul - tj
        return b + self.lane_down(el * u - tj) + self.row_down(ej * u)

    def setup_all(self, lo, hi):
        cl, cj, cjl = self.cells(self.C[lo - 1:hi])
        valid = self.row_valid((1, self.rows, self.lanes)) * self.plane_valid_many(lo, hi)
        ei, ej, el, k5, w = self.coefficients(
            (cl[1:], cj[1:], cjl[1:]), (cl[:-1], cj[:-1], cjl[:-1]), valid
        )
        self.Ei[lo - 1:hi] = cjl
        self.Ej[lo:hi] = ej
        self.El[lo:hi] = el
        self.K5[lo:hi] = k5
        self.W[lo:hi] = w

    def apply_all(self, u_ref, lo, hi):
        u = u_ref[lo - 1:hi + 1]
        ul, uj, v = self.parts(u)
        t = self.C[lo - 1:hi] * (v[:-1] + v[1:])
        return self.combine(
            u[1:-1], u[2:], u[:-2], ul[1:-1], uj[1:-1], t[1:] + t[:-1],
            self.Ei[lo:hi], self.Ei[lo - 1:hi - 1], self.Ej[lo:hi], self.El[lo:hi], self.K5[lo:hi],
        )

    def first_all(self, lo, hi):
        self.U[lo:hi] = self.W[lo:hi] * self.F[lo:hi]

    def sweep_all(self, source, target, lo, hi):
        b = self.apply_all(source, lo, hi)
        target[lo:hi] = source[lo:hi] + self.W[lo:hi] * (self.F[lo:hi] - b)

    def residual_all(self, source, lo, hi):
        return self.F[lo:hi] - self.apply_all(source, lo, hi)

    def planes_loop(self, lo, hi, step, carry, unroll):
        whole = (hi - lo) // unroll

        def body(k, c):
            for m in range(unroll):
                c = step(lo + k * unroll + m, c)
            return c

        carry = lax.fori_loop(0, whole, body, carry)
        for i in range(lo + whole * unroll, hi):
            carry = step(i, carry)
        return carry

    def apply_loop(self, u_ref, lo, hi, emit, unroll):
        _, _, v0 = self.parts(u_ref[lo - 1])
        ul, uj, v = self.parts(u_ref[lo])
        t = self.C[lo - 1] * (v0 + v)

        def step(i, carry):
            ul, uj, v, t = carry
            u = u_ref[i]
            un = u_ref[i + 1]
            uln, ujn, vn = self.parts(un)
            tn = self.C[i] * (v + vn)
            b = self.combine(
                u, un, u_ref[i - 1], ul, uj, t + tn,
                self.Ei[i], self.Ei[i - 1], self.Ej[i], self.El[i], self.K5[i],
            )
            emit(i, u, b)
            return uln, ujn, vn, tn

        self.planes_loop(lo, hi, step, (ul, uj, v, t), unroll)


def kernel(*refs):
    rhs, phase, fine_out, coarse_out = refs[:4]
    refs = refs[4:]
    windows = [refs[9 * k:9 * k + 9] for k in range(4)]
    (
        ph, upk, dpk, rxl0, rxh0, rs, s0, out, ct1, n1, h0,
        rxl1, rxh1, crl1, crh1, c1w, s1, ct2, pf2, pn2, rf2, rn2, n2w, n3s, s2, pf3, pc3, rf3, rc3,
        r0_mat, r1_mat, r2_mat, p0_mat, p1_mat,
        lsem, ss0, rs0, sf1, qf1, sc1, qc1, sf2, qf2, sc2, qc2, sf3, qf3, sc3, qc3,
    ) = refs[36:]
    g = lax.axis_index("grp")
    l = lax.axis_index("loc")
    lv = [Level(k, g, l, windows[k]) for k in range(4)]
    L0, L1, L2, L3 = lv
    sent = []

    def device(dg, dl):
        return lax.rem(g + dg + NG, NG), lax.rem(l + dl + NL, NL)

    def inside(dg, dl):
        tests = [t for t in (
            g + dg >= 0 if dg < 0 else None, g + dg < NG if dg > 0 else None,
            l + dl >= 0 if dl < 0 else None, l + dl < NL if dl > 0 else None,
        ) if t is not None]
        return functools.reduce(jnp.logical_and, tests)

    def run(test, action):
        action() if test is None else pl.when(test)(action)

    class Sent:
        def __init__(self, src, dst, s_sem, r_sem, to, wrap):
            self.copy = pltpu.make_async_remote_copy(
                src_ref=src, dst_ref=dst, send_sem=s_sem, recv_sem=r_sem,
                device_id=device(*to), device_id_type=MESH,
            )
            self.out = None if wrap else inside(*to)
            self.back = None if wrap else inside(-to[0], -to[1])
            run(self.out, self.copy.start)
            sent.append(self)

        def wait_recv(self):
            run(self.back, self.copy.wait_recv)

        def wait_send(self):
            run(self.out, self.copy.wait_send)

    def send(src, dst, s_sem, r_sem, to, wrap=False):
        return Sent(src, dst, s_sem, r_sem, to, wrap)

    load_f = pltpu.make_async_copy(rhs, L0.F.at[4:20, 0:32], lsem.at[0])
    load_p = pltpu.make_async_copy(phase, ph, lsem.at[1])
    load_p.start()
    load_f.start()
    barrier = pltpu.get_barrier_semaphore()
    expected = jnp.int32(0)
    for to in GREET:
        test = inside(*to) if to[0] or to[1] < 0 else None

        def greet(to=to):
            pl.semaphore_signal(barrier, inc=1, device_id=device(*to), device_id_type=MESH)

        run(test, greet)
        expected = expected + (1 if test is None else jnp.where(test, 1, 0))

    def clear(test, *refs):
        @pl.when(test)
        def _():
            for ref in refs:
                ref[...] = jnp.zeros(ref.shape, F32)

    near_tiles = (rxl1, rxh1, crl1, crh1)
    clear(
        g == 0, L0.F.at[0:4, 0:32], L0.C.at[0:4, 0:32], L1.F.at[0:4, 0:16], L1.C.at[0:4, 0:16],
        *[x.at[0:4] for x in (rxl0, rxh0) + near_tiles],
    )
    clear(
        g == NG - 1, L0.F.at[20:22, 0:32], L0.C.at[20:22, 0:32], L1.F.at[12:14, 0:16], L1.C.at[12:14, 0:16],
        *[x.at[20:22] for x in (rxl0, rxh0)], *[x.at[12:14] for x in near_tiles],
    )
    clear(l == 0, rxl0, rxl1, crl1, rf2.at[:, 0], rn2.at[:, 0])
    clear(l == NL - 1, rxh0, rxh1, crh1, rf2.at[:, 2], rn2.at[:, 2])
    for d in (1, 2, 3):
        clear(g < d, rf2.at[3 - d], rn2.at[3 - d])
        clear(g >= NG - d, rf2.at[3 + d], rn2.at[3 + d])

    load_p.wait()
    gas = ph[...].astype(F32)
    L0.C[4:20, 0:32] = 1.0 + 999.0 * gas
    load_f.wait()
    sub = row_ids((1, 8, 256)) < 4
    upk[...] = jnp.where(sub, pltpu.roll(L0.C[4:20, 24:32], 4, 1), L0.F[4:20, 24:32])
    dpk[...] = jnp.where(sub, L0.F[4:20, 0:8], pltpu.roll(L0.C[4:20, 0:8], 4, 1))
    pl.semaphore_wait(barrier, expected)

    first = []
    k = 0
    for src, dst, to in (
        (upk, rxl0.at[4:20], (0, 1)),
        (dpk, rxh0.at[4:20], (0, -1)),
        (L0.C.at[16:20, 0:32], L0.C.at[0:4, 0:32], (1, 0)),
        (L0.F.at[17:20, 0:32], L0.F.at[1:4, 0:32], (1, 0)),
        (L0.C.at[4:6, 0:32], L0.C.at[20:22, 0:32], (-1, 0)),
        (L0.F.at[4:6, 0:32], L0.F.at[20:22, 0:32], (-1, 0)),
        (upk.at[12:16], rxl0.at[0:4], (1, 1)),
        (dpk.at[12:16], rxh0.at[0:4], (1, -1)),
        (upk.at[0:2], rxl0.at[20:22], (-1, 1)),
        (dpk.at[0:2], rxh0.at[20:22], (-1, -1)),
    ):
        first.append(send(src, dst, ss0.at[k], rs0.at[k], to))
        k += 1

    def near_sends(ref, low, high, ssem, rsem, depth):
        copies = []
        for k, (dg, dl) in enumerate(NEAR):
            lo, hi, at = {1: (12 - depth, 12, 4 - depth), 0: (4, 12, 4), -1: (4, 6, 12)}[dg]
            rows, target = {1: (slice(8, 16), low), 0: (slice(0, 16), ref), -1: (slice(0, 8), high)}[dl]
            where = pl.ds(at, hi - lo)
            dst = target.at[where, 0:16] if dl == 0 else target.at[where]
            copies.append(send(ref.at[lo:hi, rows], dst, ssem.at[k], rsem.at[k], (dg, dl)))
        return copies

    def wide_sends(src, slots, ssem, rsem):
        return [
            send(src, slots.at[3 - dg, 1 - dl], ssem.at[k], rsem.at[k], (dg, dl))
            for k, (dg, dl) in enumerate(WIDE)
        ]

    def along_sends(src, slots, ssem, rsem):
        mine = slots.at[lax.div(l, 2), lax.rem(l, 2)]
        return [send(src, mine, ssem.at[k], rsem.at[k], to, True) for k, to in enumerate(ALONG)]

    weights = ((r0_mat, 256), (r1_mat, 128), (r2_mat, 64))
    for ref, used in weights:
        k, c = row_ids(ref.shape), lane_ids(ref.shape)
        near = jnp.abs(k - 2 * c)
        live = (k < used) & (c < used // 2)
        ref[...] = jnp.where(
            live & (near == 0), 0.5, jnp.where(live & (near == 1), 0.25, 0.0)
        ).astype(BF16)
    for ref in (p0_mat, p1_mat):
        half = row_ids(ref.shape) - 2 * lane_ids(ref.shape)
        ref[...] = jnp.where((half == 0) | (half == 1), 1.0, 0.0).astype(BF16)

    pairs = jnp.concatenate([gas[2 * i:2 * i + 1] + gas[2 * i + 1:2 * i + 2] for i in range(8)], 0)
    ct1[...] = jnp.dot(
        pairs.reshape(8 * 32, 256).astype(BF16), p0_mat[...], preferred_element_type=F32
    ).reshape(8, 32, 128)
    n1[...] = ct1[:, pl.ds(0, 16, stride=2), :] + ct1[:, pl.ds(1, 16, stride=2), :]
    count1 = n1[...]
    L1.C[4:12, 0:16] = 1.0 + 124.875 * count1
    pairs = jnp.concatenate([count1[2 * i:2 * i + 1] + count1[2 * i + 1:2 * i + 2] for i in range(4)], 0)
    ct2[...] = jnp.dot(
        pairs.reshape(4 * 16, 128).astype(BF16), p1_mat[...], preferred_element_type=F32
    ).reshape(4, 16, 128)
    count2 = ct2[:, pl.ds(0, 8, stride=2), :] + ct2[:, pl.ds(1, 8, stride=2), :]
    pn2[...] = count2[0:2] + pltpu.roll(count2[2:4], 64, 2)
    rn2[3, 1] = pn2[...]

    for ref in (L3.F, L3.C):
        ref[:, 64:72] = jnp.zeros((PLANES[3], 8, 128), F32)

    got_c1 = near_sends(L1.C, crl1, crh1, sc1, qc1, 4)
    got_c2 = wide_sends(pn2, rn2, sc2, qc2)

    rows0 = L0.row_valid((40, 256))
    sub = row_ids((8, 256)) < 4

    def merge(i, _):
        low, high = rxl0[i], rxh0[i]
        L0.F[i, 32:40] = jnp.where(sub, high, low)
        L0.C[i, 32:40] = pltpu.roll(jnp.where(sub, low, high), 4, 0) * rows0[32:40] * L0.plane_valid(i)
        return 0

    def setup(i, before):
        cells = L0.cells(L0.C[i])
        ei, ej, el, k5, w = L0.coefficients(cells, before, rows0 * L0.plane_valid(i))
        L0.Ei[i], L0.Ej[i], L0.El[i], L0.K5[i], L0.W[i] = ei, ej, el, k5, w
        L0.U[i] = w * (12.0 * L0.F[i])
        return cells

    def second(i, u, b):
        L0.V[i] = u + L0.W[i] * (12.0 * L0.F[i] - b)

    def residual(i, u, b):
        r = (12.0 * L0.F[i] - b) * (rows0 * L0.plane_valid(i))
        for half in range(2):
            lanes = slice(128 * half, 128 * half + 128)
            rs[i - 3, half, 0:8] = r[32:40, lanes]
            rs[i - 3, half, 8:40] = r[0:32, lanes]
        out[jnp.maximum(i - 4, 0)] = r[0:32] * (1.0 / 12.0)

    def setup_planes(lo, hi):
        before = L0.cells(L0.C[lo - 1])
        L0.Ei[lo - 1] = before[2]
        L0.planes_loop(lo, hi, setup, before, 3)

    for copy in first[:2]:
        copy.wait_recv()
    lax.fori_loop(4, 20, merge, 0)
    setup_planes(5, 20)
    L0.apply_loop(L0.U, 6, 19, second, 3)
    for copy in first[2:]:
        copy.wait_recv()
    for i in (0, 1, 2, 3, 20, 21):
        merge(i, 0)
        L0.C[i, 0:32] = L0.C[i, 0:32] * L0.plane_valid(i)
    setup_planes(1, 5)
    setup_planes(20, 22)
    L0.apply_loop(L0.U, 2, 6, second, 4)
    L0.apply_loop(L0.U, 19, 21, second, 2)
    L0.apply_loop(L0.V, 3, 20, residual, 3)
    store = pltpu.make_async_copy(out, fine_out, lsem.at[2])
    store.start()

    def coarser_planes(r):
        return [0.5 * (r[2 * i] + r[2 * i + 2]) + r[2 * i + 1] for i in range((r.shape[0] - 1) // 2)]

    def coarser_rows(ref, kept):
        return 0.5 * (
            ref[:, pl.ds(7, kept, stride=2), :] + ref[:, pl.ds(9, kept, stride=2), :]
        ) + ref[:, pl.ds(8, kept, stride=2), :]

    total = jnp.zeros((8 * 16, 128), F32)
    for half in range(2):
        for i, plane in enumerate(coarser_planes(rs[:, half])):
            s0[half, i] = plane
        total = total + split_dot(
            coarser_rows(s0.at[half], 16).reshape(8 * 16, 128), r0_mat[128 * half:128 * half + 128]
        )
    L1.F[4:12, 0:16] = total.reshape(8, 16, 128)
    got_f1 = near_sends(L1.F, rxl1, rxh1, sf1, qf1, 3)

    for copy in got_c1:
        copy.wait_recv()
    sub1 = row_ids((1, 8, 128)) < 4
    valid1 = L1.row_valid((1, 24, 128)) * L1.plane_valid_many(0, 14)
    c1w[:, 0:16] = L1.C[:, 0:16] * valid1[:, 0:16]
    c1w[:, 16:24] = jnp.where(sub1, crh1[...], crl1[...]) * valid1[:, 16:24]
    L1.C = c1w
    L1.setup_all(1, 14)

    def unpack_wide(slots, put):
        lane = lane_ids((1, 1, 1, 128)) < 64
        own = slots[:, 1]
        halo = jnp.where(row_ids((1, 1, 8, 128)) < 4, slots[:, 2], slots[:, 0])
        for tile, rows in ((own, slice(0, 8)), (halo, slice(8, 16))):
            first = jnp.where(lane, tile, 0.0)
            later = jnp.where(lane, pltpu.roll(tile, 64, 3), 0.0)
            for d in range(7):
                for half in range(2):
                    put(4 * d + half, rows, first[d, half])
                    put(4 * d + 2 + half, rows, later[d, half])

    for copy in got_c2:
        copy.wait_recv()

    def put_n2(i, rows, value):
        n2w[i, rows] = value

    unpack_wide(rn2, put_n2)
    valid2 = L2.row_valid((1, 16, 128)) * L2.plane_valid_many(0, 28)
    L2.C[...] = (1.0 + (999.0 / 64.0) * n2w[...]) * valid2
    L2.setup_all(1, 26)

    count2 = n2w[2:24, 0:8]
    pairs = jnp.concatenate([count2[2 * i:2 * i + 1] + count2[2 * i + 1:2 * i + 2] for i in range(11)], 0)
    n3s[...] = jnp.dot(
        pairs.reshape(11 * 8, 128).astype(BF16), p1_mat[...], preferred_element_type=F32
    ).reshape(11, 8, 128)
    count3 = n3s[:, pl.ds(0, 4, stride=2), :] + n3s[:, pl.ds(1, 4, stride=2), :]

    odd = lax.rem(l, 2) == 1

    def pack(planes, ref):
        for t in range(2):
            for h in range(2):
                total = jnp.zeros((4, 128), F32)
                for q in range(4):
                    p = 8 * t + 4 * h + q
                    if p < len(planes):
                        total = total + (pltpu.roll(planes[p], 32 * q, 1) if q else planes[p])
                ref[t, 4 * h:4 * h + 4] = total
        tiles = ref[...]
        ref[...] = jnp.where(odd, pltpu.roll(tiles, 4, 1), tiles)

    def unpack_along(slots, count, put):
        sub = row_ids((1, 8, 128)) < 4
        lane = lane_ids((1, 8, 128)) < 32
        for p in range(count):
            t, h, q = p // 8, (p % 8) // 4, p % 4
            even, other = slots[:, 0, t], slots[:, 1, t]
            tile = jnp.where(sub, even, other) if h == 0 else pltpu.roll(jnp.where(sub, other, even), 4, 1)
            if q:
                tile = pltpu.roll(tile, 128 - 32 * q, 2)
            put(p, jnp.where(lane, tile, 0.0).reshape(64, 128))

    pack([count3[i] for i in range(11)], pc3)
    rc3[lax.div(l, 2), lax.rem(l, 2)] = pc3[...]
    got_c3 = along_sends(pc3, rc3, sc3, qc3)

    for copy in got_f1:
        copy.wait_recv()
    L1.F[1:14, 16:24] = jnp.where(sub1, rxh1[1:14], rxl1[1:14])
    L1.first_all(1, 14)
    L1.sweep_all(L1.U, L1.V, 2, 13)
    r1 = L1.residual_all(L1.V, 3, 12) * valid1[3:12]
    r1 = jnp.concatenate([r1[:, 16:24], r1[:, 0:16]], 1)
    for i, plane in enumerate(coarser_planes(r1)):
        s1[i] = plane
    f2 = split_dot(coarser_rows(s1, 8).reshape(4 * 8, 128), r1_mat[...]).reshape(4, 8, 128)
    pf2[...] = f2[0:2] + pltpu.roll(f2[2:4], 64, 2)
    rf2[3, 1] = pf2[...]
    got_f2 = wide_sends(pf2, rf2, sf2, qf2)

    for copy in got_c3:
        copy.wait_recv()

    def put_c3(p, value):
        L3.C[p, 0:64] = (1.0 + (999.0 / 512.0) * value) * (
            L3.row_valid((72, 128))[0:64] * L3.plane_valid(p)
        )

    unpack_along(rc3, 11, put_c3)
    L3.setup_all(1, 11)

    for copy in got_f2:
        copy.wait_recv()

    def put_f2(i, rows, value):
        L2.F[i, rows] = value

    unpack_wide(rf2, put_f2)
    L2.first_all(1, 26)
    L2.sweep_all(L2.U, L2.V, 2, 25)
    r2 = L2.residual_all(L2.V, 3, 24) * valid2[3:24]
    for i, plane in enumerate(coarser_planes(r2)):
        s2[i, 0:8] = plane[8:16]
        s2[i, 8:24] = plane
    f3 = split_dot(coarser_rows(s2, 8).reshape(10 * 8, 128), r2_mat[...]).reshape(10, 8, 128)
    pack([f3[i, 0:4] for i in range(10)], pf3)
    rf3[lax.div(l, 2), lax.rem(l, 2)] = pf3[...]
    got_f3 = along_sends(pf3, rf3, sf3, qf3)
    for copy in got_f3:
        copy.wait_recv()

    def put_f3(p, value):
        L3.F[p + 1, 0:64] = value

    unpack_along(rf3, 10, put_f3)
    L3.first_all(1, 11)
    source, target = L3.U, L3.V
    for sweep in range(COARSE_SWEEPS - 1):
        L3.sweep_all(source, target, 2 + sweep, 10 - sweep)
        source, target = target, source
    last = (8.0 / 12.0) * L3.residual_all(source, 5, 7)
    for i in range(2):
        coarse_out[i] = jnp.transpose(last[i, 0:64], (1, 0))[0:32]

    store.wait()
    for copy in sent:
        copy.wait_send()


def per_device(right_side, phase):
    scratch = []
    for k in range(4):
        shape = (PLANES[k], ROWS[k], LANES[k])
        scratch += [pltpu.VMEM(shape, F32) for _ in range(9)]
    scratch += [
        pltpu.VMEM(s, d)
        for s, d in (
            ((16, 32, 256), jnp.int32),
            ((16, 8, 256), F32), ((16, 8, 256), F32),
            ((22, 8, 256), F32), ((22, 8, 256), F32),
            ((17, 2, 40, 128), F32), ((2, 8, 40, 128), F32),
            ((16, 32, 256), F32),
            ((8, 32, 128), F32), ((8, 16, 128), F32), ((17, 16, 128), F32),
            ((14, 8, 128), F32), ((14, 8, 128), F32), ((14, 8, 128), F32), ((14, 8, 128), F32),
            ((14, 24, 128), F32),
            ((4, 24, 128), F32),
            ((4, 16, 128), F32),
            ((2, 8, 128), F32), ((2, 8, 128), F32),
            ((7, 3, 2, 8, 128), F32), ((7, 3, 2, 8, 128), F32),
            ((28, 16, 128), F32), ((11, 8, 128), F32), ((10, 24, 128), F32),
            ((2, 8, 128), F32), ((2, 8, 128), F32),
            ((8, 2, 2, 8, 128), F32), ((8, 2, 2, 8, 128), F32),
            ((256, 128), BF16), ((128, 128), BF16), ((128, 128), BF16),
            ((256, 128), BF16), ((128, 128), BF16),
        )
    ]
    scratch.append(pltpu.SemaphoreType.DMA((3,)))
    for n in (10, len(NEAR), len(NEAR), len(WIDE), len(WIDE), len(ALONG), len(ALONG)):
        scratch += [pltpu.SemaphoreType.DMA((n,)), pltpu.SemaphoreType.DMA((n,))]
    vmem = pl.BlockSpec(memory_space=pltpu.VMEM)
    hbm = pl.BlockSpec(memory_space=pl.ANY)
    fine, coarse = pl.pallas_call(
        kernel,
        out_shape=(
            jax.ShapeDtypeStruct((16, 32, 256), F32),
            jax.ShapeDtypeStruct((2, 32, 64), F32),
        ),
        in_specs=[hbm, hbm],
        out_specs=(hbm, vmem),
        scratch_shapes=scratch,
        compiler_params=pltpu.CompilerParams(
            collective_id=0, has_side_effects=True, vmem_limit_bytes=24 * 2**20
        ),
    )(pltpu.with_memory_space_constraint(right_side, pltpu.HBM), pltpu.with_memory_space_constraint(phase, pltpu.HBM))
    return fine, jnp.transpose(coarse, (0, 2, 1))


def solution(mesh):
    in_specs = (P("grp", "loc", None), P("grp", "loc", None))
    out_specs = (P("grp", "loc", None), P("grp", None, None))
    return jax.shard_map(
        per_device, mesh=mesh, in_specs=in_specs, out_specs=out_specs, check_vma=False
    )
```

```python
import functools

import jax
import jax.numpy as jnp
from jax import lax
from jax.experimental import pallas as pl
from jax.experimental.pallas import tpu as pltpu
from jax.sharding import PartitionSpec as P

MESH = pl.DeviceIdType.MESH
NG, NL = 16, 16
COARSE_SWEEPS = 4
F32 = jnp.float32
BF16 = jnp.bfloat16
WHOLE = ((256, 512, 256), (128, 256, 128), (64, 128, 64), (32, 64, 32))
BLOCK = ((16, 32, 256), (8, 16, 128), (4, 8, 64), (2, 64, 32))
LOW = (4, 4, 12, 5)
PLANES = (22, 14, 28, 11)
ROWS = (40, 24, 16, 72)
LANES = (256, 128, 128, 128)

NEAR = [(a, b) for a in (-1, 0, 1) for b in (-1, 0, 1) if (a, b) != (0, 0)]
WIDE = [(a, b) for c in (3, 2, 1, 0) for a in (-c, c)[:1 + (c > 0)] for b in (-1, 1, 0) if (a, b) != (0, 0)]
ALONG = [(0, k) for k in (10, 9, 11, 6, 5, 7, 14, 13, 2, 8, 3, 15, 12, 4, 1)]


def lane_ids(shape):
    return lax.broadcasted_iota(jnp.int32, shape, len(shape) - 1)


def row_ids(shape):
    return lax.broadcasted_iota(jnp.int32, shape, len(shape) - 2)


def split_dot(values, matrix):
    high = values.astype(BF16)
    rest = values - high.astype(F32)
    mid = rest.astype(BF16)
    low = (rest - mid.astype(F32)).astype(BF16)
    dot = functools.partial(jnp.dot, preferred_element_type=F32)
    return dot(high, matrix) + (dot(mid, matrix) + dot(low, matrix))


class Level:
    def __init__(self, index, g, l, refs):
        self.index = index
        self.F, self.C, self.U, self.V, self.Ei, self.Ej, self.El, self.K5, self.W = refs
        self.n = BLOCK[index]
        self.low = LOW[index]
        self.rows, self.lanes = ROWS[index], LANES[index]
        self.g, self.l = g, l

    def up(self, x, axis):
        return pltpu.roll(x, x.shape[axis] - 1, axis)

    def down(self, x, axis):
        return pltpu.roll(x, 1, axis)

    def lane_up(self, x):
        y = self.up(x, x.ndim - 1)
        return jnp.where(lane_ids(y.shape) == self.n[2] - 1, 0.0, y) if self.n[2] == self.lanes else y

    def lane_down(self, x):
        y = self.down(x, x.ndim - 1)
        return jnp.where(lane_ids(y.shape) == 0, 0.0, y) if self.n[2] == self.lanes else y

    def row_up(self, x):
        return self.up(x, x.ndim - 2)

    def row_down(self, x):
        return self.down(x, x.ndim - 2)

    def row_valid(self, shape):
        r = row_ids(shape)
        if self.index == 3:
            ok = r < self.n[1]
        else:
            j = jnp.where(r < self.n[1] + 4, r, r - self.rows) + self.l * self.n[1]
            ok = (j >= 0) & (j < WHOLE[self.index][1])
        if self.n[2] < self.lanes:
            ok = ok & (lane_ids(shape) < self.n[2])
        return jnp.where(ok, 1.0, 0.0).astype(F32)

    def plane_valid(self, i):
        p = self.g * self.n[0] + (i - self.low)
        return jnp.where((p >= 0) & (p < WHOLE[self.index][0]), 1.0, 0.0).astype(F32)

    def plane_valid_many(self, lo, hi):
        shape = (hi - lo, self.rows, self.lanes)
        p = self.g * self.n[0] + (lo - self.low) + lax.broadcasted_iota(jnp.int32, shape, 0)
        return jnp.where((p >= 0) & (p < WHOLE[self.index][0]), 1.0, 0.0).astype(F32)

    def cells(self, c):
        cl = c + self.lane_down(c)
        cj = c + self.row_down(c)
        cjl = cl + self.row_down(cl)
        return cl, cj, cjl

    def coefficients(self, cells, before, valid):
        cl, cj, cjl = cells
        pl_, pj, pjl = before
        k = cjl + pjl
        el = cj + pj
        if self.n[2] == self.lanes:
            el = jnp.where(lane_ids(el.shape) == self.n[2] - 1, 0.0, el)
        return cjl, cl + pl_, el, 5.0 * k, valid * (0.15 / jnp.maximum(k, 1.0))

    def parts(self, u):
        ul = self.lane_up(u)
        uj = self.row_up(u)
        a = u + ul
        return ul, uj, a + self.row_up(a)

    def combine(self, u, un, up, ul, uj, t, ei, eip, ej, el, k5):
        tj = t + self.row_down(t)
        b = k5 * u + ei * un + eip * up + ej * uj + el * ul - tj
        return b + self.lane_down(el * u - tj) + self.row_down(ej * u)

    def setup_all(self, lo, hi):
        cl, cj, cjl = self.cells(self.C[lo - 1:hi])
        valid = self.row_valid((1, self.rows, self.lanes)) * self.plane_valid_many(lo, hi)
        ei, ej, el, k5, w = self.coefficients(
            (cl[1:], cj[1:], cjl[1:]), (cl[:-1], cj[:-1], cjl[:-1]), valid
        )
        self.Ei[lo - 1:hi] = cjl
        self.Ej[lo:hi] = ej
        self.El[lo:hi] = el
        self.K5[lo:hi] = k5
        self.W[lo:hi] = w

    def apply_all(self, u_ref, lo, hi):
        u = u_ref[lo - 1:hi + 1]
        ul, uj, v = self.parts(u)
        t = self.C[lo - 1:hi] * (v[:-1] + v[1:])
        return self.combine(
            u[1:-1], u[2:], u[:-2], ul[1:-1], uj[1:-1], t[1:] + t[:-1],
            self.Ei[lo:hi], self.Ei[lo - 1:hi - 1], self.Ej[lo:hi], self.El[lo:hi], self.K5[lo:hi],
        )

    def first_all(self, lo, hi):
        self.U[lo:hi] = self.W[lo:hi] * self.F[lo:hi]

    def sweep_all(self, source, target, lo, hi):
        b = self.apply_all(source, lo, hi)
        target[lo:hi] = source[lo:hi] + self.W[lo:hi] * (self.F[lo:hi] - b)

    def residual_all(self, source, lo, hi):
        return self.F[lo:hi] - self.apply_all(source, lo, hi)

    def planes_loop(self, lo, hi, step, carry, unroll):
        whole = (hi - lo) // unroll

        def body(k, c):
            for m in range(unroll):
                c = step(lo + k * unroll + m, c)
            return c

        carry = lax.fori_loop(0, whole, body, carry)
        for i in range(lo + whole * unroll, hi):
            carry = step(i, carry)
        return carry

    def apply_loop(self, u_ref, lo, hi, emit, unroll):
        _, _, v0 = self.parts(u_ref[lo - 1])
        ul, uj, v = self.parts(u_ref[lo])
        t = self.C[lo - 1] * (v0 + v)

        def step(i, carry):
            ul, uj, v, t = carry
            u = u_ref[i]
            un = u_ref[i + 1]
            uln, ujn, vn = self.parts(un)
            tn = self.C[i] * (v + vn)
            b = self.combine(
                u, un, u_ref[i - 1], ul, uj, t + tn,
                self.Ei[i], self.Ei[i - 1], self.Ej[i], self.El[i], self.K5[i],
            )
            emit(i, u, b)
            return uln, ujn, vn, tn

        self.planes_loop(lo, hi, step, (ul, uj, v, t), unroll)


def kernel(*refs):
    rhs, phase, fine_out, coarse_out = refs[:4]
    refs = refs[4:]
    windows = [refs[9 * k:9 * k + 9] for k in range(4)]
    (
        ph, upk, dpk, rxl0, rxh0, rs, s0, out, ct1, n1, h0,
        rxl1, rxh1, crl1, crh1, c1w, s1, ct2, pf2, pn2, rf2, rn2, n2w, n3s, s2, pf3, pc3, rf3, rc3,
        r0_mat, r1_mat, r2_mat, p0_mat, p1_mat,
        lsem, known, ss0, rs0, sf1, qf1, sc1, qc1, sf2, qf2, sc2, qc2, sf3, qf3, sc3, qc3,
    ) = refs[36:]
    g = lax.axis_index("grp")
    l = lax.axis_index("loc")
    lv = [Level(k, g, l, windows[k]) for k in range(4)]
    L0, L1, L2, L3 = lv
    sent = []

    def device(dg, dl):
        return lax.rem(g + dg + NG, NG), lax.rem(l + dl + NL, NL)

    def inside(dg, dl):
        tests = [t for t in (
            g + dg >= 0 if dg < 0 else None, g + dg < NG if dg > 0 else None,
            l + dl >= 0 if dl < 0 else None, l + dl < NL if dl > 0 else None,
        ) if t is not None]
        return functools.reduce(jnp.logical_and, tests)

    def run(test, action):
        action() if test is None else pl.when(test)(action)

    class Sent:
        def __init__(self, src, dst, s_sem, r_sem, to, wrap):
            self.copy = pltpu.make_async_remote_copy(
                src_ref=src, dst_ref=dst, send_sem=s_sem, recv_sem=r_sem,
                device_id=device(*to), device_id_type=MESH,
            )
            self.out = None if wrap else inside(*to)
            self.back = None if wrap else inside(-to[0], -to[1])
            run(self.out, self.copy.start)
            sent.append(self)

        def wait_recv(self):
            run(self.back, self.copy.wait_recv)

        def wait_send(self):
            run(self.out, self.copy.wait_send)

    def send(src, dst, s_sem, r_sem, to, wrap=False):
        return Sent(src, dst, s_sem, r_sem, to, wrap)

    load_f = pltpu.make_async_copy(rhs, L0.F.at[4:20, 0:32], lsem.at[0])
    load_p = pltpu.make_async_copy(phase, ph, lsem.at[1])
    load_p.start()
    load_f.start()
    barrier = pltpu.get_barrier_semaphore()
    def greet(sem, targets):
        count = jnp.int32(0)
        for to in targets:
            test = inside(*to)

            def signal(to=to):
                pl.semaphore_signal(sem, inc=1, device_id=device(*to), device_id_type=MESH)

            run(test, signal)
            count = count + jnp.where(test, 1, 0)
        return count

    around = greet(barrier, NEAR)

    def clear(test, *refs):
        @pl.when(test)
        def _():
            for ref in refs:
                ref[...] = jnp.zeros(ref.shape, F32)

    near_tiles = (rxl1, rxh1, crl1, crh1)
    clear(
        g == 0, L0.F.at[0:4, 0:32], L0.C.at[0:4, 0:32], L1.F.at[0:4, 0:16], L1.C.at[0:4, 0:16],
        *[x.at[0:4] for x in (rxl0, rxh0) + near_tiles],
    )
    clear(
        g == NG - 1, L0.F.at[20:22, 0:32], L0.C.at[20:22, 0:32], L1.F.at[12:14, 0:16], L1.C.at[12:14, 0:16],
        *[x.at[20:22] for x in (rxl0, rxh0)], *[x.at[12:14] for x in near_tiles],
    )
    clear(l == 0, rxl0, rxl1, crl1, rf2.at[:, 0], rn2.at[:, 0])
    clear(l == NL - 1, rxh0, rxh1, crh1, rf2.at[:, 2], rn2.at[:, 2])
    for d in (1, 2, 3):
        clear(g < d, rf2.at[3 - d], rn2.at[3 - d])
        clear(g >= NG - d, rf2.at[3 + d], rn2.at[3 + d])

    load_p.wait()
    gas = ph[...].astype(F32)
    L0.C[4:20, 0:32] = 1.0 + 999.0 * gas
    load_f.wait()
    sub = row_ids((1, 8, 256)) < 4
    upk[...] = jnp.where(sub, pltpu.roll(L0.C[4:20, 24:32], 4, 1), L0.F[4:20, 24:32])
    dpk[...] = jnp.where(sub, L0.F[4:20, 0:8], pltpu.roll(L0.C[4:20, 0:8], 4, 1))
    pl.semaphore_wait(barrier, around)

    first = []
    k = 0
    for src, dst, to in (
        (upk.at[0:8], rxl0.at[4:12], (0, 1)),
        (dpk.at[0:8], rxh0.at[4:12], (0, -1)),
        (upk.at[8:16], rxl0.at[12:20], (0, 1)),
        (dpk.at[8:16], rxh0.at[12:20], (0, -1)),
        (L0.C.at[16:20, 0:32], L0.C.at[0:4, 0:32], (1, 0)),
        (L0.F.at[17:20, 0:32], L0.F.at[1:4, 0:32], (1, 0)),
        (L0.C.at[4:6, 0:32], L0.C.at[20:22, 0:32], (-1, 0)),
        (L0.F.at[4:6, 0:32], L0.F.at[20:22, 0:32], (-1, 0)),
        (upk.at[12:16], rxl0.at[0:4], (1, 1)),
        (dpk.at[12:16], rxh0.at[0:4], (1, -1)),
        (upk.at[0:2], rxl0.at[20:22], (-1, 1)),
        (dpk.at[0:2], rxh0.at[20:22], (-1, -1)),
    ):
        first.append(send(src, dst, ss0.at[k], rs0.at[k], to))
        k += 1

    def near_sends(ref, low, high, ssem, rsem, depth):
        copies = []
        for k, (dg, dl) in enumerate(NEAR):
            lo, hi, at = {1: (12 - depth, 12, 4 - depth), 0: (4, 12, 4), -1: (4, 6, 12)}[dg]
            rows, target = {1: (slice(8, 16), low), 0: (slice(0, 16), ref), -1: (slice(0, 8), high)}[dl]
            where = pl.ds(at, hi - lo)
            dst = target.at[where, 0:16] if dl == 0 else target.at[where]
            copies.append(send(ref.at[lo:hi, rows], dst, ssem.at[k], rsem.at[k], (dg, dl)))
        return copies

    def wide_sends(src, slots, ssem, rsem):
        return [
            send(src, slots.at[3 - dg, 1 - dl], ssem.at[k], rsem.at[k], (dg, dl))
            for k, (dg, dl) in enumerate(WIDE)
        ]

    def along_sends(src, slots, ssem, rsem):
        mine = slots.at[lax.div(l, 2), lax.rem(l, 2)]
        return [send(src, mine, ssem.at[k], rsem.at[k], to, True) for k, to in enumerate(ALONG)]

    greet(known.at[0], NEAR)

    weights = ((r0_mat, 256), (r1_mat, 128), (r2_mat, 64))
    for ref, used in weights:
        k, c = row_ids(ref.shape), lane_ids(ref.shape)
        near = jnp.abs(k - 2 * c)
        live = (k < used) & (c < used // 2)
        ref[...] = jnp.where(
            live & (near == 0), 0.5, jnp.where(live & (near == 1), 0.25, 0.0)
        ).astype(BF16)
    for ref in (p0_mat, p1_mat):
        half = row_ids(ref.shape) - 2 * lane_ids(ref.shape)
        ref[...] = jnp.where((half == 0) | (half == 1), 1.0, 0.0).astype(BF16)

    pairs = jnp.concatenate([gas[2 * i:2 * i + 1] + gas[2 * i + 1:2 * i + 2] for i in range(8)], 0)
    ct1[...] = jnp.dot(
        pairs.reshape(8 * 32, 256).astype(BF16), p0_mat[...], preferred_element_type=F32
    ).reshape(8, 32, 128)
    n1[...] = ct1[:, pl.ds(0, 16, stride=2), :] + ct1[:, pl.ds(1, 16, stride=2), :]
    count1 = n1[...]
    L1.C[4:12, 0:16] = 1.0 + 124.875 * count1
    pairs = jnp.concatenate([count1[2 * i:2 * i + 1] + count1[2 * i + 1:2 * i + 2] for i in range(4)], 0)
    ct2[...] = jnp.dot(
        pairs.reshape(4 * 16, 128).astype(BF16), p1_mat[...], preferred_element_type=F32
    ).reshape(4, 16, 128)
    count2 = ct2[:, pl.ds(0, 8, stride=2), :] + ct2[:, pl.ds(1, 8, stride=2), :]
    pn2[...] = count2[0:2] + pltpu.roll(count2[2:4], 64, 2)
    rn2[3, 1] = pn2[...]

    for ref in (L3.F, L3.C):
        ref[:, 64:72] = jnp.zeros((PLANES[3], 8, 128), F32)

    got_c1 = near_sends(L1.C, crl1, crh1, sc1, qc1, 4)
    pl.semaphore_wait(known.at[0], around)
    known_1 = greet(known.at[1], [(-1, 0), (1, 0)])
    known_2 = greet(known.at[2], [(0, -2), (0, 2)])

    rows0 = L0.row_valid((40, 256))
    sub = row_ids((8, 256)) < 4

    def merge(i, _):
        low, high = rxl0[i], rxh0[i]
        L0.F[i, 32:40] = jnp.where(sub, high, low)
        L0.C[i, 32:40] = pltpu.roll(jnp.where(sub, low, high), 4, 0) * rows0[32:40] * L0.plane_valid(i)
        return 0

    def setup(i, before):
        cells = L0.cells(L0.C[i])
        ei, ej, el, k5, w = L0.coefficients(cells, before, rows0 * L0.plane_valid(i))
        L0.Ei[i], L0.Ej[i], L0.El[i], L0.K5[i], L0.W[i] = ei, ej, el, k5, w
        L0.U[i] = w * (12.0 * L0.F[i])
        return cells

    def second(i, u, b):
        L0.V[i] = u + L0.W[i] * (12.0 * L0.F[i] - b)

    def residual(i, u, b):
        r = (12.0 * L0.F[i] - b) * (rows0 * L0.plane_valid(i))
        for half in range(2):
            lanes = slice(128 * half, 128 * half + 128)
            rs[i - 3, half, 0:8] = r[32:40, lanes]
            rs[i - 3, half, 8:40] = r[0:32, lanes]
        out[jnp.maximum(i - 4, 0)] = r[0:32] * (1.0 / 12.0)

    def setup_planes(lo, hi):
        before = L0.cells(L0.C[lo - 1])
        L0.Ei[lo - 1] = before[2]
        L0.planes_loop(lo, hi, setup, before, 8)

    for copy in first[:2]:
        copy.wait_recv()
    lax.fori_loop(4, 12, merge, 0)
    setup_planes(5, 12)
    L0.apply_loop(L0.U, 6, 11, second, 6)
    for copy in first[2:4]:
        copy.wait_recv()
    lax.fori_loop(12, 20, merge, 0)
    setup_planes(12, 20)
    L0.apply_loop(L0.U, 11, 19, second, 4)
    L0.apply_loop(L0.V, 7, 18, residual, 6)
    for copy in first[4:]:
        copy.wait_recv()
    for i in (0, 1, 2, 3, 20, 21):
        merge(i, 0)
        L0.C[i, 0:32] = L0.C[i, 0:32] * L0.plane_valid(i)
    setup_planes(1, 5)
    setup_planes(20, 22)
    L0.apply_loop(L0.U, 2, 6, second, 4)
    L0.apply_loop(L0.U, 19, 21, second, 4)
    L0.apply_loop(L0.V, 3, 7, residual, 4)
    L0.apply_loop(L0.V, 18, 20, residual, 4)
    store = pltpu.make_async_copy(out, fine_out, lsem.at[2])
    store.start()

    def coarser_planes(r):
        return [0.5 * (r[2 * i] + r[2 * i + 2]) + r[2 * i + 1] for i in range((r.shape[0] - 1) // 2)]

    def coarser_rows(ref, kept):
        return 0.5 * (
            ref[:, pl.ds(7, kept, stride=2), :] + ref[:, pl.ds(9, kept, stride=2), :]
        ) + ref[:, pl.ds(8, kept, stride=2), :]

    total = jnp.zeros((8 * 16, 128), F32)
    for half in range(2):
        for i, plane in enumerate(coarser_planes(rs[:, half])):
            s0[half, i] = plane
        total = total + split_dot(
            coarser_rows(s0.at[half], 16).reshape(8 * 16, 128), r0_mat[128 * half:128 * half + 128]
        )
    L1.F[4:12, 0:16] = total.reshape(8, 16, 128)
    got_f1 = near_sends(L1.F, rxl1, rxh1, sf1, qf1, 3)

    pl.semaphore_wait(known.at[1], known_1)
    pl.semaphore_wait(known.at[2], known_2)
    known_3 = greet(known.at[3], [(0, -4), (0, 4)])
    got_c2 = wide_sends(pn2, rn2, sc2, qc2)

    for copy in got_c1:
        copy.wait_recv()
    sub1 = row_ids((1, 8, 128)) < 4
    valid1 = L1.row_valid((1, 24, 128)) * L1.plane_valid_many(0, 14)
    c1w[:, 0:16] = L1.C[:, 0:16] * valid1[:, 0:16]
    c1w[:, 16:24] = jnp.where(sub1, crh1[...], crl1[...]) * valid1[:, 16:24]
    L1.C = c1w
    L1.setup_all(1, 14)

    pl.semaphore_wait(known.at[3], known_3)
    known_4 = greet(known.at[4], [(0, -8), (0, 8)])

    for copy in got_f1:
        copy.wait_recv()
    L1.F[1:14, 16:24] = jnp.where(sub1, rxh1[1:14], rxl1[1:14])
    L1.first_all(1, 14)
    L1.sweep_all(L1.U, L1.V, 2, 13)
    r1 = L1.residual_all(L1.V, 3, 12) * valid1[3:12]
    r1 = jnp.concatenate([r1[:, 16:24], r1[:, 0:16]], 1)
    for i, plane in enumerate(coarser_planes(r1)):
        s1[i] = plane
    f2 = split_dot(coarser_rows(s1, 8).reshape(4 * 8, 128), r1_mat[...]).reshape(4, 8, 128)
    pf2[...] = f2[0:2] + pltpu.roll(f2[2:4], 64, 2)
    rf2[3, 1] = pf2[...]
    got_f2 = wide_sends(pf2, rf2, sf2, qf2)

    pl.semaphore_wait(known.at[4], known_4)

    def unpack_wide(slots, put):
        lane = lane_ids((1, 1, 1, 128)) < 64
        own = slots[:, 1]
        halo = jnp.where(row_ids((1, 1, 8, 128)) < 4, slots[:, 2], slots[:, 0])
        for tile, rows in ((own, slice(0, 8)), (halo, slice(8, 16))):
            first = jnp.where(lane, tile, 0.0)
            later = jnp.where(lane, pltpu.roll(tile, 64, 3), 0.0)
            for d in range(7):
                for half in range(2):
                    put(4 * d + half, rows, first[d, half])
                    put(4 * d + 2 + half, rows, later[d, half])

    for copy in got_c2:
        copy.wait_recv()

    def put_n2(i, rows, value):
        n2w[i, rows] = value

    unpack_wide(rn2, put_n2)
    valid2 = L2.row_valid((1, 16, 128)) * L2.plane_valid_many(0, 28)
    L2.C[...] = (1.0 + (999.0 / 64.0) * n2w[...]) * valid2
    L2.setup_all(1, 26)

    count2 = n2w[2:24, 0:8]
    pairs = jnp.concatenate([count2[2 * i:2 * i + 1] + count2[2 * i + 1:2 * i + 2] for i in range(11)], 0)
    n3s[...] = jnp.dot(
        pairs.reshape(11 * 8, 128).astype(BF16), p1_mat[...], preferred_element_type=F32
    ).reshape(11, 8, 128)
    count3 = n3s[:, pl.ds(0, 4, stride=2), :] + n3s[:, pl.ds(1, 4, stride=2), :]

    odd = lax.rem(l, 2) == 1

    def pack(planes, ref):
        for t in range(2):
            for h in range(2):
                total = jnp.zeros((4, 128), F32)
                for q in range(4):
                    p = 8 * t + 4 * h + q
                    if p < len(planes):
                        total = total + (pltpu.roll(planes[p], 32 * q, 1) if q else planes[p])
                ref[t, 4 * h:4 * h + 4] = total
        tiles = ref[...]
        ref[...] = jnp.where(odd, pltpu.roll(tiles, 4, 1), tiles)

    def unpack_along(slots, count, put):
        sub = row_ids((1, 8, 128)) < 4
        lane = lane_ids((1, 8, 128)) < 32
        for p in range(count):
            t, h, q = p // 8, (p % 8) // 4, p % 4
            even, other = slots[:, 0, t], slots[:, 1, t]
            tile = jnp.where(sub, even, other) if h == 0 else pltpu.roll(jnp.where(sub, other, even), 4, 1)
            if q:
                tile = pltpu.roll(tile, 128 - 32 * q, 2)
            put(p, jnp.where(lane, tile, 0.0).reshape(64, 128))

    pack([count3[i] for i in range(11)], pc3)
    rc3[lax.div(l, 2), lax.rem(l, 2)] = pc3[...]
    got_c3 = along_sends(pc3, rc3, sc3, qc3)

    for copy in got_f2:
        copy.wait_recv()

    def put_f2(i, rows, value):
        L2.F[i, rows] = value

    unpack_wide(rf2, put_f2)
    L2.first_all(1, 26)
    L2.sweep_all(L2.U, L2.V, 2, 25)
    r2 = L2.residual_all(L2.V, 3, 24) * valid2[3:24]
    for i, plane in enumerate(coarser_planes(r2)):
        s2[i, 0:8] = plane[8:16]
        s2[i, 8:24] = plane
    f3 = split_dot(coarser_rows(s2, 8).reshape(10 * 8, 128), r2_mat[...]).reshape(10, 8, 128)
    pack([f3[i, 0:4] for i in range(10)], pf3)
    rf3[lax.div(l, 2), lax.rem(l, 2)] = pf3[...]
    got_f3 = along_sends(pf3, rf3, sf3, qf3)

    for copy in got_c3:
        copy.wait_recv()

    def put_c3(p, value):
        L3.C[p, 0:64] = (1.0 + (999.0 / 512.0) * value) * (
            L3.row_valid((72, 128))[0:64] * L3.plane_valid(p)
        )

    unpack_along(rc3, 11, put_c3)
    L3.setup_all(1, 11)

    for copy in got_f3:
        copy.wait_recv()

    def put_f3(p, value):
        L3.F[p + 1, 0:64] = value

    unpack_along(rf3, 10, put_f3)
    L3.first_all(1, 11)
    source, target = L3.U, L3.V
    for sweep in range(COARSE_SWEEPS - 1):
        L3.sweep_all(source, target, 2 + sweep, 10 - sweep)
        source, target = target, source
    last = (8.0 / 12.0) * L3.residual_all(source, 5, 7)
    for i in range(2):
        coarse_out[i] = jnp.transpose(last[i, 0:64], (1, 0))[0:32]

    store.wait()
    for copy in sent:
        copy.wait_send()


def per_device(right_side, phase):
    scratch = []
    for k in range(4):
        shape = (PLANES[k], ROWS[k], LANES[k])
        scratch += [pltpu.VMEM(shape, F32) for _ in range(9)]
    scratch += [
        pltpu.VMEM(s, d)
        for s, d in (
            ((16, 32, 256), jnp.int32),
            ((16, 8, 256), F32), ((16, 8, 256), F32),
            ((22, 8, 256), F32), ((22, 8, 256), F32),
            ((17, 2, 40, 128), F32), ((2, 8, 40, 128), F32),
            ((16, 32, 256), F32),
            ((8, 32, 128), F32), ((8, 16, 128), F32), ((17, 16, 128), F32),
            ((14, 8, 128), F32), ((14, 8, 128), F32), ((14, 8, 128), F32), ((14, 8, 128), F32),
            ((14, 24, 128), F32),
            ((4, 24, 128), F32),
            ((4, 16, 128), F32),
            ((2, 8, 128), F32), ((2, 8, 128), F32),
            ((7, 3, 2, 8, 128), F32), ((7, 3, 2, 8, 128), F32),
            ((28, 16, 128), F32), ((11, 8, 128), F32), ((10, 24, 128), F32),
            ((2, 8, 128), F32), ((2, 8, 128), F32),
            ((8, 2, 2, 8, 128), F32), ((8, 2, 2, 8, 128), F32),
            ((256, 128), BF16), ((128, 128), BF16), ((128, 128), BF16),
            ((256, 128), BF16), ((128, 128), BF16),
        )
    ]
    scratch += [pltpu.SemaphoreType.DMA((3,)), pltpu.SemaphoreType.REGULAR((5,))]
    for n in (12, len(NEAR), len(NEAR), len(WIDE), len(WIDE), len(ALONG), len(ALONG)):
        scratch += [pltpu.SemaphoreType.DMA((n,)), pltpu.SemaphoreType.DMA((n,))]
    vmem = pl.BlockSpec(memory_space=pltpu.VMEM)
    hbm = pl.BlockSpec(memory_space=pl.ANY)
    fine, coarse = pl.pallas_call(
        kernel,
        out_shape=(
            jax.ShapeDtypeStruct((16, 32, 256), F32),
            jax.ShapeDtypeStruct((2, 32, 64), F32),
        ),
        in_specs=[hbm, hbm],
        out_specs=(hbm, vmem),
        scratch_shapes=scratch,
        compiler_params=pltpu.CompilerParams(
            collective_id=0, has_side_effects=True, vmem_limit_bytes=24 * 2**20
        ),
    )(pltpu.with_memory_space_constraint(right_side, pltpu.HBM), pltpu.with_memory_space_constraint(phase, pltpu.HBM))
    return fine, jnp.transpose(coarse, (0, 2, 1))


def solution(mesh):
    in_specs = (P("grp", "loc", None), P("grp", "loc", None))
    out_specs = (P("grp", "loc", None), P("grp", None, None))
    return jax.shard_map(
        per_device, mesh=mesh, in_specs=in_specs, out_specs=out_specs, check_vma=False
    )
```

```python
import functools

import jax
import jax.numpy as jnp
from jax import lax
from jax.experimental import pallas as pl
from jax.experimental.pallas import tpu as pltpu
from jax.sharding import PartitionSpec as P

MESH = pl.DeviceIdType.MESH
NG, NL = 16, 16
COARSE_SWEEPS = 4
F32 = jnp.float32
BF16 = jnp.bfloat16
WHOLE = ((256, 512, 256), (128, 256, 128), (64, 128, 64), (32, 64, 32))
BLOCK = ((16, 32, 256), (8, 16, 128), (4, 8, 64), (2, 64, 32))
LOW = (4, 4, 12, 5)
PLANES = (22, 14, 28, 11)
ROWS = (40, 32, 16, 16)
LANES = (256, 128, 128, 128)

NEAR = [(a, b) for a in (-1, 0, 1) for b in (-1, 0, 1) if (a, b) != (0, 0)]
WIDE = [(a, 0) for a in (-3, 3, -2, 2, -1, 1)]
ALONG = [(0, k) for k in (10, 9, 11, 6, 5, 7, 14, 13, 2, 8, 3, 15, 12, 4, 1)]


def lane_ids(shape):
    return lax.broadcasted_iota(jnp.int32, shape, len(shape) - 1)


def row_ids(shape):
    return lax.broadcasted_iota(jnp.int32, shape, len(shape) - 2)


def split_dot(values, matrix):
    high = values.astype(BF16)
    rest = values - high.astype(F32)
    mid = rest.astype(BF16)
    low = (rest - mid.astype(F32)).astype(BF16)
    dot = functools.partial(jnp.dot, preferred_element_type=F32)
    return dot(high, matrix) + (dot(mid, matrix) + dot(low, matrix))


class Level:
    def __init__(self, index, g, l, refs):
        self.index = index
        self.F, self.C, self.U, self.V, self.Ei, self.Ej, self.El, self.K5, self.W = refs
        self.n = BLOCK[index]
        self.low = LOW[index]
        self.rows, self.lanes = ROWS[index], LANES[index]
        self.edges = index != 2
        self.g, self.l = g, l

    def up(self, x, axis):
        return pltpu.roll(x, x.shape[axis] - 1, axis)

    def down(self, x, axis):
        return pltpu.roll(x, 1, axis)

    def lane_up(self, x):
        y = self.up(x, x.ndim - 1)
        return jnp.where(self.at_end(y.shape), 0.0, y) if self.edges else y

    def lane_down(self, x):
        y = self.down(x, x.ndim - 1)
        return jnp.where(self.at_start(y.shape), 0.0, y) if self.edges else y

    def own_lane(self, shape):
        lane = lane_ids(shape)
        return lane & (self.n[2] - 1) if self.index == 3 else lane

    def at_start(self, shape):
        return self.own_lane(shape) == 0

    def at_end(self, shape):
        return self.own_lane(shape) == self.n[2] - 1

    def row_up(self, x):
        y = self.up(x, x.ndim - 2)
        if self.index < 3:
            return y
        tile = y[:, 8:16]
        after = jnp.where(lane_ids(tile.shape) < 96, pltpu.roll(tile, 96, 2), 0.0)
        return jnp.concatenate([y[:, 0:8], jnp.where(row_ids(tile.shape) == 7, after, tile)], 1)

    def row_down(self, x):
        y = self.down(x, x.ndim - 2)
        if self.index < 3:
            return y
        tile = y[:, 0:8]
        before = jnp.where(lane_ids(tile.shape) >= 32, pltpu.roll(tile, 32, 2), 0.0)
        return jnp.concatenate([jnp.where(row_ids(tile.shape) == 0, before, tile), y[:, 8:16]], 1)

    def row_valid(self, shape):
        r = row_ids(shape)
        if self.index == 3:
            return jnp.ones(shape, F32)
        ahead = self.n[1] + (4, 6, 4)[self.index]
        j = jnp.where(r < ahead, r, r - self.rows) + self.l * self.n[1]
        ok = (j >= 0) & (j < WHOLE[self.index][1])
        if self.n[2] < self.lanes:
            ok = ok & (lane_ids(shape) < self.n[2])
        return jnp.where(ok, 1.0, 0.0).astype(F32)

    def plane_valid(self, i):
        p = self.g * self.n[0] + (i - self.low)
        return jnp.where((p >= 0) & (p < WHOLE[self.index][0]), 1.0, 0.0).astype(F32)

    def plane_valid_many(self, lo, hi):
        shape = (hi - lo, self.rows, self.lanes)
        p = self.g * self.n[0] + (lo - self.low) + lax.broadcasted_iota(jnp.int32, shape, 0)
        return jnp.where((p >= 0) & (p < WHOLE[self.index][0]), 1.0, 0.0).astype(F32)

    def cells(self, c):
        cl = c + self.lane_down(c)
        cj = c + self.row_down(c)
        cjl = cl + self.row_down(cl)
        return cl, cj, cjl

    def coefficients(self, cells, before, valid):
        cl, cj, cjl = cells
        pl_, pj, pjl = before
        k = cjl + pjl
        el = cj + pj
        if self.edges:
            el = jnp.where(self.at_end(el.shape), 0.0, el)
        return cjl, cl + pl_, el, 5.0 * k, valid * (0.15 / jnp.maximum(k, 1.0))

    def parts(self, u):
        ul = self.lane_up(u)
        uj = self.row_up(u)
        a = u + ul
        return ul, uj, a + self.row_up(a)

    def combine(self, u, un, up, ul, uj, t, ei, eip, ej, el, k5):
        tj = t + self.row_down(t)
        b = k5 * u + ei * un + eip * up + ej * uj + el * ul - tj
        return b + self.lane_down(el * u - tj) + self.row_down(ej * u)

    def setup_all(self, lo, hi):
        cl, cj, cjl = self.cells(self.C[lo - 1:hi])
        valid = self.row_valid((1, self.rows, self.lanes)) * self.plane_valid_many(lo, hi)
        ei, ej, el, k5, w = self.coefficients(
            (cl[1:], cj[1:], cjl[1:]), (cl[:-1], cj[:-1], cjl[:-1]), valid
        )
        self.Ei[lo - 1:hi] = cjl
        self.Ej[lo:hi] = ej
        self.El[lo:hi] = el
        self.K5[lo:hi] = k5
        self.W[lo:hi] = w

    def apply_all(self, u_ref, lo, hi):
        u = u_ref[lo - 1:hi + 1]
        ul, uj, v = self.parts(u)
        t = self.C[lo - 1:hi] * (v[:-1] + v[1:])
        return self.combine(
            u[1:-1], u[2:], u[:-2], ul[1:-1], uj[1:-1], t[1:] + t[:-1],
            self.Ei[lo:hi], self.Ei[lo - 1:hi - 1], self.Ej[lo:hi], self.El[lo:hi], self.K5[lo:hi],
        )

    def first_all(self, lo, hi):
        self.U[lo:hi] = self.W[lo:hi] * self.F[lo:hi]

    def sweep_all(self, source, target, lo, hi):
        b = self.apply_all(source, lo, hi)
        target[lo:hi] = source[lo:hi] + self.W[lo:hi] * (self.F[lo:hi] - b)

    def residual_all(self, source, lo, hi):
        return self.F[lo:hi] - self.apply_all(source, lo, hi)

    def planes_loop(self, lo, hi, step, carry, unroll):
        whole = (hi - lo) // unroll

        def body(k, c):
            for m in range(unroll):
                c = step(lo + k * unroll + m, c)
            return c

        carry = lax.fori_loop(0, whole, body, carry)
        for i in range(lo + whole * unroll, hi):
            carry = step(i, carry)
        return carry

    def apply_loop(self, u_ref, lo, hi, emit, unroll):
        _, _, v0 = self.parts(u_ref[lo - 1])
        ul, uj, v = self.parts(u_ref[lo])
        t = self.C[lo - 1] * (v0 + v)

        def step(i, carry):
            ul, uj, v, t = carry
            u = u_ref[i]
            un = u_ref[i + 1]
            uln, ujn, vn = self.parts(un)
            tn = self.C[i] * (v + vn)
            b = self.combine(
                u, un, u_ref[i - 1], ul, uj, t + tn,
                self.Ei[i], self.Ei[i - 1], self.Ej[i], self.El[i], self.K5[i],
            )
            emit(i, u, b)
            return uln, ujn, vn, tn

        self.planes_loop(lo, hi, step, (ul, uj, v, t), unroll)


def kernel(*refs):
    rhs, phase, fine_out, coarse_out = refs[:4]
    refs = refs[4:]
    windows = [refs[9 * k:9 * k + 9] for k in range(4)]
    (
        ph, upk, dpk, rxl0, rxh0, rs, s0, out, ct1, n1, h0,
        rxl1, rxh1, crl1, crh1, c1w, s1, ct2, pf2, pn2, rf2, rn2, n2w, n3s, s2, pf3, pc3, rf3, rc3,
        r0_mat, r1_mat, r2_mat, p0_mat, p1_mat,
        lsem, known, ss0, rs0, sf1, qf1, sc1, qc1, sf2, qf2, sc2, qc2, sf3, qf3, sc3, qc3,
    ) = refs[36:]
    g = lax.axis_index("grp")
    l = lax.axis_index("loc")
    lv = [Level(k, g, l, windows[k]) for k in range(4)]
    L0, L1, L2, L3 = lv
    sent = []

    def device(dg, dl):
        return lax.rem(g + dg + NG, NG), lax.rem(l + dl + NL, NL)

    def inside(dg, dl):
        tests = [t for t in (
            g + dg >= 0 if dg < 0 else None, g + dg < NG if dg > 0 else None,
            l + dl >= 0 if dl < 0 else None, l + dl < NL if dl > 0 else None,
        ) if t is not None]
        return functools.reduce(jnp.logical_and, tests)

    def run(test, action):
        action() if test is None else pl.when(test)(action)

    class Sent:
        def __init__(self, src, dst, s_sem, r_sem, to, wrap):
            self.copy = pltpu.make_async_remote_copy(
                src_ref=src, dst_ref=dst, send_sem=s_sem, recv_sem=r_sem,
                device_id=device(*to), device_id_type=MESH,
            )
            self.out = None if wrap else inside(*to)
            self.back = None if wrap else inside(-to[0], -to[1])
            run(self.out, self.copy.start)
            sent.append(self)

        def wait_recv(self):
            run(self.back, self.copy.wait_recv)

        def wait_send(self):
            run(self.out, self.copy.wait_send)

    def send(src, dst, s_sem, r_sem, to, wrap=False):
        return Sent(src, dst, s_sem, r_sem, to, wrap)

    def flush(copies):
        for copy in copies:
            copy.wait_send()

    load_f = pltpu.make_async_copy(rhs, L0.F.at[4:20, 0:32], lsem.at[0])
    load_p = pltpu.make_async_copy(phase, ph, lsem.at[1])
    load_p.start()
    load_f.start()
    barrier = pltpu.get_barrier_semaphore()
    def greet(sem, targets):
        count = jnp.int32(0)
        for to in targets:
            test = inside(*to)

            def signal(to=to):
                pl.semaphore_signal(sem, inc=1, device_id=device(*to), device_id_type=MESH)

            run(test, signal)
            count = count + jnp.where(test, 1, 0)
        return count

    around = greet(barrier, NEAR)

    def clear(test, *refs):
        @pl.when(test)
        def _():
            for ref in refs:
                ref[...] = jnp.zeros(ref.shape, F32)

    near_tiles = (rxl1, rxh1, crl1, crh1)
    clear(
        g == 0, L0.F.at[0:4, 0:32], L0.C.at[0:4, 0:32], L1.F.at[0:4, 0:16], L1.C.at[0:4, 0:16],
        *[x.at[0:4] for x in (rxl0, rxh0) + near_tiles],
    )
    clear(
        g == NG - 1, L0.F.at[20:22, 0:32], L0.C.at[20:22, 0:32], L1.F.at[12:14, 0:16], L1.C.at[12:14, 0:16],
        *[x.at[20:22] for x in (rxl0, rxh0)], *[x.at[12:14] for x in near_tiles],
    )
    clear(l == 0, rxl0, rxl1, crl1)
    clear(l == NL - 1, rxh0, rxh1, crh1)
    for d in (1, 2, 3):
        clear(g < d, rf2.at[3 - d], rn2.at[3 - d])
        clear(g >= NG - d, rf2.at[3 + d], rn2.at[3 + d])

    load_p.wait()
    gas = ph[...].astype(F32)
    L0.C[4:20, 0:32] = 1.0 + 999.0 * gas
    load_f.wait()
    sub = row_ids((1, 8, 256)) < 4
    upk[...] = jnp.where(sub, pltpu.roll(L0.C[4:20, 24:32], 4, 1), L0.F[4:20, 24:32])
    dpk[...] = jnp.where(sub, L0.F[4:20, 0:8], pltpu.roll(L0.C[4:20, 0:8], 4, 1))
    pl.semaphore_wait(barrier, around)

    first = []
    k = 0
    for src, dst, to in (
        (upk.at[0:8], rxl0.at[4:12], (0, 1)),
        (dpk.at[0:8], rxh0.at[4:12], (0, -1)),
        (upk.at[8:16], rxl0.at[12:20], (0, 1)),
        (dpk.at[8:16], rxh0.at[12:20], (0, -1)),
        (L0.C.at[16:20, 0:32], L0.C.at[0:4, 0:32], (1, 0)),
        (L0.F.at[17:20, 0:32], L0.F.at[1:4, 0:32], (1, 0)),
        (L0.C.at[4:6, 0:32], L0.C.at[20:22, 0:32], (-1, 0)),
        (L0.F.at[4:6, 0:32], L0.F.at[20:22, 0:32], (-1, 0)),
        (upk.at[12:16], rxl0.at[0:4], (1, 1)),
        (dpk.at[12:16], rxh0.at[0:4], (1, -1)),
        (upk.at[0:2], rxl0.at[20:22], (-1, 1)),
        (dpk.at[0:2], rxh0.at[20:22], (-1, -1)),
    ):
        first.append(send(src, dst, ss0.at[k], rs0.at[k], to))
        k += 1

    def near_sends(ref, low, high, ssem, rsem, depth):
        copies = []
        for k, (dg, dl) in enumerate(NEAR):
            lo, hi, at = {1: (12 - depth, 12, 4 - depth), 0: (4, 12, 4), -1: (4, 6, 12)}[dg]
            rows, target = {1: (slice(0, 16), low), 0: (slice(0, 16), ref), -1: (slice(0, 8), high)}[dl]
            where = pl.ds(at, hi - lo)
            dst = target.at[where, 0:16] if dl == 0 else target.at[where]
            copies.append(send(ref.at[lo:hi, rows], dst, ssem.at[k], rsem.at[k], (dg, dl)))
        return copies

    def wide_sends(src, slots, ssem, rsem):
        return [
            send(src, slots.at[3 - dg], ssem.at[k], rsem.at[k], (dg, dl))
            for k, (dg, dl) in enumerate(WIDE)
        ]

    def along_sends(src, slots, ssem, rsem):
        for to in ALONG:
            pltpu.make_async_remote_copy(
                src_ref=src, dst_ref=slots.at[l], send_sem=ssem.at[0], recv_sem=rsem.at[0],
                device_id=device(*to), device_id_type=MESH,
            ).start()
        whole = slots.at[0:NL - 1]
        return [pltpu.make_async_copy(whole, whole, sem.at[0]) for sem in (rsem, ssem)]

    greet(known.at[0], NEAR)

    weights = ((r0_mat, 256), (r1_mat, 128), (r2_mat, 64))
    for ref, used in weights:
        k, c = row_ids(ref.shape), lane_ids(ref.shape)
        near = jnp.abs(k - 2 * c)
        live = (k < used) & (c < used // 2)
        ref[...] = jnp.where(
            live & (near == 0), 0.5, jnp.where(live & (near == 1), 0.25, 0.0)
        ).astype(BF16)
    for ref in (p0_mat, p1_mat):
        half = row_ids(ref.shape) - 2 * lane_ids(ref.shape)
        ref[...] = jnp.where((half == 0) | (half == 1), 1.0, 0.0).astype(BF16)

    pairs = jnp.concatenate([gas[2 * i:2 * i + 1] + gas[2 * i + 1:2 * i + 2] for i in range(8)], 0)
    ct1[...] = jnp.dot(
        pairs.reshape(8 * 32, 256).astype(BF16), p0_mat[...], preferred_element_type=F32
    ).reshape(8, 32, 128)
    n1[...] = ct1[:, pl.ds(0, 16, stride=2), :] + ct1[:, pl.ds(1, 16, stride=2), :]
    count1 = n1[...]
    L1.C[4:12, 0:16] = count1
    got_c1 = near_sends(L1.C, crl1, crh1, sc1, qc1, 4)
    pl.semaphore_wait(known.at[0], around)
    known_1 = greet(known.at[1], [(-1, 0), (1, 0)])
    known_2 = greet(known.at[2], [(0, -2), (0, 2)])

    rows0 = L0.row_valid((40, 256))
    sub = row_ids((8, 256)) < 4

    def merge(i, _):
        low, high = rxl0[i], rxh0[i]
        L0.F[i, 32:40] = jnp.where(sub, high, low)
        L0.C[i, 32:40] = pltpu.roll(jnp.where(sub, low, high), 4, 0) * rows0[32:40] * L0.plane_valid(i)
        return 0

    def setup(i, before):
        cells = L0.cells(L0.C[i])
        ei, ej, el, k5, w = L0.coefficients(cells, before, rows0 * L0.plane_valid(i))
        L0.Ei[i], L0.Ej[i], L0.El[i], L0.K5[i], L0.W[i] = ei, ej, el, k5, w
        L0.U[i] = w * (12.0 * L0.F[i])
        return cells

    def second(i, u, b):
        L0.V[i] = u + L0.W[i] * (12.0 * L0.F[i] - b)

    def residual(i, u, b):
        r = (12.0 * L0.F[i] - b) * (rows0 * L0.plane_valid(i))
        for half in range(2):
            lanes = slice(128 * half, 128 * half + 128)
            rs[i - 3, half, 0:8] = r[32:40, lanes]
            rs[i - 3, half, 8:40] = r[0:32, lanes]
        out[jnp.maximum(i - 4, 0)] = r[0:32] * (1.0 / 12.0)

    def setup_planes(lo, hi):
        before = L0.cells(L0.C[lo - 1])
        L0.Ei[lo - 1] = before[2]
        L0.planes_loop(lo, hi, setup, before, 8)

    for copy in first[:2]:
        copy.wait_recv()
    lax.fori_loop(4, 12, merge, 0)
    setup_planes(5, 12)
    L0.apply_loop(L0.U, 6, 11, second, 6)
    for copy in first[2:4]:
        copy.wait_recv()
    lax.fori_loop(12, 20, merge, 0)
    setup_planes(12, 20)
    L0.apply_loop(L0.U, 11, 19, second, 4)
    L0.apply_loop(L0.V, 7, 18, residual, 6)
    for copy in first[4:]:
        copy.wait_recv()
    for i in (0, 1, 2, 3, 20, 21):
        merge(i, 0)
        L0.C[i, 0:32] = L0.C[i, 0:32] * L0.plane_valid(i)
    setup_planes(1, 5)
    setup_planes(20, 22)
    L0.apply_loop(L0.U, 2, 6, second, 4)
    L0.apply_loop(L0.U, 19, 21, second, 4)
    L0.apply_loop(L0.V, 3, 7, residual, 4)
    L0.apply_loop(L0.V, 18, 20, residual, 4)
    store = pltpu.make_async_copy(out, fine_out, lsem.at[2])
    store.start()

    def coarser_planes(r):
        return [0.5 * (r[2 * i] + r[2 * i + 2]) + r[2 * i + 1] for i in range((r.shape[0] - 1) // 2)]

    def coarser_rows(ref, kept):
        return 0.5 * (
            ref[:, pl.ds(7, kept, stride=2), :] + ref[:, pl.ds(9, kept, stride=2), :]
        ) + ref[:, pl.ds(8, kept, stride=2), :]

    total = jnp.zeros((8 * 16, 128), F32)
    for half in range(2):
        for i, plane in enumerate(coarser_planes(rs[:, half])):
            s0[half, i] = plane
        total = total + split_dot(
            coarser_rows(s0.at[half], 16).reshape(8 * 16, 128), r0_mat[128 * half:128 * half + 128]
        )
    L1.F[4:12, 0:16] = total.reshape(8, 16, 128)
    earlier, sent[:] = sent[:], []
    got_f1 = near_sends(L1.F, rxl1, rxh1, sf1, qf1, 3)

    pl.semaphore_wait(known.at[1], known_1)
    pl.semaphore_wait(known.at[2], known_2)
    known_3 = greet(known.at[3], [(0, -4), (0, 4)])

    for copy in got_c1:
        copy.wait_recv()
    def merge_rows(ref, low, high, lo, hi):
        inner = row_ids((1, 8, 128)) < 6
        ref[lo:hi, 16:24] = jnp.where(inner, high[lo:hi], low[lo:hi, 0:8])
        ref[lo:hi, 24:32] = low[lo:hi, 8:16]

    merge_rows(L1.C, crl1, crh1, 0, 14)
    for i in range(4):
        s1[i, 0:32] = L1.C[2 * i + 4] + L1.C[2 * i + 5]
    pairs = s1[:, pl.ds(0, 16, stride=2), :] + s1[:, pl.ds(1, 16, stride=2), :]
    count2 = jnp.dot(
        pairs.reshape(4 * 16, 128).astype(BF16), p1_mat[...], preferred_element_type=F32
    ).reshape(4, 16, 128)
    pn2[...] = count2[0:2] + pltpu.roll(count2[2:4], 64, 2)
    rn2[3] = pn2[...]
    got_c2 = wide_sends(pn2, rn2, sc2, qc2)
    valid1 = L1.row_valid((1, 32, 128)) * L1.plane_valid_many(0, 14)
    c1w[...] = (1.0 + 124.875 * L1.C[...]) * valid1
    L1.C = c1w
    L1.setup_all(1, 14)

    flush(earlier)
    pl.semaphore_wait(known.at[3], known_3)
    known_4 = greet(known.at[4], [(0, -8), (0, 8)])

    for copy in got_f1:
        copy.wait_recv()
    merge_rows(L1.F, rxl1, rxh1, 1, 14)
    L1.first_all(1, 14)
    L1.sweep_all(L1.U, L1.V, 2, 13)
    r1 = L1.residual_all(L1.V, 3, 12) * valid1[3:12]
    for i, plane in enumerate(coarser_planes(r1)):
        s1[i, 0:8] = plane[24:32]
        s1[i, 8:40] = plane
    f2 = split_dot(coarser_rows(s1, 16).reshape(4 * 16, 128), r1_mat[...]).reshape(4, 16, 128)
    pf2[...] = f2[0:2] + pltpu.roll(f2[2:4], 64, 2)
    rf2[3] = pf2[...]
    earlier, sent[:] = sent[:], []
    got_f2 = wide_sends(pf2, rf2, sf2, qf2)

    pl.semaphore_wait(known.at[4], known_4)

    def unpack_wide(slots, ref):
        lane = lane_ids((1, 1, 1, 128)) < 64
        tiles = slots[...]
        first = jnp.where(lane, tiles, 0.0)
        later = jnp.where(lane, pltpu.roll(tiles, 64, 3), 0.0)
        for d in range(7):
            ref[4 * d:4 * d + 2] = first[d]
            ref[4 * d + 2:4 * d + 4] = later[d]

    for copy in got_c2:
        copy.wait_recv()

    unpack_wide(rn2, n2w)
    valid2 = L2.row_valid((1, 16, 128)) * L2.plane_valid_many(0, 28)
    L2.C[...] = (1.0 + (999.0 / 64.0) * n2w[...]) * valid2
    L2.setup_all(1, 26)

    count2 = n2w[2:24, 0:8]
    pairs = jnp.concatenate([count2[2 * i:2 * i + 1] + count2[2 * i + 1:2 * i + 2] for i in range(11)], 0)
    n3s[...] = jnp.dot(
        pairs.reshape(11 * 8, 128).astype(BF16), p1_mat[...], preferred_element_type=F32
    ).reshape(11, 8, 128)
    count3 = n3s[:, pl.ds(0, 4, stride=2), :] + n3s[:, pl.ds(1, 4, stride=2), :]

    def pack(planes, ref):
        for t in range(2):
            for h in range(2):
                total = jnp.zeros((4, 128), F32)
                for q in range(4):
                    p = 8 * t + 4 * h + q
                    if p < len(planes):
                        total = total + (pltpu.roll(planes[p], 32 * q, 1) if q else planes[p])
                ref[t, 4 * h:4 * h + 4] = total
        tiles = ref[...]
        tiles = jnp.where(lax.rem(l, 2) == 1, pltpu.roll(tiles, 4, 1), tiles)
        tiles = jnp.where(lax.rem(lax.div(l, 4), 2) == 1, pltpu.roll(tiles, 32, 2), tiles)
        ref[...] = jnp.where(l >= 8, pltpu.roll(tiles, 64, 2), tiles)

    def unpack_along(slots, count, put):
        half, group = row_ids((8, 128)) // 4, lane_ids((8, 128)) // 32
        cell = [[(half == h) & (group == q) for q in range(4)] for h in range(2)]
        for p in range(count):
            t, h, q = p // 8, (p % 8) // 4, p % 4
            for tile in range(2):
                total = slots[2 * tile, t]
                for owner in range(1, 8):
                    e, o = owner % 2, owner // 2
                    total = jnp.where(cell[(h + e) % 2][(q + o) % 4], slots[4 * o + 2 * tile + e, t], total)
                if h:
                    total = pltpu.roll(total, 4, 0)
                if q:
                    total = pltpu.roll(total, 128 - 32 * q, 1)
                put(p, slice(8 * tile, 8 * tile + 8), total)

    pack([count3[i] for i in range(11)], pc3)
    rc3[l] = pc3[...]
    got_c3 = along_sends(pc3, rc3, sc3, qc3)
    flush(earlier)

    for copy in got_f2:
        copy.wait_recv()

    unpack_wide(rf2, L2.F)
    L2.first_all(1, 26)
    L2.sweep_all(L2.U, L2.V, 2, 25)
    r2 = L2.residual_all(L2.V, 3, 24) * valid2[3:24]
    for i, plane in enumerate(coarser_planes(r2)):
        s2[i, 0:8] = plane[8:16]
        s2[i, 8:24] = plane
    f3 = split_dot(coarser_rows(s2, 8).reshape(10 * 8, 128), r2_mat[...]).reshape(10, 8, 128)
    pack([f3[i, 0:4] for i in range(10)], pf3)
    rf3[l] = pf3[...]
    earlier = sent[:]
    got_f3 = along_sends(pf3, rf3, sf3, qf3)

    flush(earlier)
    got_c3[0].wait()

    def put_c3(p, rows, value):
        L3.C[p, rows] = (1.0 + (999.0 / 512.0) * value) * L3.plane_valid(p)

    unpack_along(rc3, 11, put_c3)
    L3.setup_all(1, 11)

    got_f3[0].wait()

    def put_f3(p, rows, value):
        L3.F[p + 1, rows] = value

    unpack_along(rf3, 10, put_f3)
    L3.first_all(1, 11)
    source, target = L3.U, L3.V
    for sweep in range(COARSE_SWEEPS - 1):
        L3.sweep_all(source, target, 2 + sweep, 10 - sweep)
        source, target = target, source
    last = (8.0 / 12.0) * L3.residual_all(source, 5, 7)
    for i in range(2):
        turned = jnp.transpose(last[i], (1, 0))
        coarse_out[i] = jnp.concatenate([turned[32 * q:32 * q + 32] for q in range(4)], 1)

    store.wait()
    got_c3[1].wait()
    got_f3[1].wait()


def per_device(right_side, phase):
    scratch = []
    for k in range(4):
        shape = (PLANES[k], ROWS[k], LANES[k])
        scratch += [pltpu.VMEM(shape, F32) for _ in range(9)]
    scratch += [
        pltpu.VMEM(s, d)
        for s, d in (
            ((16, 32, 256), jnp.int32),
            ((16, 8, 256), F32), ((16, 8, 256), F32),
            ((22, 8, 256), F32), ((22, 8, 256), F32),
            ((17, 2, 40, 128), F32), ((2, 8, 40, 128), F32),
            ((16, 32, 256), F32),
            ((8, 32, 128), F32), ((8, 16, 128), F32), ((17, 16, 128), F32),
            ((14, 16, 128), F32), ((14, 8, 128), F32), ((14, 16, 128), F32), ((14, 8, 128), F32),
            ((14, 32, 128), F32),
            ((4, 40, 128), F32),
            ((4, 16, 128), F32),
            ((2, 16, 128), F32), ((2, 16, 128), F32),
            ((7, 2, 16, 128), F32), ((7, 2, 16, 128), F32),
            ((28, 16, 128), F32), ((11, 8, 128), F32), ((10, 24, 128), F32),
            ((2, 8, 128), F32), ((2, 8, 128), F32),
            ((16, 2, 8, 128), F32), ((16, 2, 8, 128), F32),
            ((256, 128), BF16), ((128, 128), BF16), ((128, 128), BF16),
            ((256, 128), BF16), ((128, 128), BF16),
        )
    ]
    scratch += [pltpu.SemaphoreType.DMA((3,)), pltpu.SemaphoreType.REGULAR((5,))]
    for n in (12, len(NEAR), len(NEAR), len(WIDE), len(WIDE), 1, 1):
        scratch += [pltpu.SemaphoreType.DMA((n,)), pltpu.SemaphoreType.DMA((n,))]
    vmem = pl.BlockSpec(memory_space=pltpu.VMEM)
    hbm = pl.BlockSpec(memory_space=pl.ANY)
    fine, coarse = pl.pallas_call(
        kernel,
        out_shape=(
            jax.ShapeDtypeStruct((16, 32, 256), F32),
            jax.ShapeDtypeStruct((2, 32, 64), F32),
        ),
        in_specs=[hbm, hbm],
        out_specs=(hbm, vmem),
        scratch_shapes=scratch,
        compiler_params=pltpu.CompilerParams(
            collective_id=0, has_side_effects=True, vmem_limit_bytes=24 * 2**20
        ),
    )(pltpu.with_memory_space_constraint(right_side, pltpu.HBM), pltpu.with_memory_space_constraint(phase, pltpu.HBM))
    return fine, jnp.transpose(coarse, (0, 2, 1))


def solution(mesh):
    in_specs = (P("grp", "loc", None), P("grp", "loc", None))
    out_specs = (P("grp", "loc", None), P("grp", None, None))
    return jax.shard_map(
        per_device, mesh=mesh, in_specs=in_specs, out_specs=out_specs, check_vma=False
    )
```

```python
import functools

import jax
import jax.numpy as jnp
from jax import lax
from jax.experimental import pallas as pl
from jax.experimental.pallas import tpu as pltpu
from jax.sharding import PartitionSpec as P

MESH = pl.DeviceIdType.MESH
NG, NL = 16, 16
COARSE_SWEEPS = 4
F32 = jnp.float32
BF16 = jnp.bfloat16
WHOLE = ((256, 512, 256), (128, 256, 128), (64, 128, 64), (32, 64, 32))
BLOCK = ((16, 32, 256), (8, 16, 128), (4, 8, 64), (2, 64, 32))
LOW = (4, 4, 12, 5)
PLANES = (22, 14, 28, 11)
ROWS = (40, 32, 16, 16)
LANES = (256, 128, 128, 128)

NEAR = [(a, b) for a in (-1, 0, 1) for b in (-1, 0, 1) if (a, b) != (0, 0)]
FACES = [(0, 1), (0, -1), (1, 0), (-1, 0)]
WIDE = [(a, 0) for a in (-3, 3, -2, 2, -1, 1)]
ALONG = [(0, k) for k in (10, 9, 11, 6, 5, 7, 14, 13, 2, 8, 3, 15, 12, 4, 1)]


def lane_ids(shape):
    return lax.broadcasted_iota(jnp.int32, shape, len(shape) - 1)


def row_ids(shape):
    return lax.broadcasted_iota(jnp.int32, shape, len(shape) - 2)


def split_dot(values, matrix):
    high = values.astype(BF16)
    rest = values - high.astype(F32)
    mid = rest.astype(BF16)
    low = (rest - mid.astype(F32)).astype(BF16)
    dot = functools.partial(jnp.dot, preferred_element_type=F32)
    return dot(high, matrix) + (dot(mid, matrix) + dot(low, matrix))


class Level:
    def __init__(self, index, g, l, refs):
        self.index = index
        self.F, self.C, self.U, self.V, self.Ei, self.Ej, self.El, self.K5, self.W = refs
        self.n = BLOCK[index]
        self.low = LOW[index]
        self.rows, self.lanes = ROWS[index], LANES[index]
        self.edges = index != 2
        self.g, self.l = g, l

    def up(self, x, axis):
        return pltpu.roll(x, x.shape[axis] - 1, axis)

    def down(self, x, axis):
        return pltpu.roll(x, 1, axis)

    def lane_up(self, x):
        y = self.up(x, x.ndim - 1)
        return jnp.where(self.at_end(y.shape), 0.0, y) if self.edges else y

    def lane_down(self, x):
        y = self.down(x, x.ndim - 1)
        return jnp.where(self.at_start(y.shape), 0.0, y) if self.edges else y

    def own_lane(self, shape):
        lane = lane_ids(shape)
        return lane & (self.n[2] - 1) if self.index == 3 else lane

    def at_start(self, shape):
        return self.own_lane(shape) == 0

    def at_end(self, shape):
        return self.own_lane(shape) == self.n[2] - 1

    def row_up(self, x):
        y = self.up(x, x.ndim - 2)
        if self.index < 3:
            return y
        tile = y[:, 8:16]
        after = jnp.where(lane_ids(tile.shape) < 96, pltpu.roll(tile, 96, 2), 0.0)
        return jnp.concatenate([y[:, 0:8], jnp.where(row_ids(tile.shape) == 7, after, tile)], 1)

    def row_down(self, x):
        y = self.down(x, x.ndim - 2)
        if self.index < 3:
            return y
        tile = y[:, 0:8]
        before = jnp.where(lane_ids(tile.shape) >= 32, pltpu.roll(tile, 32, 2), 0.0)
        return jnp.concatenate([jnp.where(row_ids(tile.shape) == 0, before, tile), y[:, 8:16]], 1)

    def row_valid(self, shape):
        r = row_ids(shape)
        if self.index == 3:
            return jnp.ones(shape, F32)
        ahead = self.n[1] + (4, 6, 4)[self.index]
        j = jnp.where(r < ahead, r, r - self.rows) + self.l * self.n[1]
        ok = (j >= 0) & (j < WHOLE[self.index][1])
        if self.n[2] < self.lanes:
            ok = ok & (lane_ids(shape) < self.n[2])
        return jnp.where(ok, 1.0, 0.0).astype(F32)

    def plane_valid(self, i):
        p = self.g * self.n[0] + (i - self.low)
        return jnp.where((p >= 0) & (p < WHOLE[self.index][0]), 1.0, 0.0).astype(F32)

    def plane_valid_many(self, lo, hi):
        shape = (hi - lo, self.rows, self.lanes)
        p = self.g * self.n[0] + (lo - self.low) + lax.broadcasted_iota(jnp.int32, shape, 0)
        return jnp.where((p >= 0) & (p < WHOLE[self.index][0]), 1.0, 0.0).astype(F32)

    def cells(self, c):
        cl = c + self.lane_down(c)
        cj = c + self.row_down(c)
        cjl = cl + self.row_down(cl)
        return cl, cj, cjl

    def coefficients(self, cells, before, valid):
        cl, cj, cjl = cells
        pl_, pj, pjl = before
        k = cjl + pjl
        el = cj + pj
        if self.edges:
            el = jnp.where(self.at_end(el.shape), 0.0, el)
        return cjl, cl + pl_, el, 5.0 * k, valid * (0.15 / jnp.maximum(k, 1.0))

    def parts(self, u):
        ul = self.lane_up(u)
        uj = self.row_up(u)
        a = u + ul
        return ul, uj, a + self.row_up(a)

    def combine(self, u, un, up, ul, uj, t, ei, eip, ej, el, k5):
        tj = t + self.row_down(t)
        b = k5 * u + ei * un + eip * up + ej * uj + el * ul - tj
        return b + self.lane_down(el * u - tj) + self.row_down(ej * u)

    def setup_all(self, lo, hi):
        cl, cj, cjl = self.cells(self.C[lo - 1:hi])
        valid = self.row_valid((1, self.rows, self.lanes)) * self.plane_valid_many(lo, hi)
        ei, ej, el, k5, w = self.coefficients(
            (cl[1:], cj[1:], cjl[1:]), (cl[:-1], cj[:-1], cjl[:-1]), valid
        )
        self.Ei[lo - 1:hi] = cjl
        self.Ej[lo:hi] = ej
        self.El[lo:hi] = el
        self.K5[lo:hi] = k5
        self.W[lo:hi] = w

    def apply_all(self, u_ref, lo, hi):
        u = u_ref[lo - 1:hi + 1]
        ul, uj, v = self.parts(u)
        t = self.C[lo - 1:hi] * (v[:-1] + v[1:])
        return self.combine(
            u[1:-1], u[2:], u[:-2], ul[1:-1], uj[1:-1], t[1:] + t[:-1],
            self.Ei[lo:hi], self.Ei[lo - 1:hi - 1], self.Ej[lo:hi], self.El[lo:hi], self.K5[lo:hi],
        )

    def first_all(self, lo, hi):
        self.U[lo:hi] = self.W[lo:hi] * self.F[lo:hi]

    def sweep_all(self, source, target, lo, hi):
        b = self.apply_all(source, lo, hi)
        target[lo:hi] = source[lo:hi] + self.W[lo:hi] * (self.F[lo:hi] - b)

    def residual_all(self, source, lo, hi):
        return self.F[lo:hi] - self.apply_all(source, lo, hi)

    def planes_loop(self, lo, hi, step, carry, unroll):
        whole = (hi - lo) // unroll

        def body(k, c):
            for m in range(unroll):
                c = step(lo + k * unroll + m, c)
            return c

        carry = lax.fori_loop(0, whole, body, carry)
        for i in range(lo + whole * unroll, hi):
            carry = step(i, carry)
        return carry

    def apply_loop(self, u_ref, lo, hi, emit, unroll):
        _, _, v0 = self.parts(u_ref[lo - 1])
        ul, uj, v = self.parts(u_ref[lo])
        t = self.C[lo - 1] * (v0 + v)

        def step(i, carry):
            ul, uj, v, t = carry
            u = u_ref[i]
            un = u_ref[i + 1]
            uln, ujn, vn = self.parts(un)
            tn = self.C[i] * (v + vn)
            b = self.combine(
                u, un, u_ref[i - 1], ul, uj, t + tn,
                self.Ei[i], self.Ei[i - 1], self.Ej[i], self.El[i], self.K5[i],
            )
            emit(i, u, b)
            return uln, ujn, vn, tn

        self.planes_loop(lo, hi, step, (ul, uj, v, t), unroll)


def kernel(*refs):
    rhs, phase, fine_out, coarse_out = refs[:4]
    refs = refs[4:]
    windows = [refs[9 * k:9 * k + 9] for k in range(4)]
    (
        ph, upk, dpk, rxl0, rxh0, rs, s0, out, ct1, n1, h0,
        rxl1, rxh1, crl1, crh1, c1w, s1, ct2, pf2, pn2, rf2, rn2, n2w, n3s, s2, pf3, pc3, rf3, rc3,
        r0_mat, r1_mat, r2_mat, p0_mat, p1_mat,
        lsem, known, ss0, rs0, sf1, qf1, sc1, qc1, sf2, qf2, sc2, qc2, sf3, qf3, sc3, qc3,
    ) = refs[36:]
    g = lax.axis_index("grp")
    l = lax.axis_index("loc")
    lv = [Level(k, g, l, windows[k]) for k in range(4)]
    L0, L1, L2, L3 = lv
    sent = []

    def device(dg, dl):
        return lax.rem(g + dg + NG, NG), lax.rem(l + dl + NL, NL)

    def inside(dg, dl):
        tests = [t for t in (
            g + dg >= 0 if dg < 0 else None, g + dg < NG if dg > 0 else None,
            l + dl >= 0 if dl < 0 else None, l + dl < NL if dl > 0 else None,
        ) if t is not None]
        return functools.reduce(jnp.logical_and, tests)

    def run(test, action):
        action() if test is None else pl.when(test)(action)

    class Sent:
        def __init__(self, src, dst, s_sem, r_sem, to, wrap):
            self.copy = pltpu.make_async_remote_copy(
                src_ref=src, dst_ref=dst, send_sem=s_sem, recv_sem=r_sem,
                device_id=device(*to), device_id_type=MESH,
            )
            self.out = None if wrap else inside(*to)
            self.back = None if wrap else inside(-to[0], -to[1])
            run(self.out, self.copy.start)
            sent.append(self)

        def wait_recv(self):
            run(self.back, self.copy.wait_recv)

        def wait_send(self):
            run(self.out, self.copy.wait_send)

    def send(src, dst, s_sem, r_sem, to, wrap=False):
        return Sent(src, dst, s_sem, r_sem, to, wrap)

    def flush(copies):
        for copy in copies:
            copy.wait_send()

    load_f = pltpu.make_async_copy(rhs, L0.F.at[4:20, 0:32], lsem.at[0])
    load_p = pltpu.make_async_copy(phase, ph, lsem.at[1])
    load_p.start()
    load_f.start()
    barrier = pltpu.get_barrier_semaphore()
    def greet(sem, targets):
        count = jnp.int32(0)
        for to in targets:
            test = inside(*to)

            def signal(to=to):
                pl.semaphore_signal(sem, inc=1, device_id=device(*to), device_id_type=MESH)

            run(test, signal)
            count = count + jnp.where(test, 1, 0)
        return count

    around = greet(barrier, FACES)

    def clear(test, *refs):
        @pl.when(test)
        def _():
            for ref in refs:
                ref[...] = jnp.zeros(ref.shape, F32)

    near_tiles = (rxl1, rxh1, crl1, crh1)
    clear(
        g == 0, L0.F.at[0:4, 0:32], L0.C.at[0:4, 0:32], L1.F.at[0:4, 0:16], L1.C.at[0:4, 0:16],
        *[x.at[0:4] for x in (rxl0, rxh0) + near_tiles],
    )
    clear(
        g == NG - 1, L0.F.at[20:22, 0:32], L0.C.at[20:22, 0:32], L1.F.at[12:14, 0:16], L1.C.at[12:14, 0:16],
        *[x.at[20:22] for x in (rxl0, rxh0)], *[x.at[12:14] for x in near_tiles],
    )
    clear(l == 0, rxl0, rxl1, crl1)
    clear(l == NL - 1, rxh0, rxh1, crh1)
    for d in (1, 2, 3):
        clear(g < d, rf2.at[3 - d], rn2.at[3 - d])
        clear(g >= NG - d, rf2.at[3 + d], rn2.at[3 + d])

    load_p.wait()
    gas = ph[...].astype(F32)
    L0.C[4:20, 0:32] = 1.0 + 999.0 * gas
    load_f.wait()
    sub = row_ids((1, 8, 256)) < 4
    upk[...] = jnp.where(sub, pltpu.roll(L0.C[4:20, 24:32], 4, 1), L0.F[4:20, 24:32])
    dpk[...] = jnp.where(sub, L0.F[4:20, 0:8], pltpu.roll(L0.C[4:20, 0:8], 4, 1))
    pl.semaphore_wait(barrier, around)

    first = []
    for src, dst, to in (
        (upk.at[0:4], rxl0.at[4:8], (0, 1)),
        (dpk.at[0:4], rxh0.at[4:8], (0, -1)),
        (upk.at[4:8], rxl0.at[8:12], (0, 1)),
        (dpk.at[4:8], rxh0.at[8:12], (0, -1)),
        (upk.at[8:12], rxl0.at[12:16], (0, 1)),
        (dpk.at[8:12], rxh0.at[12:16], (0, -1)),
        (upk.at[12:16], rxl0.at[16:20], (0, 1)),
        (dpk.at[12:16], rxh0.at[16:20], (0, -1)),
        (L0.C.at[16:20, 0:32], L0.C.at[0:4, 0:32], (1, 0)),
        (L0.F.at[17:20, 0:32], L0.F.at[1:4, 0:32], (1, 0)),
        (L0.C.at[4:6, 0:32], L0.C.at[20:22, 0:32], (-1, 0)),
        (L0.F.at[4:6, 0:32], L0.F.at[20:22, 0:32], (-1, 0)),
    ):
        first.append(send(src, dst, ss0.at[len(first)], rs0.at[len(first)], to))

    def near_sends(ref, low, high, ssem, rsem, depth):
        copies = []
        for k, (dg, dl) in enumerate(NEAR):
            lo, hi, at = {1: (12 - depth, 12, 4 - depth), 0: (4, 12, 4), -1: (4, 6, 12)}[dg]
            rows, target = {1: (slice(0, 16), low), 0: (slice(0, 16), ref), -1: (slice(0, 8), high)}[dl]
            where = pl.ds(at, hi - lo)
            dst = target.at[where, 0:16] if dl == 0 else target.at[where]
            copies.append(send(ref.at[lo:hi, rows], dst, ssem.at[k], rsem.at[k], (dg, dl)))
        return copies

    def wide_sends(src, slots, ssem, rsem):
        return [
            send(src, slots.at[3 - dg], ssem.at[k], rsem.at[k], (dg, dl))
            for k, (dg, dl) in enumerate(WIDE)
        ]

    def along_sends(src, slots, ssem, rsem):
        for to in ALONG:
            pltpu.make_async_remote_copy(
                src_ref=src, dst_ref=slots.at[l], send_sem=ssem.at[0], recv_sem=rsem.at[0],
                device_id=device(*to), device_id_type=MESH,
            ).start()
        whole = slots.at[0:NL - 1]
        return [pltpu.make_async_copy(whole, whole, sem.at[0]) for sem in (rsem, ssem)]

    greet(known.at[0], FACES)

    weights = ((r0_mat, 256), (r1_mat, 128), (r2_mat, 64))
    for ref, used in weights:
        k, c = row_ids(ref.shape), lane_ids(ref.shape)
        near = jnp.abs(k - 2 * c)
        live = (k < used) & (c < used // 2)
        ref[...] = jnp.where(
            live & (near == 0), 0.5, jnp.where(live & (near == 1), 0.25, 0.0)
        ).astype(BF16)
    for ref in (p0_mat, p1_mat):
        half = row_ids(ref.shape) - 2 * lane_ids(ref.shape)
        ref[...] = jnp.where((half == 0) | (half == 1), 1.0, 0.0).astype(BF16)

    pairs = jnp.concatenate([gas[2 * i:2 * i + 1] + gas[2 * i + 1:2 * i + 2] for i in range(8)], 0)
    ct1[...] = jnp.dot(
        pairs.reshape(8 * 32, 256).astype(BF16), p0_mat[...], preferred_element_type=F32
    ).reshape(8, 32, 128)
    n1[...] = ct1[:, pl.ds(0, 16, stride=2), :] + ct1[:, pl.ds(1, 16, stride=2), :]
    count1 = n1[...]
    L1.C[4:12, 0:16] = count1
    pl.semaphore_wait(known.at[0], around)
    for src, dst, to in (
        (upk.at[12:16], rxl0.at[0:4], (1, 1)),
        (dpk.at[12:16], rxh0.at[0:4], (1, -1)),
        (upk.at[0:2], rxl0.at[20:22], (-1, 1)),
        (dpk.at[0:2], rxh0.at[20:22], (-1, -1)),
    ):
        first.append(send(src, dst, ss0.at[len(first)], rs0.at[len(first)], to))
    got_c1 = near_sends(L1.C, crl1, crh1, sc1, qc1, 4)
    known_1 = greet(known.at[1], [(-1, 0), (1, 0)])
    known_2 = greet(known.at[2], [(0, -2), (0, 2)])

    rows0 = L0.row_valid((40, 256))
    sub = row_ids((8, 256)) < 4

    def merge(i, _):
        low, high = rxl0[i], rxh0[i]
        L0.F[i, 32:40] = jnp.where(sub, high, low)
        L0.C[i, 32:40] = pltpu.roll(jnp.where(sub, low, high), 4, 0) * rows0[32:40] * L0.plane_valid(i)
        return 0

    def setup(i, before):
        cells = L0.cells(L0.C[i])
        ei, ej, el, k5, w = L0.coefficients(cells, before, rows0 * L0.plane_valid(i))
        L0.Ei[i], L0.Ej[i], L0.El[i], L0.K5[i], L0.W[i] = ei, ej, el, k5, w
        L0.U[i] = w * (12.0 * L0.F[i])
        return cells

    def second(i, u, b):
        L0.V[i] = u + L0.W[i] * (12.0 * L0.F[i] - b)

    def residual(i, u, b):
        r = (12.0 * L0.F[i] - b) * (rows0 * L0.plane_valid(i))
        for half in range(2):
            lanes = slice(128 * half, 128 * half + 128)
            rs[i - 3, half, 0:8] = r[32:40, lanes]
            rs[i - 3, half, 8:40] = r[0:32, lanes]
        out[jnp.maximum(i - 4, 0)] = r[0:32] * (1.0 / 12.0)

    def setup_planes(lo, hi):
        before = L0.cells(L0.C[lo - 1])
        L0.Ei[lo - 1] = before[2]
        L0.planes_loop(lo, hi, setup, before, 8)

    for copy in first[0:2]:
        copy.wait_recv()
    lax.fori_loop(4, 8, merge, 0)
    setup_planes(5, 8)
    L0.apply_loop(L0.U, 6, 7, second, 8)
    for copy in first[2:4]:
        copy.wait_recv()
    lax.fori_loop(8, 12, merge, 0)
    setup_planes(8, 12)
    L0.apply_loop(L0.U, 7, 11, second, 8)
    for copy in first[4:6]:
        copy.wait_recv()
    lax.fori_loop(12, 16, merge, 0)
    setup_planes(12, 16)
    L0.apply_loop(L0.U, 11, 15, second, 8)
    for copy in first[6:8]:
        copy.wait_recv()
    lax.fori_loop(16, 20, merge, 0)
    setup_planes(16, 20)
    L0.apply_loop(L0.U, 15, 19, second, 8)
    L0.apply_loop(L0.V, 7, 18, residual, 6)
    for copy in first[8:]:
        copy.wait_recv()
    for i in (0, 1, 2, 3, 20, 21):
        merge(i, 0)
        L0.C[i, 0:32] = L0.C[i, 0:32] * L0.plane_valid(i)
    setup_planes(1, 5)
    setup_planes(20, 22)
    L0.apply_loop(L0.U, 2, 6, second, 4)
    L0.apply_loop(L0.U, 19, 21, second, 4)
    L0.apply_loop(L0.V, 3, 7, residual, 4)
    L0.apply_loop(L0.V, 18, 20, residual, 4)
    store = pltpu.make_async_copy(out, fine_out, lsem.at[2])
    store.start()

    def coarser_planes(r):
        return [0.5 * (r[2 * i] + r[2 * i + 2]) + r[2 * i + 1] for i in range((r.shape[0] - 1) // 2)]

    def coarser_rows(ref, kept):
        return 0.5 * (
            ref[:, pl.ds(7, kept, stride=2), :] + ref[:, pl.ds(9, kept, stride=2), :]
        ) + ref[:, pl.ds(8, kept, stride=2), :]

    total = jnp.zeros((8 * 16, 128), F32)
    for half in range(2):
        for i, plane in enumerate(coarser_planes(rs[:, half])):
            s0[half, i] = plane
        total = total + split_dot(
            coarser_rows(s0.at[half], 16).reshape(8 * 16, 128), r0_mat[128 * half:128 * half + 128]
        )
    L1.F[4:12, 0:16] = total.reshape(8, 16, 128)
    earlier, sent[:] = sent[:], []
    got_f1 = near_sends(L1.F, rxl1, rxh1, sf1, qf1, 3)

    pl.semaphore_wait(known.at[1], known_1)
    pl.semaphore_wait(known.at[2], known_2)
    known_3 = greet(known.at[3], [(0, -4), (0, 4)])

    for copy in got_c1:
        copy.wait_recv()
    def merge_rows(ref, low, high, lo, hi):
        inner = row_ids((1, 8, 128)) < 6
        ref[lo:hi, 16:24] = jnp.where(inner, high[lo:hi], low[lo:hi, 0:8])
        ref[lo:hi, 24:32] = low[lo:hi, 8:16]

    merge_rows(L1.C, crl1, crh1, 0, 14)
    for i in range(4):
        s1[i, 0:32] = L1.C[2 * i + 4] + L1.C[2 * i + 5]
    pairs = s1[:, pl.ds(0, 16, stride=2), :] + s1[:, pl.ds(1, 16, stride=2), :]
    count2 = jnp.dot(
        pairs.reshape(4 * 16, 128).astype(BF16), p1_mat[...], preferred_element_type=F32
    ).reshape(4, 16, 128)
    pn2[...] = count2[0:2] + pltpu.roll(count2[2:4], 64, 2)
    rn2[3] = pn2[...]
    got_c2 = wide_sends(pn2, rn2, sc2, qc2)
    valid1 = L1.row_valid((1, 32, 128)) * L1.plane_valid_many(0, 14)
    c1w[...] = (1.0 + 124.875 * L1.C[...]) * valid1
    L1.C = c1w
    L1.setup_all(1, 14)

    flush(earlier)
    pl.semaphore_wait(known.at[3], known_3)
    known_4 = greet(known.at[4], [(0, -8), (0, 8)])

    for copy in got_f1:
        copy.wait_recv()
    merge_rows(L1.F, rxl1, rxh1, 1, 14)
    L1.first_all(1, 14)
    L1.sweep_all(L1.U, L1.V, 2, 13)
    r1 = L1.residual_all(L1.V, 3, 12) * valid1[3:12]
    for i, plane in enumerate(coarser_planes(r1)):
        s1[i, 0:8] = plane[24:32]
        s1[i, 8:40] = plane
    f2 = split_dot(coarser_rows(s1, 16).reshape(4 * 16, 128), r1_mat[...]).reshape(4, 16, 128)
    pf2[...] = f2[0:2] + pltpu.roll(f2[2:4], 64, 2)
    rf2[3] = pf2[...]
    earlier, sent[:] = sent[:], []
    got_f2 = wide_sends(pf2, rf2, sf2, qf2)

    pl.semaphore_wait(known.at[4], known_4)

    def unpack_wide(slots, ref):
        lane = lane_ids((1, 1, 1, 128)) < 64
        tiles = slots[...]
        first = jnp.where(lane, tiles, 0.0)
        later = jnp.where(lane, pltpu.roll(tiles, 64, 3), 0.0)
        for d in range(7):
            ref[4 * d:4 * d + 2] = first[d]
            ref[4 * d + 2:4 * d + 4] = later[d]

    for copy in got_c2:
        copy.wait_recv()

    unpack_wide(rn2, n2w)
    valid2 = L2.row_valid((1, 16, 128)) * L2.plane_valid_many(0, 28)
    L2.C[...] = (1.0 + (999.0 / 64.0) * n2w[...]) * valid2
    L2.setup_all(1, 26)

    count2 = n2w[2:24, 0:8]
    pairs = jnp.concatenate([count2[2 * i:2 * i + 1] + count2[2 * i + 1:2 * i + 2] for i in range(11)], 0)
    n3s[...] = jnp.dot(
        pairs.reshape(11 * 8, 128).astype(BF16), p1_mat[...], preferred_element_type=F32
    ).reshape(11, 8, 128)
    count3 = n3s[:, pl.ds(0, 4, stride=2), :] + n3s[:, pl.ds(1, 4, stride=2), :]

    def pack(planes, ref):
        for t in range(2):
            for h in range(2):
                total = jnp.zeros((4, 128), F32)
                for q in range(4):
                    p = 8 * t + 4 * h + q
                    if p < len(planes):
                        total = total + (pltpu.roll(planes[p], 32 * q, 1) if q else planes[p])
                ref[t, 4 * h:4 * h + 4] = total
        tiles = ref[...]
        tiles = jnp.where(lax.rem(l, 2) == 1, pltpu.roll(tiles, 4, 1), tiles)
        tiles = jnp.where(lax.rem(lax.div(l, 4), 2) == 1, pltpu.roll(tiles, 32, 2), tiles)
        ref[...] = jnp.where(l >= 8, pltpu.roll(tiles, 64, 2), tiles)

    def unpack_along(slots, count, put):
        half, group = row_ids((8, 128)) // 4, lane_ids((8, 128)) // 32
        cell = [[(half == h) & (group == q) for q in range(4)] for h in range(2)]
        for p in range(count):
            t, h, q = p // 8, (p % 8) // 4, p % 4
            for tile in range(2):
                total = slots[2 * tile, t]
                for owner in range(1, 8):
                    e, o = owner % 2, owner // 2
                    total = jnp.where(cell[(h + e) % 2][(q + o) % 4], slots[4 * o + 2 * tile + e, t], total)
                if h:
                    total = pltpu.roll(total, 4, 0)
                if q:
                    total = pltpu.roll(total, 128 - 32 * q, 1)
                put(p, slice(8 * tile, 8 * tile + 8), total)

    pack([count3[i] for i in range(11)], pc3)
    rc3[l] = pc3[...]
    got_c3 = along_sends(pc3, rc3, sc3, qc3)
    flush(earlier)

    for copy in got_f2:
        copy.wait_recv()

    unpack_wide(rf2, L2.F)
    L2.first_all(1, 26)
    L2.sweep_all(L2.U, L2.V, 2, 25)
    r2 = L2.residual_all(L2.V, 3, 24) * valid2[3:24]
    for i, plane in enumerate(coarser_planes(r2)):
        s2[i, 0:8] = plane[8:16]
        s2[i, 8:24] = plane
    f3 = split_dot(coarser_rows(s2, 8).reshape(10 * 8, 128), r2_mat[...]).reshape(10, 8, 128)
    pack([f3[i, 0:4] for i in range(10)], pf3)
    rf3[l] = pf3[...]
    earlier = sent[:]
    got_f3 = along_sends(pf3, rf3, sf3, qf3)

    flush(earlier)
    got_c3[0].wait()

    def put_c3(p, rows, value):
        L3.C[p, rows] = (1.0 + (999.0 / 512.0) * value) * L3.plane_valid(p)

    unpack_along(rc3, 11, put_c3)
    L3.setup_all(1, 11)

    got_f3[0].wait()

    def put_f3(p, rows, value):
        L3.F[p + 1, rows] = value

    unpack_along(rf3, 10, put_f3)
    L3.first_all(1, 11)
    source, target = L3.U, L3.V
    for sweep in range(COARSE_SWEEPS - 1):
        L3.sweep_all(source, target, 2 + sweep, 10 - sweep)
        source, target = target, source
    last = (8.0 / 12.0) * L3.residual_all(source, 5, 7)
    for i in range(2):
        turned = jnp.transpose(last[i], (1, 0))
        coarse_out[i] = jnp.concatenate([turned[32 * q:32 * q + 32] for q in range(4)], 1)

    store.wait()
    got_c3[1].wait()
    got_f3[1].wait()


def per_device(right_side, phase):
    scratch = []
    for k in range(4):
        shape = (PLANES[k], ROWS[k], LANES[k])
        scratch += [pltpu.VMEM(shape, F32) for _ in range(9)]
    scratch += [
        pltpu.VMEM(s, d)
        for s, d in (
            ((16, 32, 256), jnp.int32),
            ((16, 8, 256), F32), ((16, 8, 256), F32),
            ((22, 8, 256), F32), ((22, 8, 256), F32),
            ((17, 2, 40, 128), F32), ((2, 8, 40, 128), F32),
            ((16, 32, 256), F32),
            ((8, 32, 128), F32), ((8, 16, 128), F32), ((17, 16, 128), F32),
            ((14, 16, 128), F32), ((14, 8, 128), F32), ((14, 16, 128), F32), ((14, 8, 128), F32),
            ((14, 32, 128), F32),
            ((4, 40, 128), F32),
            ((4, 16, 128), F32),
            ((2, 16, 128), F32), ((2, 16, 128), F32),
            ((7, 2, 16, 128), F32), ((7, 2, 16, 128), F32),
            ((28, 16, 128), F32), ((11, 8, 128), F32), ((10, 24, 128), F32),
            ((2, 8, 128), F32), ((2, 8, 128), F32),
            ((16, 2, 8, 128), F32), ((16, 2, 8, 128), F32),
            ((256, 128), BF16), ((128, 128), BF16), ((128, 128), BF16),
            ((256, 128), BF16), ((128, 128), BF16),
        )
    ]
    scratch += [pltpu.SemaphoreType.DMA((3,)), pltpu.SemaphoreType.REGULAR((5,))]
    for n in (16, len(NEAR), len(NEAR), len(WIDE), len(WIDE), 1, 1):
        scratch += [pltpu.SemaphoreType.DMA((n,)), pltpu.SemaphoreType.DMA((n,))]
    vmem = pl.BlockSpec(memory_space=pltpu.VMEM)
    hbm = pl.BlockSpec(memory_space=pl.ANY)
    fine, coarse = pl.pallas_call(
        kernel,
        out_shape=(
            jax.ShapeDtypeStruct((16, 32, 256), F32),
            jax.ShapeDtypeStruct((2, 32, 64), F32),
        ),
        in_specs=[hbm, hbm],
        out_specs=(hbm, vmem),
        scratch_shapes=scratch,
        compiler_params=pltpu.CompilerParams(
            collective_id=0, has_side_effects=True, vmem_limit_bytes=24 * 2**20
        ),
    )(pltpu.with_memory_space_constraint(right_side, pltpu.HBM), pltpu.with_memory_space_constraint(phase, pltpu.HBM))
    return fine, jnp.transpose(coarse, (0, 2, 1))


def solution(mesh):
    in_specs = (P("grp", "loc", None), P("grp", "loc", None))
    out_specs = (P("grp", "loc", None), P("grp", None, None))
    return jax.shard_map(
        per_device, mesh=mesh, in_specs=in_specs, out_specs=out_specs, check_vma=False
    )
```

```python
import functools

import jax
import jax.numpy as jnp
from jax import lax
from jax.experimental import pallas as pl
from jax.experimental.pallas import tpu as pltpu
from jax.sharding import PartitionSpec as P

MESH = pl.DeviceIdType.MESH
NG, NL = 16, 16
COARSE_SWEEPS = 4
F32 = jnp.float32
BF16 = jnp.bfloat16
WHOLE = ((256, 512, 256), (128, 256, 128), (64, 128, 64), (32, 64, 32))
BLOCK = ((16, 32, 256), (8, 16, 128), (4, 8, 64), (2, 64, 32))
LOW = (4, 4, 12, 5)
PLANES = (22, 14, 28, 11)
ROWS = (40, 32, 16, 16)
LANES = (256, 128, 128, 128)

NEAR = [(1, 1), (1, -1), (-1, 1), (-1, -1), (0, 1), (0, -1), (1, 0), (-1, 0)]
FACES = [(0, 1), (0, -1), (1, 0), (-1, 0)]
WIDE = [(a, 0) for a in (-3, 3, -2, 2, -1, 1)]
ALONG = [(0, k) for k in (10, 9, 11, 6, 5, 7, 14, 13, 2, 8, 3, 15, 12, 4, 1)]


def lane_ids(shape):
    return lax.broadcasted_iota(jnp.int32, shape, len(shape) - 1)


def row_ids(shape):
    return lax.broadcasted_iota(jnp.int32, shape, len(shape) - 2)


def split_dot(values, matrix):
    high = values.astype(BF16)
    rest = values - high.astype(F32)
    mid = rest.astype(BF16)
    low = (rest - mid.astype(F32)).astype(BF16)
    dot = functools.partial(jnp.dot, preferred_element_type=F32)
    return dot(high, matrix) + (dot(mid, matrix) + dot(low, matrix))


class Level:
    def __init__(self, index, g, l, refs):
        self.index = index
        self.F, self.C, self.U, self.V, self.Ei, self.Ej, self.El, self.K5, self.W = refs
        self.n = BLOCK[index]
        self.low = LOW[index]
        self.rows, self.lanes = ROWS[index], LANES[index]
        self.edges = index != 2
        self.g, self.l = g, l

    def up(self, x, axis):
        return pltpu.roll(x, x.shape[axis] - 1, axis)

    def down(self, x, axis):
        return pltpu.roll(x, 1, axis)

    def lane_up(self, x):
        y = self.up(x, x.ndim - 1)
        return jnp.where(self.at_end(y.shape), 0.0, y) if self.edges else y

    def lane_down(self, x):
        y = self.down(x, x.ndim - 1)
        return jnp.where(self.at_start(y.shape), 0.0, y) if self.edges else y

    def own_lane(self, shape):
        lane = lane_ids(shape)
        return lane & (self.n[2] - 1) if self.index == 3 else lane

    def at_start(self, shape):
        return self.own_lane(shape) == 0

    def at_end(self, shape):
        return self.own_lane(shape) == self.n[2] - 1

    def row_up(self, x):
        y = self.up(x, x.ndim - 2)
        if self.index < 3:
            return y
        tile = y[:, 8:16]
        after = jnp.where(lane_ids(tile.shape) < 96, pltpu.roll(tile, 96, 2), 0.0)
        return jnp.concatenate([y[:, 0:8], jnp.where(row_ids(tile.shape) == 7, after, tile)], 1)

    def row_down(self, x):
        y = self.down(x, x.ndim - 2)
        if self.index < 3:
            return y
        tile = y[:, 0:8]
        before = jnp.where(lane_ids(tile.shape) >= 32, pltpu.roll(tile, 32, 2), 0.0)
        return jnp.concatenate([jnp.where(row_ids(tile.shape) == 0, before, tile), y[:, 8:16]], 1)

    def row_valid(self, shape):
        r = row_ids(shape)
        if self.index == 3:
            return jnp.ones(shape, F32)
        ahead = self.n[1] + (4, 6, 4)[self.index]
        j = jnp.where(r < ahead, r, r - self.rows) + self.l * self.n[1]
        ok = (j >= 0) & (j < WHOLE[self.index][1])
        if self.n[2] < self.lanes:
            ok = ok & (lane_ids(shape) < self.n[2])
        return jnp.where(ok, 1.0, 0.0).astype(F32)

    def plane_valid(self, i):
        p = self.g * self.n[0] + (i - self.low)
        return jnp.where((p >= 0) & (p < WHOLE[self.index][0]), 1.0, 0.0).astype(F32)

    def plane_valid_many(self, lo, hi):
        shape = (hi - lo, self.rows, self.lanes)
        p = self.g * self.n[0] + (lo - self.low) + lax.broadcasted_iota(jnp.int32, shape, 0)
        return jnp.where((p >= 0) & (p < WHOLE[self.index][0]), 1.0, 0.0).astype(F32)

    def cells(self, c):
        cl = c + self.lane_down(c)
        cj = c + self.row_down(c)
        cjl = cl + self.row_down(cl)
        return cl, cj, cjl

    def coefficients(self, cells, before, valid):
        cl, cj, cjl = cells
        pl_, pj, pjl = before
        k = cjl + pjl
        el = cj + pj
        if self.edges:
            el = jnp.where(self.at_end(el.shape), 0.0, el)
        return cjl, cl + pl_, el, 5.0 * k, valid * (0.15 / jnp.maximum(k, 1.0))

    def parts(self, u):
        ul = self.lane_up(u)
        uj = self.row_up(u)
        a = u + ul
        return ul, uj, a + self.row_up(a)

    def combine(self, u, un, up, ul, uj, t, ei, eip, ej, el, k5):
        tj = t + self.row_down(t)
        b = k5 * u + ei * un + eip * up + ej * uj + el * ul - tj
        return b + self.lane_down(el * u - tj) + self.row_down(ej * u)

    def setup_all(self, lo, hi):
        cl, cj, cjl = self.cells(self.C[lo - 1:hi])
        valid = self.row_valid((1, self.rows, self.lanes)) * self.plane_valid_many(lo, hi)
        ei, ej, el, k5, w = self.coefficients(
            (cl[1:], cj[1:], cjl[1:]), (cl[:-1], cj[:-1], cjl[:-1]), valid
        )
        self.Ei[lo - 1:hi] = cjl
        self.Ej[lo:hi] = ej
        self.El[lo:hi] = el
        self.K5[lo:hi] = k5
        self.W[lo:hi] = w

    def apply_all(self, u_ref, lo, hi):
        u = u_ref[lo - 1:hi + 1]
        ul, uj, v = self.parts(u)
        t = self.C[lo - 1:hi] * (v[:-1] + v[1:])
        return self.combine(
            u[1:-1], u[2:], u[:-2], ul[1:-1], uj[1:-1], t[1:] + t[:-1],
            self.Ei[lo:hi], self.Ei[lo - 1:hi - 1], self.Ej[lo:hi], self.El[lo:hi], self.K5[lo:hi],
        )

    def first_all(self, lo, hi):
        self.U[lo:hi] = self.W[lo:hi] * self.F[lo:hi]

    def sweep_all(self, source, target, lo, hi):
        b = self.apply_all(source, lo, hi)
        target[lo:hi] = source[lo:hi] + self.W[lo:hi] * (self.F[lo:hi] - b)

    def residual_all(self, source, lo, hi):
        return self.F[lo:hi] - self.apply_all(source, lo, hi)

    def planes_loop(self, lo, hi, step, carry, unroll):
        whole = (hi - lo) // unroll

        def body(k, c):
            for m in range(unroll):
                c = step(lo + k * unroll + m, c)
            return c

        carry = lax.fori_loop(0, whole, body, carry)
        for i in range(lo + whole * unroll, hi):
            carry = step(i, carry)
        return carry

    def apply_loop(self, u_ref, lo, hi, emit, unroll):
        _, _, v0 = self.parts(u_ref[lo - 1])
        ul, uj, v = self.parts(u_ref[lo])
        t = self.C[lo - 1] * (v0 + v)

        def step(i, carry):
            ul, uj, v, t = carry
            u = u_ref[i]
            un = u_ref[i + 1]
            uln, ujn, vn = self.parts(un)
            tn = self.C[i] * (v + vn)
            b = self.combine(
                u, un, u_ref[i - 1], ul, uj, t + tn,
                self.Ei[i], self.Ei[i - 1], self.Ej[i], self.El[i], self.K5[i],
            )
            emit(i, u, b)
            return uln, ujn, vn, tn

        self.planes_loop(lo, hi, step, (ul, uj, v, t), unroll)


def kernel(*refs):
    rhs, phase, fine_out, coarse_out = refs[:4]
    refs = refs[4:]
    windows = [refs[9 * k:9 * k + 9] for k in range(4)]
    (
        ph, upk, dpk, rxl0, rxh0, rs, s0, out, ct1, n1, h0,
        rxl1, rxh1, crl1, crh1, c1w, s1, ct2, pf2, pn2, rf2, rn2, n2w, n3s, s2, pf3, pc3, rf3, rc3,
        r0_mat, r1_mat, r2_mat, p0_mat, p1_mat,
        lsem, known, ss0, rs0, sf1, qf1, sc1, qc1, sf2, qf2, sc2, qc2, sf3, qf3, sc3, qc3,
    ) = refs[36:]
    g = lax.axis_index("grp")
    l = lax.axis_index("loc")
    lv = [Level(k, g, l, windows[k]) for k in range(4)]
    L0, L1, L2, L3 = lv
    sent = []

    def device(dg, dl):
        return lax.rem(g + dg + NG, NG), lax.rem(l + dl + NL, NL)

    def inside(dg, dl):
        tests = [t for t in (
            g + dg >= 0 if dg < 0 else None, g + dg < NG if dg > 0 else None,
            l + dl >= 0 if dl < 0 else None, l + dl < NL if dl > 0 else None,
        ) if t is not None]
        return functools.reduce(jnp.logical_and, tests)

    def run(test, action):
        action() if test is None else pl.when(test)(action)

    class Sent:
        def __init__(self, src, dst, s_sem, r_sem, to, wrap):
            self.copy = pltpu.make_async_remote_copy(
                src_ref=src, dst_ref=dst, send_sem=s_sem, recv_sem=r_sem,
                device_id=device(*to), device_id_type=MESH,
            )
            self.out = None if wrap else inside(*to)
            self.back = None if wrap else inside(-to[0], -to[1])
            run(self.out, self.copy.start)
            sent.append(self)

        def wait_recv(self):
            run(self.back, self.copy.wait_recv)

        def wait_send(self):
            run(self.out, self.copy.wait_send)

    def send(src, dst, s_sem, r_sem, to, wrap=False):
        return Sent(src, dst, s_sem, r_sem, to, wrap)

    def flush(copies):
        for copy in copies:
            copy.wait_send()

    load_f = pltpu.make_async_copy(rhs, L0.F.at[4:20, 0:32], lsem.at[0])
    load_p = pltpu.make_async_copy(phase, ph, lsem.at[1])
    load_p.start()
    load_f.start()
    barrier = pltpu.get_barrier_semaphore()
    def greet(sem, targets):
        count = jnp.int32(0)
        for to in targets:
            test = inside(*to)

            def signal(to=to):
                pl.semaphore_signal(sem, inc=1, device_id=device(*to), device_id_type=MESH)

            run(test, signal)
            count = count + jnp.where(test, 1, 0)
        return count

    around = greet(barrier, FACES)

    def clear(test, *refs):
        @pl.when(test)
        def _():
            for ref in refs:
                ref[...] = jnp.zeros(ref.shape, F32)

    near_tiles = (rxl1, rxh1, crl1, crh1)
    clear(
        g == 0, L0.F.at[0:4, 0:32], L0.C.at[0:4, 0:32], L1.F.at[0:4, 0:16], L1.C.at[0:4, 0:16],
        *[x.at[0:4] for x in (rxl0, rxh0) + near_tiles],
    )
    clear(
        g == NG - 1, L0.F.at[20:22, 0:32], L0.C.at[20:22, 0:32], L1.F.at[12:14, 0:16], L1.C.at[12:14, 0:16],
        *[x.at[20:22] for x in (rxl0, rxh0)], *[x.at[12:14] for x in near_tiles],
    )
    clear(l == 0, rxl0, rxl1, crl1)
    clear(l == NL - 1, rxh0, rxh1, crh1)
    for d in (1, 2, 3):
        clear(g < d, rf2.at[3 - d], rn2.at[3 - d])
        clear(g >= NG - d, rf2.at[3 + d], rn2.at[3 + d])

    load_p.wait()
    gas = ph[...].astype(F32)
    L0.C[4:20, 0:32] = 1.0 + 999.0 * gas
    load_f.wait()
    sub = row_ids((1, 8, 256)) < 4
    upk[...] = jnp.where(sub, pltpu.roll(L0.C[4:20, 24:32], 4, 1), L0.F[4:20, 24:32])
    dpk[...] = jnp.where(sub, L0.F[4:20, 0:8], pltpu.roll(L0.C[4:20, 0:8], 4, 1))
    pl.semaphore_wait(barrier, around)

    first = []
    for src, dst, to in (
        (upk.at[0:4], rxl0.at[4:8], (0, 1)),
        (dpk.at[0:4], rxh0.at[4:8], (0, -1)),
        (L0.C.at[16:20, 0:32], L0.C.at[0:4, 0:32], (1, 0)),
        (L0.F.at[17:20, 0:32], L0.F.at[1:4, 0:32], (1, 0)),
        (L0.C.at[4:6, 0:32], L0.C.at[20:22, 0:32], (-1, 0)),
        (L0.F.at[4:6, 0:32], L0.F.at[20:22, 0:32], (-1, 0)),
        (upk.at[4:8], rxl0.at[8:12], (0, 1)),
        (dpk.at[4:8], rxh0.at[8:12], (0, -1)),
        (upk.at[8:12], rxl0.at[12:16], (0, 1)),
        (dpk.at[8:12], rxh0.at[12:16], (0, -1)),
        (upk.at[12:16], rxl0.at[16:20], (0, 1)),
        (dpk.at[12:16], rxh0.at[16:20], (0, -1)),
    ):
        first.append(send(src, dst, ss0.at[len(first)], rs0.at[len(first)], to))

    def near_sends(ref, low, high, ssem, rsem, depth):
        copies = []
        for k, (dg, dl) in enumerate(NEAR):
            lo, hi, at = {1: (12 - depth, 12, 4 - depth), 0: (4, 12, 4), -1: (4, 6, 12)}[dg]
            rows, target = {1: (slice(0, 16), low), 0: (slice(0, 16), ref), -1: (slice(0, 8), high)}[dl]
            where = pl.ds(at, hi - lo)
            dst = target.at[where, 0:16] if dl == 0 else target.at[where]
            copies.append(send(ref.at[lo:hi, rows], dst, ssem.at[k], rsem.at[k], (dg, dl)))
        return copies

    def wide_sends(src, slots, ssem, rsem):
        return [
            send(src, slots.at[3 - dg], ssem.at[k], rsem.at[k], (dg, dl))
            for k, (dg, dl) in enumerate(WIDE)
        ]

    def along_sends(src, slots, ssem, rsem):
        for to in ALONG:
            pltpu.make_async_remote_copy(
                src_ref=src, dst_ref=slots.at[l], send_sem=ssem.at[0], recv_sem=rsem.at[0],
                device_id=device(*to), device_id_type=MESH,
            ).start()
        whole = slots.at[0:NL - 1]
        return [pltpu.make_async_copy(whole, whole, sem.at[0]) for sem in (rsem, ssem)]

    greet(known.at[0], FACES)

    weights = ((r0_mat, 256), (r1_mat, 128), (r2_mat, 64))
    for ref, used in weights:
        k, c = row_ids(ref.shape), lane_ids(ref.shape)
        near = jnp.abs(k - 2 * c)
        live = (k < used) & (c < used // 2)
        ref[...] = jnp.where(
            live & (near == 0), 0.5, jnp.where(live & (near == 1), 0.25, 0.0)
        ).astype(BF16)
    for ref in (p0_mat, p1_mat):
        half = row_ids(ref.shape) - 2 * lane_ids(ref.shape)
        ref[...] = jnp.where((half == 0) | (half == 1), 1.0, 0.0).astype(BF16)

    pairs = jnp.concatenate([gas[2 * i:2 * i + 1] + gas[2 * i + 1:2 * i + 2] for i in range(8)], 0)
    ct1[...] = jnp.dot(
        pairs.reshape(8 * 32, 256).astype(BF16), p0_mat[...], preferred_element_type=F32
    ).reshape(8, 32, 128)
    n1[...] = ct1[:, pl.ds(0, 16, stride=2), :] + ct1[:, pl.ds(1, 16, stride=2), :]
    count1 = n1[...]
    L1.C[4:12, 0:16] = count1
    pl.semaphore_wait(known.at[0], around)
    for src, dst, to in (
        (upk.at[12:16], rxl0.at[0:4], (1, 1)),
        (dpk.at[12:16], rxh0.at[0:4], (1, -1)),
        (upk.at[0:2], rxl0.at[20:22], (-1, 1)),
        (dpk.at[0:2], rxh0.at[20:22], (-1, -1)),
    ):
        first.append(send(src, dst, ss0.at[len(first)], rs0.at[len(first)], to))
    known_1 = greet(known.at[1], [(-1, 0), (1, 0)])
    known_2 = greet(known.at[2], [(0, -2), (0, 2)])

    rows0 = L0.row_valid((40, 256))
    sub = row_ids((8, 256)) < 4

    def merge(i, _):
        low, high = rxl0[i], rxh0[i]
        L0.F[i, 32:40] = jnp.where(sub, high, low)
        L0.C[i, 32:40] = pltpu.roll(jnp.where(sub, low, high), 4, 0) * rows0[32:40] * L0.plane_valid(i)
        return 0

    def setup(i, before):
        cells = L0.cells(L0.C[i])
        ei, ej, el, k5, w = L0.coefficients(cells, before, rows0 * L0.plane_valid(i))
        L0.Ei[i], L0.Ej[i], L0.El[i], L0.K5[i], L0.W[i] = ei, ej, el, k5, w
        L0.U[i] = w * (12.0 * L0.F[i])
        return cells

    def second(i, u, b):
        L0.V[i] = u + L0.W[i] * (12.0 * L0.F[i] - b)

    def residual(i, u, b):
        r = (12.0 * L0.F[i] - b) * (rows0 * L0.plane_valid(i))
        for half in range(2):
            lanes = slice(128 * half, 128 * half + 128)
            rs[i - 3, half, 0:8] = r[32:40, lanes]
            rs[i - 3, half, 8:40] = r[0:32, lanes]
        out[jnp.maximum(i - 4, 0)] = r[0:32] * (1.0 / 12.0)

    def setup_planes(lo, hi):
        before = L0.cells(L0.C[lo - 1])
        L0.Ei[lo - 1] = before[2]
        L0.planes_loop(lo, hi, setup, before, 8)

    for copy in first[0:2]:
        copy.wait_recv()
    lax.fori_loop(4, 8, merge, 0)
    setup_planes(5, 8)
    L0.apply_loop(L0.U, 6, 7, second, 8)
    for copy in first[6:8]:
        copy.wait_recv()
    lax.fori_loop(8, 12, merge, 0)
    setup_planes(8, 12)
    L0.apply_loop(L0.U, 7, 11, second, 8)
    for copy in first[8:10]:
        copy.wait_recv()
    lax.fori_loop(12, 16, merge, 0)
    setup_planes(12, 16)
    L0.apply_loop(L0.U, 11, 15, second, 8)
    for copy in first[10:12]:
        copy.wait_recv()
    lax.fori_loop(16, 20, merge, 0)
    setup_planes(16, 20)
    L0.apply_loop(L0.U, 15, 19, second, 8)
    L0.apply_loop(L0.V, 7, 18, residual, 6)
    got_c1 = near_sends(L1.C, crl1, crh1, sc1, qc1, 4)
    for copy in first[2:6] + first[12:]:
        copy.wait_recv()
    for i in (0, 1, 2, 3, 20, 21):
        merge(i, 0)
        L0.C[i, 0:32] = L0.C[i, 0:32] * L0.plane_valid(i)
    setup_planes(1, 5)
    setup_planes(20, 22)
    L0.apply_loop(L0.U, 2, 6, second, 4)
    L0.apply_loop(L0.U, 19, 21, second, 4)
    L0.apply_loop(L0.V, 3, 7, residual, 4)
    L0.apply_loop(L0.V, 18, 20, residual, 4)
    store = pltpu.make_async_copy(out, fine_out, lsem.at[2])
    store.start()

    def coarser_planes(r):
        return [0.5 * (r[2 * i] + r[2 * i + 2]) + r[2 * i + 1] for i in range((r.shape[0] - 1) // 2)]

    def coarser_rows(ref, kept):
        return 0.5 * (
            ref[:, pl.ds(7, kept, stride=2), :] + ref[:, pl.ds(9, kept, stride=2), :]
        ) + ref[:, pl.ds(8, kept, stride=2), :]

    total = jnp.zeros((8 * 16, 128), F32)
    for half in range(2):
        for i, plane in enumerate(coarser_planes(rs[:, half])):
            s0[half, i] = plane
        total = total + split_dot(
            coarser_rows(s0.at[half], 16).reshape(8 * 16, 128), r0_mat[128 * half:128 * half + 128]
        )
    L1.F[4:12, 0:16] = total.reshape(8, 16, 128)
    earlier, sent[:] = sent[:], []
    got_f1 = near_sends(L1.F, rxl1, rxh1, sf1, qf1, 3)

    pl.semaphore_wait(known.at[1], known_1)
    pl.semaphore_wait(known.at[2], known_2)
    known_3 = greet(known.at[3], [(0, -4), (0, 4)])

    for copy in got_c1:
        copy.wait_recv()
    def merge_rows(ref, low, high, lo, hi):
        inner = row_ids((1, 8, 128)) < 6
        ref[lo:hi, 16:24] = jnp.where(inner, high[lo:hi], low[lo:hi, 0:8])
        ref[lo:hi, 24:32] = low[lo:hi, 8:16]

    merge_rows(L1.C, crl1, crh1, 0, 14)
    for i in range(4):
        s1[i, 0:32] = L1.C[2 * i + 4] + L1.C[2 * i + 5]
    pairs = s1[:, pl.ds(0, 16, stride=2), :] + s1[:, pl.ds(1, 16, stride=2), :]
    count2 = jnp.dot(
        pairs.reshape(4 * 16, 128).astype(BF16), p1_mat[...], preferred_element_type=F32
    ).reshape(4, 16, 128)
    pn2[...] = count2[0:2] + pltpu.roll(count2[2:4], 64, 2)
    rn2[3] = pn2[...]
    got_c2 = wide_sends(pn2, rn2, sc2, qc2)
    valid1 = L1.row_valid((1, 32, 128)) * L1.plane_valid_many(0, 14)
    c1w[...] = (1.0 + 124.875 * L1.C[...]) * valid1
    L1.C = c1w
    L1.setup_all(1, 14)

    flush(earlier)
    pl.semaphore_wait(known.at[3], known_3)
    known_4 = greet(known.at[4], [(0, -8), (0, 8)])

    for copy in got_f1:
        copy.wait_recv()
    merge_rows(L1.F, rxl1, rxh1, 1, 14)
    L1.first_all(1, 14)
    L1.sweep_all(L1.U, L1.V, 2, 13)
    r1 = L1.residual_all(L1.V, 3, 12) * valid1[3:12]
    for i, plane in enumerate(coarser_planes(r1)):
        s1[i, 0:8] = plane[24:32]
        s1[i, 8:40] = plane
    f2 = split_dot(coarser_rows(s1, 16).reshape(4 * 16, 128), r1_mat[...]).reshape(4, 16, 128)
    pf2[...] = f2[0:2] + pltpu.roll(f2[2:4], 64, 2)
    rf2[3] = pf2[...]
    earlier, sent[:] = sent[:], []
    got_f2 = wide_sends(pf2, rf2, sf2, qf2)

    pl.semaphore_wait(known.at[4], known_4)

    def unpack_wide(slots, ref):
        lane = lane_ids((1, 1, 1, 128)) < 64
        tiles = slots[...]
        first = jnp.where(lane, tiles, 0.0)
        later = jnp.where(lane, pltpu.roll(tiles, 64, 3), 0.0)
        for d in range(7):
            ref[4 * d:4 * d + 2] = first[d]
            ref[4 * d + 2:4 * d + 4] = later[d]

    for copy in got_c2:
        copy.wait_recv()

    unpack_wide(rn2, n2w)
    valid2 = L2.row_valid((1, 16, 128)) * L2.plane_valid_many(0, 28)
    L2.C[...] = (1.0 + (999.0 / 64.0) * n2w[...]) * valid2
    L2.setup_all(1, 26)

    count2 = n2w[2:24, 0:8]
    pairs = jnp.concatenate([count2[2 * i:2 * i + 1] + count2[2 * i + 1:2 * i + 2] for i in range(11)], 0)
    n3s[...] = jnp.dot(
        pairs.reshape(11 * 8, 128).astype(BF16), p1_mat[...], preferred_element_type=F32
    ).reshape(11, 8, 128)
    count3 = n3s[:, pl.ds(0, 4, stride=2), :] + n3s[:, pl.ds(1, 4, stride=2), :]

    def pack(planes, ref):
        for t in range(2):
            for h in range(2):
                total = jnp.zeros((4, 128), F32)
                for q in range(4):
                    p = 8 * t + 4 * h + q
                    if p < len(planes):
                        total = total + (pltpu.roll(planes[p], 32 * q, 1) if q else planes[p])
                ref[t, 4 * h:4 * h + 4] = total
        tiles = ref[...]
        tiles = jnp.where(lax.rem(l, 2) == 1, pltpu.roll(tiles, 4, 1), tiles)
        tiles = jnp.where(lax.rem(lax.div(l, 4), 2) == 1, pltpu.roll(tiles, 32, 2), tiles)
        ref[...] = jnp.where(l >= 8, pltpu.roll(tiles, 64, 2), tiles)

    def unpack_along(slots, count, put):
        half, group = row_ids((8, 128)) // 4, lane_ids((8, 128)) // 32
        cell = [[(half == h) & (group == q) for q in range(4)] for h in range(2)]
        for p in range(count):
            t, h, q = p // 8, (p % 8) // 4, p % 4
            for tile in range(2):
                total = slots[2 * tile, t]
                for owner in range(1, 8):
                    e, o = owner % 2, owner // 2
                    total = jnp.where(cell[(h + e) % 2][(q + o) % 4], slots[4 * o + 2 * tile + e, t], total)
                if h:
                    total = pltpu.roll(total, 4, 0)
                if q:
                    total = pltpu.roll(total, 128 - 32 * q, 1)
                put(p, slice(8 * tile, 8 * tile + 8), total)

    pack([count3[i] for i in range(11)], pc3)
    rc3[l] = pc3[...]
    got_c3 = along_sends(pc3, rc3, sc3, qc3)
    flush(earlier)

    for copy in got_f2:
        copy.wait_recv()

    unpack_wide(rf2, L2.F)
    L2.first_all(1, 26)
    L2.sweep_all(L2.U, L2.V, 2, 25)
    r2 = L2.residual_all(L2.V, 3, 24) * valid2[3:24]
    for i, plane in enumerate(coarser_planes(r2)):
        s2[i, 0:8] = plane[8:16]
        s2[i, 8:24] = plane
    f3 = split_dot(coarser_rows(s2, 8).reshape(10 * 8, 128), r2_mat[...]).reshape(10, 8, 128)
    pack([f3[i, 0:4] for i in range(10)], pf3)
    rf3[l] = pf3[...]
    earlier = sent[:]
    got_f3 = along_sends(pf3, rf3, sf3, qf3)

    flush(earlier)
    got_c3[0].wait()

    def put_c3(p, rows, value):
        L3.C[p, rows] = (1.0 + (999.0 / 512.0) * value) * L3.plane_valid(p)

    unpack_along(rc3, 11, put_c3)
    L3.setup_all(1, 11)

    got_f3[0].wait()

    def put_f3(p, rows, value):
        L3.F[p + 1, rows] = value

    unpack_along(rf3, 10, put_f3)
    L3.first_all(1, 11)
    source, target = L3.U, L3.V
    for sweep in range(COARSE_SWEEPS - 1):
        L3.sweep_all(source, target, 2 + sweep, 10 - sweep)
        source, target = target, source
    last = (8.0 / 12.0) * L3.residual_all(source, 5, 7)
    for i in range(2):
        turned = jnp.transpose(last[i], (1, 0))
        coarse_out[i] = jnp.concatenate([turned[32 * q:32 * q + 32] for q in range(4)], 1)

    store.wait()
    got_c3[1].wait()
    got_f3[1].wait()


def per_device(right_side, phase):
    scratch = []
    for k in range(4):
        shape = (PLANES[k], ROWS[k], LANES[k])
        scratch += [pltpu.VMEM(shape, F32) for _ in range(9)]
    scratch += [
        pltpu.VMEM(s, d)
        for s, d in (
            ((16, 32, 256), jnp.int32),
            ((16, 8, 256), F32), ((16, 8, 256), F32),
            ((22, 8, 256), F32), ((22, 8, 256), F32),
            ((17, 2, 40, 128), F32), ((2, 8, 40, 128), F32),
            ((16, 32, 256), F32),
            ((8, 32, 128), F32), ((8, 16, 128), F32), ((17, 16, 128), F32),
            ((14, 16, 128), F32), ((14, 8, 128), F32), ((14, 16, 128), F32), ((14, 8, 128), F32),
            ((14, 32, 128), F32),
            ((4, 40, 128), F32),
            ((4, 16, 128), F32),
            ((2, 16, 128), F32), ((2, 16, 128), F32),
            ((7, 2, 16, 128), F32), ((7, 2, 16, 128), F32),
            ((28, 16, 128), F32), ((11, 8, 128), F32), ((10, 24, 128), F32),
            ((2, 8, 128), F32), ((2, 8, 128), F32),
            ((16, 2, 8, 128), F32), ((16, 2, 8, 128), F32),
            ((256, 128), BF16), ((128, 128), BF16), ((128, 128), BF16),
            ((256, 128), BF16), ((128, 128), BF16),
        )
    ]
    scratch += [pltpu.SemaphoreType.DMA((3,)), pltpu.SemaphoreType.REGULAR((5,))]
    for n in (16, len(NEAR), len(NEAR), len(WIDE), len(WIDE), 1, 1):
        scratch += [pltpu.SemaphoreType.DMA((n,)), pltpu.SemaphoreType.DMA((n,))]
    vmem = pl.BlockSpec(memory_space=pltpu.VMEM)
    hbm = pl.BlockSpec(memory_space=pl.ANY)
    fine, coarse = pl.pallas_call(
        kernel,
        out_shape=(
            jax.ShapeDtypeStruct((16, 32, 256), F32),
            jax.ShapeDtypeStruct((2, 32, 64), F32),
        ),
        in_specs=[hbm, hbm],
        out_specs=(hbm, vmem),
        scratch_shapes=scratch,
        compiler_params=pltpu.CompilerParams(
            collective_id=0, has_side_effects=True, vmem_limit_bytes=24 * 2**20
        ),
    )(pltpu.with_memory_space_constraint(right_side, pltpu.HBM), pltpu.with_memory_space_constraint(phase, pltpu.HBM))
    return fine, jnp.transpose(coarse, (0, 2, 1))


def solution(mesh):
    in_specs = (P("grp", "loc", None), P("grp", "loc", None))
    out_specs = (P("grp", "loc", None), P("grp", None, None))
    return jax.shard_map(
        per_device, mesh=mesh, in_specs=in_specs, out_specs=out_specs, check_vma=False
    )
```

```python
import functools

import jax
import jax.numpy as jnp
from jax import lax
from jax.experimental import pallas as pl
from jax.experimental.pallas import tpu as pltpu
from jax.sharding import PartitionSpec as P

MESH = pl.DeviceIdType.MESH
NG, NL = 16, 16
COARSE_SWEEPS = 4
F32 = jnp.float32
BF16 = jnp.bfloat16
WHOLE = ((256, 512, 256), (128, 256, 128), (64, 128, 64), (32, 64, 32))
BLOCK = ((16, 32, 256), (8, 16, 128), (4, 8, 64), (2, 64, 32))
LOW = (4, 4, 12, 5)
PLANES = (22, 14, 28, 11)
ROWS = (40, 32, 16, 16)
LANES = (256, 128, 128, 128)

NEAR = [(1, 1), (1, -1), (-1, 1), (-1, -1), (0, 1), (0, -1), (1, 0), (-1, 0)]
FACES = [(0, 1), (0, -1), (1, 0), (-1, 0)]
WIDE = [(a, 0) for a in (-3, 3, -2, 2, -1, 1)]
ALONG = [(0, k) for k in (10, 9, 11, 6, 5, 7, 14, 13, 2, 8, 3, 15, 12, 4, 1)]


def lane_ids(shape):
    return lax.broadcasted_iota(jnp.int32, shape, len(shape) - 1)


def row_ids(shape):
    return lax.broadcasted_iota(jnp.int32, shape, len(shape) - 2)


def split_dot(values, matrix):
    high = values.astype(BF16)
    rest = values - high.astype(F32)
    mid = rest.astype(BF16)
    low = (rest - mid.astype(F32)).astype(BF16)
    dot = functools.partial(jnp.dot, preferred_element_type=F32)
    return dot(high, matrix) + (dot(mid, matrix) + dot(low, matrix))


class Level:
    def __init__(self, index, g, l, refs):
        self.index = index
        self.F, self.C, self.U, self.V, self.Ei, self.Ej, self.El, self.K5, self.W = refs
        self.n = BLOCK[index]
        self.low = LOW[index]
        self.rows, self.lanes = ROWS[index], LANES[index]
        self.edges = index != 2
        self.g, self.l = g, l

    def up(self, x, axis):
        return pltpu.roll(x, x.shape[axis] - 1, axis)

    def down(self, x, axis):
        return pltpu.roll(x, 1, axis)

    def lane_up(self, x):
        y = self.up(x, x.ndim - 1)
        return jnp.where(self.at_end(y.shape), 0.0, y) if self.edges else y

    def lane_down(self, x):
        y = self.down(x, x.ndim - 1)
        return jnp.where(self.at_start(y.shape), 0.0, y) if self.edges else y

    def own_lane(self, shape):
        lane = lane_ids(shape)
        return lane & (self.n[2] - 1) if self.index == 3 else lane

    def at_start(self, shape):
        return self.own_lane(shape) == 0

    def at_end(self, shape):
        return self.own_lane(shape) == self.n[2] - 1

    def row_up(self, x):
        y = self.up(x, x.ndim - 2)
        if self.index < 3:
            return y
        tile = y[:, 8:16]
        after = jnp.where(lane_ids(tile.shape) < 96, pltpu.roll(tile, 96, 2), 0.0)
        return jnp.concatenate([y[:, 0:8], jnp.where(row_ids(tile.shape) == 7, after, tile)], 1)

    def row_down(self, x):
        y = self.down(x, x.ndim - 2)
        if self.index < 3:
            return y
        tile = y[:, 0:8]
        before = jnp.where(lane_ids(tile.shape) >= 32, pltpu.roll(tile, 32, 2), 0.0)
        return jnp.concatenate([jnp.where(row_ids(tile.shape) == 0, before, tile), y[:, 8:16]], 1)

    def row_valid(self, shape):
        r = row_ids(shape)
        if self.index == 3:
            return jnp.ones(shape, F32)
        ahead = self.n[1] + (4, 6, 4)[self.index]
        j = jnp.where(r < ahead, r, r - self.rows) + self.l * self.n[1]
        ok = (j >= 0) & (j < WHOLE[self.index][1])
        if self.n[2] < self.lanes:
            ok = ok & (lane_ids(shape) < self.n[2])
        return jnp.where(ok, 1.0, 0.0).astype(F32)

    def plane_valid(self, i):
        p = self.g * self.n[0] + (i - self.low)
        return jnp.where((p >= 0) & (p < WHOLE[self.index][0]), 1.0, 0.0).astype(F32)

    def plane_valid_many(self, lo, hi):
        shape = (hi - lo, self.rows, self.lanes)
        p = self.g * self.n[0] + (lo - self.low) + lax.broadcasted_iota(jnp.int32, shape, 0)
        return jnp.where((p >= 0) & (p < WHOLE[self.index][0]), 1.0, 0.0).astype(F32)

    def cells(self, c):
        cl = c + self.lane_down(c)
        cj = c + self.row_down(c)
        cjl = cl + self.row_down(cl)
        return cl, cj, cjl

    def coefficients(self, cells, before, valid):
        cl, cj, cjl = cells
        pl_, pj, pjl = before
        k = cjl + pjl
        el = cj + pj
        if self.edges:
            el = jnp.where(self.at_end(el.shape), 0.0, el)
        return cjl, cl + pl_, el, 5.0 * k, valid * (0.15 / jnp.maximum(k, 1.0))

    def parts(self, u):
        ul = self.lane_up(u)
        uj = self.row_up(u)
        a = u + ul
        return ul, uj, a + self.row_up(a)

    def combine(self, u, un, up, ul, uj, t, ei, eip, ej, el, k5):
        tj = t + self.row_down(t)
        b = k5 * u + ei * un + eip * up + ej * uj + el * ul - tj
        return b + self.lane_down(el * u - tj) + self.row_down(ej * u)

    def setup_all(self, lo, hi):
        cl, cj, cjl = self.cells(self.C[lo - 1:hi])
        valid = self.row_valid((1, self.rows, self.lanes)) * self.plane_valid_many(lo, hi)
        ei, ej, el, k5, w = self.coefficients(
            (cl[1:], cj[1:], cjl[1:]), (cl[:-1], cj[:-1], cjl[:-1]), valid
        )
        self.Ei[lo - 1:hi] = cjl
        self.Ej[lo:hi] = ej
        self.El[lo:hi] = el
        self.K5[lo:hi] = k5
        self.W[lo:hi] = w

    def apply_all(self, u_ref, lo, hi):
        u = u_ref[lo - 1:hi + 1]
        ul, uj, v = self.parts(u)
        t = self.C[lo - 1:hi] * (v[:-1] + v[1:])
        return self.combine(
            u[1:-1], u[2:], u[:-2], ul[1:-1], uj[1:-1], t[1:] + t[:-1],
            self.Ei[lo:hi], self.Ei[lo - 1:hi - 1], self.Ej[lo:hi], self.El[lo:hi], self.K5[lo:hi],
        )

    def first_all(self, lo, hi):
        self.U[lo:hi] = self.W[lo:hi] * self.F[lo:hi]

    def sweep_all(self, source, target, lo, hi):
        b = self.apply_all(source, lo, hi)
        target[lo:hi] = source[lo:hi] + self.W[lo:hi] * (self.F[lo:hi] - b)

    def residual_all(self, source, lo, hi):
        return self.F[lo:hi] - self.apply_all(source, lo, hi)

    def planes_loop(self, lo, hi, step, carry, unroll):
        whole = (hi - lo) // unroll

        def body(k, c):
            for m in range(unroll):
                c = step(lo + k * unroll + m, c)
            return c

        carry = lax.fori_loop(0, whole, body, carry)
        for i in range(lo + whole * unroll, hi):
            carry = step(i, carry)
        return carry

    def apply_loop(self, u_ref, lo, hi, emit, unroll):
        _, _, v0 = self.parts(u_ref[lo - 1])
        ul, uj, v = self.parts(u_ref[lo])
        t = self.C[lo - 1] * (v0 + v)

        def step(i, carry):
            ul, uj, v, t = carry
            u = u_ref[i]
            un = u_ref[i + 1]
            uln, ujn, vn = self.parts(un)
            tn = self.C[i] * (v + vn)
            b = self.combine(
                u, un, u_ref[i - 1], ul, uj, t + tn,
                self.Ei[i], self.Ei[i - 1], self.Ej[i], self.El[i], self.K5[i],
            )
            emit(i, u, b)
            return uln, ujn, vn, tn

        self.planes_loop(lo, hi, step, (ul, uj, v, t), unroll)


def kernel(*refs):
    rhs, phase, fine_out, coarse_out = refs[:4]
    refs = refs[4:]
    windows = [refs[9 * k:9 * k + 9] for k in range(4)]
    (
        ph, upk, dpk, rxl0, rxh0, rs, s0, out, ct1, n1, h0,
        rxl1, rxh1, crl1, crh1, c1w, s1, ct2, pf2, pn2, rf2, rn2, n2w, n3s, s2, pf3, pc3, rf3, rc3,
        r0_mat, r1_mat, r2_mat, p0_mat, p1_mat,
        lsem, known, ss0, rs0, sf1, qf1, sc1, qc1, sf2, qf2, sc2, qc2, sf3, qf3, sc3, qc3,
    ) = refs[36:]
    g = lax.axis_index("grp")
    l = lax.axis_index("loc")
    lv = [Level(k, g, l, windows[k]) for k in range(4)]
    L0, L1, L2, L3 = lv
    sent = []

    def device(dg, dl):
        return lax.rem(g + dg + NG, NG), lax.rem(l + dl + NL, NL)

    def inside(dg, dl):
        tests = [t for t in (
            g + dg >= 0 if dg < 0 else None, g + dg < NG if dg > 0 else None,
            l + dl >= 0 if dl < 0 else None, l + dl < NL if dl > 0 else None,
        ) if t is not None]
        return functools.reduce(jnp.logical_and, tests)

    def run(test, action):
        action() if test is None else pl.when(test)(action)

    class Sent:
        def __init__(self, src, dst, s_sem, r_sem, to, wrap):
            self.copy = pltpu.make_async_remote_copy(
                src_ref=src, dst_ref=dst, send_sem=s_sem, recv_sem=r_sem,
                device_id=device(*to), device_id_type=MESH,
            )
            self.out = None if wrap else inside(*to)
            self.back = None if wrap else inside(-to[0], -to[1])
            run(self.out, self.copy.start)
            sent.append(self)

        def wait_recv(self):
            run(self.back, self.copy.wait_recv)

        def wait_send(self):
            run(self.out, self.copy.wait_send)

    def send(src, dst, s_sem, r_sem, to, wrap=False):
        return Sent(src, dst, s_sem, r_sem, to, wrap)

    def flush(copies):
        for copy in copies:
            copy.wait_send()

    load_f = pltpu.make_async_copy(rhs, L0.F.at[4:20, 0:32], lsem.at[0])
    load_p = pltpu.make_async_copy(phase, ph, lsem.at[1])
    load_p.start()
    load_f.start()
    barrier = pltpu.get_barrier_semaphore()
    def greet(sem, targets):
        count = jnp.int32(0)
        for to in targets:
            test = inside(*to)

            def signal(to=to):
                pl.semaphore_signal(sem, inc=1, device_id=device(*to), device_id_type=MESH)

            run(test, signal)
            count = count + jnp.where(test, 1, 0)
        return count

    around = greet(barrier, FACES)

    def clear(test, *refs):
        @pl.when(test)
        def _():
            for ref in refs:
                ref[...] = jnp.zeros(ref.shape, F32)

    near_tiles = (rxl1, rxh1, crl1, crh1)
    clear(
        g == 0, L0.F.at[0:4, 0:32], L0.C.at[0:4, 0:32], L1.F.at[0:4, 0:16], L1.C.at[0:4, 0:16],
        *[x.at[0:4] for x in (rxl0, rxh0) + near_tiles],
    )
    clear(
        g == NG - 1, L0.F.at[20:22, 0:32], L0.C.at[20:22, 0:32], L1.F.at[12:14, 0:16], L1.C.at[12:14, 0:16],
        *[x.at[20:22] for x in (rxl0, rxh0)], *[x.at[12:14] for x in near_tiles],
    )
    clear(l == 0, rxl0, rxl1, crl1)
    clear(l == NL - 1, rxh0, rxh1, crh1)
    for d in (1, 2, 3):
        clear(g < d, rf2.at[3 - d], rn2.at[3 - d])
        clear(g >= NG - d, rf2.at[3 + d], rn2.at[3 + d])

    load_p.wait()
    gas = ph[...].astype(F32)
    L0.C[4:20, 0:32] = 1.0 + 999.0 * gas
    load_f.wait()
    sub = row_ids((1, 8, 256)) < 4
    upk[...] = jnp.where(sub, pltpu.roll(L0.C[4:20, 24:32], 4, 1), L0.F[4:20, 24:32])
    dpk[...] = jnp.where(sub, L0.F[4:20, 0:8], pltpu.roll(L0.C[4:20, 0:8], 4, 1))
    pl.semaphore_wait(barrier, around)

    first = []
    for src, dst, to in (
        (upk.at[0:4], rxl0.at[4:8], (0, 1)),
        (dpk.at[0:4], rxh0.at[4:8], (0, -1)),
        (L0.C.at[16:20, 0:32], L0.C.at[0:4, 0:32], (1, 0)),
        (L0.F.at[17:20, 0:32], L0.F.at[1:4, 0:32], (1, 0)),
        (L0.C.at[4:6, 0:32], L0.C.at[20:22, 0:32], (-1, 0)),
        (L0.F.at[4:6, 0:32], L0.F.at[20:22, 0:32], (-1, 0)),
        (upk.at[4:8], rxl0.at[8:12], (0, 1)),
        (dpk.at[4:8], rxh0.at[8:12], (0, -1)),
        (upk.at[8:12], rxl0.at[12:16], (0, 1)),
        (dpk.at[8:12], rxh0.at[12:16], (0, -1)),
        (upk.at[12:16], rxl0.at[16:20], (0, 1)),
        (dpk.at[12:16], rxh0.at[16:20], (0, -1)),
    ):
        first.append(send(src, dst, ss0.at[len(first)], rs0.at[len(first)], to))

    def near_sends(ref, low, high, ssem, rsem, depth):
        copies = []
        for k, (dg, dl) in enumerate(NEAR):
            lo, hi, at = {1: (12 - depth, 12, 4 - depth), 0: (4, 12, 4), -1: (4, 6, 12)}[dg]
            rows, target = {1: (slice(0, 16), low), 0: (slice(0, 16), ref), -1: (slice(0, 8), high)}[dl]
            where = pl.ds(at, hi - lo)
            dst = target.at[where, 0:16] if dl == 0 else target.at[where]
            copies.append(send(ref.at[lo:hi, rows], dst, ssem.at[k], rsem.at[k], (dg, dl)))
        return copies

    def wide_sends(src, slots, ssem, rsem):
        return [
            send(src, slots.at[3 - dg], ssem.at[k], rsem.at[k], (dg, dl))
            for k, (dg, dl) in enumerate(WIDE)
        ]

    def along_sends(src, slots, ssem, rsem):
        for to in ALONG:
            pltpu.make_async_remote_copy(
                src_ref=src, dst_ref=slots.at[l], send_sem=ssem.at[0], recv_sem=rsem.at[0],
                device_id=device(*to), device_id_type=MESH,
            ).start()
        whole = slots.at[0:NL - 1]
        return [pltpu.make_async_copy(whole, whole, sem.at[0]) for sem in (rsem, ssem)]

    greet(known.at[0], FACES)

    weights = ((r0_mat, 256), (r1_mat, 128), (r2_mat, 64))
    for ref, used in weights:
        k, c = row_ids(ref.shape), lane_ids(ref.shape)
        near = jnp.abs(k - 2 * c)
        live = (k < used) & (c < used // 2)
        ref[...] = jnp.where(
            live & (near == 0), 0.5, jnp.where(live & (near == 1), 0.25, 0.0)
        ).astype(BF16)
    for ref in (p0_mat, p1_mat):
        half = row_ids(ref.shape) - 2 * lane_ids(ref.shape)
        ref[...] = jnp.where((half == 0) | (half == 1), 1.0, 0.0).astype(BF16)

    pairs = jnp.concatenate([gas[2 * i:2 * i + 1] + gas[2 * i + 1:2 * i + 2] for i in range(8)], 0)
    ct1[...] = jnp.dot(
        pairs.reshape(8 * 32, 256).astype(BF16), p0_mat[...], preferred_element_type=F32
    ).reshape(8, 32, 128)
    n1[...] = ct1[:, pl.ds(0, 16, stride=2), :] + ct1[:, pl.ds(1, 16, stride=2), :]
    count1 = n1[...]
    L1.C[4:12, 0:16] = count1
    pl.semaphore_wait(known.at[0], around)
    for src, dst, to in (
        (upk.at[12:16], rxl0.at[0:4], (1, 1)),
        (dpk.at[12:16], rxh0.at[0:4], (1, -1)),
        (upk.at[0:2], rxl0.at[20:22], (-1, 1)),
        (dpk.at[0:2], rxh0.at[20:22], (-1, -1)),
    ):
        first.append(send(src, dst, ss0.at[len(first)], rs0.at[len(first)], to))
    known_1 = greet(known.at[1], [(-1, 0), (1, 0)])
    known_2 = greet(known.at[2], [(0, -2), (0, 2)])

    rows0 = L0.row_valid((40, 256))
    sub = row_ids((8, 256)) < 4

    def merge(i, _):
        low, high = rxl0[i], rxh0[i]
        L0.F[i, 32:40] = jnp.where(sub, high, low)
        L0.C[i, 32:40] = pltpu.roll(jnp.where(sub, low, high), 4, 0) * rows0[32:40] * L0.plane_valid(i)
        return 0

    def setup(i, before):
        cells = L0.cells(L0.C[i])
        ei, ej, el, k5, w = L0.coefficients(cells, before, rows0 * L0.plane_valid(i))
        L0.Ei[i], L0.Ej[i], L0.El[i], L0.K5[i], L0.W[i] = ei, ej, el, k5, w
        L0.U[i] = w * (12.0 * L0.F[i])
        return cells

    def second(i, u, b):
        L0.V[i] = u + L0.W[i] * (12.0 * L0.F[i] - b)

    def residual(i, u, b):
        r = (12.0 * L0.F[i] - b) * (rows0 * L0.plane_valid(i))
        for half in range(2):
            lanes = slice(128 * half, 128 * half + 128)
            rs[i - 3, half, 0:8] = r[32:40, lanes]
            rs[i - 3, half, 8:40] = r[0:32, lanes]
        out[jnp.maximum(i - 4, 0)] = r[0:32] * (1.0 / 12.0)

    def setup_planes(lo, hi):
        before = L0.cells(L0.C[lo - 1])
        L0.Ei[lo - 1] = before[2]
        L0.planes_loop(lo, hi, setup, before, 8)

    for copy in first[0:2]:
        copy.wait_recv()
    lax.fori_loop(4, 8, merge, 0)
    setup_planes(5, 8)
    L0.apply_loop(L0.U, 6, 7, second, 8)
    for copy in first[6:8]:
        copy.wait_recv()
    lax.fori_loop(8, 12, merge, 0)
    setup_planes(8, 12)
    L0.apply_loop(L0.U, 7, 11, second, 8)
    for copy in first[8:10]:
        copy.wait_recv()
    lax.fori_loop(12, 16, merge, 0)
    setup_planes(12, 16)
    L0.apply_loop(L0.U, 11, 15, second, 8)
    for copy in first[10:12]:
        copy.wait_recv()
    lax.fori_loop(16, 20, merge, 0)
    setup_planes(16, 20)
    L0.apply_loop(L0.U, 15, 19, second, 8)
    L0.apply_loop(L0.V, 7, 18, residual, 6)
    got_c1 = near_sends(L1.C, crl1, crh1, sc1, qc1, 4)
    for copy in first[2:6] + first[12:]:
        copy.wait_recv()
    for i in (0, 1, 2, 3, 20, 21):
        merge(i, 0)
        L0.C[i, 0:32] = L0.C[i, 0:32] * L0.plane_valid(i)
    setup_planes(1, 5)
    setup_planes(20, 22)
    L0.apply_loop(L0.U, 2, 6, second, 4)
    L0.apply_loop(L0.U, 19, 21, second, 4)
    L0.apply_loop(L0.V, 3, 7, residual, 4)
    L0.apply_loop(L0.V, 18, 20, residual, 4)
    store = pltpu.make_async_copy(out, fine_out, lsem.at[2])

    def coarser_planes(r):
        return [0.5 * (r[2 * i] + r[2 * i + 2]) + r[2 * i + 1] for i in range((r.shape[0] - 1) // 2)]

    def coarser_rows(ref, kept):
        return 0.5 * (
            ref[:, pl.ds(7, kept, stride=2), :] + ref[:, pl.ds(9, kept, stride=2), :]
        ) + ref[:, pl.ds(8, kept, stride=2), :]

    total = jnp.zeros((8 * 16, 128), F32)
    for half in range(2):
        for i, plane in enumerate(coarser_planes(rs[:, half])):
            s0[half, i] = plane
        total = total + split_dot(
            coarser_rows(s0.at[half], 16).reshape(8 * 16, 128), r0_mat[128 * half:128 * half + 128]
        )
    L1.F[4:12, 0:16] = total.reshape(8, 16, 128)
    earlier, sent[:] = sent[:], []
    got_f1 = near_sends(L1.F, rxl1, rxh1, sf1, qf1, 3)
    store.start()

    pl.semaphore_wait(known.at[1], known_1)
    pl.semaphore_wait(known.at[2], known_2)
    known_3 = greet(known.at[3], [(0, -4), (0, 4)])

    for copy in got_c1:
        copy.wait_recv()
    def merge_rows(ref, low, high, lo, hi):
        inner = row_ids((1, 8, 128)) < 6
        ref[lo:hi, 16:24] = jnp.where(inner, high[lo:hi], low[lo:hi, 0:8])
        ref[lo:hi, 24:32] = low[lo:hi, 8:16]

    merge_rows(L1.C, crl1, crh1, 0, 14)
    for i in range(4):
        s1[i, 0:32] = L1.C[2 * i + 4] + L1.C[2 * i + 5]
    pairs = s1[:, pl.ds(0, 16, stride=2), :] + s1[:, pl.ds(1, 16, stride=2), :]
    count2 = jnp.dot(
        pairs.reshape(4 * 16, 128).astype(BF16), p1_mat[...], preferred_element_type=F32
    ).reshape(4, 16, 128)
    pn2[...] = count2[0:2] + pltpu.roll(count2[2:4], 64, 2)
    rn2[3] = pn2[...]
    got_c2 = wide_sends(pn2, rn2, sc2, qc2)
    valid1 = L1.row_valid((1, 32, 128)) * L1.plane_valid_many(0, 14)
    c1w[...] = (1.0 + 124.875 * L1.C[...]) * valid1
    L1.C = c1w
    L1.setup_all(1, 14)

    flush(earlier)
    pl.semaphore_wait(known.at[3], known_3)
    known_4 = greet(known.at[4], [(0, -8), (0, 8)])

    for copy in got_f1:
        copy.wait_recv()
    merge_rows(L1.F, rxl1, rxh1, 1, 14)
    L1.first_all(1, 14)
    L1.sweep_all(L1.U, L1.V, 2, 13)
    r1 = L1.residual_all(L1.V, 3, 12) * valid1[3:12]
    for i, plane in enumerate(coarser_planes(r1)):
        s1[i, 0:8] = plane[24:32]
        s1[i, 8:40] = plane
    f2 = split_dot(coarser_rows(s1, 16).reshape(4 * 16, 128), r1_mat[...]).reshape(4, 16, 128)
    pf2[...] = f2[0:2] + pltpu.roll(f2[2:4], 64, 2)
    earlier, sent[:] = sent[:], []
    got_f2 = wide_sends(pf2, rf2, sf2, qf2)
    rf2[3] = pf2[...]

    pl.semaphore_wait(known.at[4], known_4)

    def unpack_wide(slots, ref):
        lane = lane_ids((1, 1, 1, 128)) < 64
        tiles = slots[...]
        first = jnp.where(lane, tiles, 0.0)
        later = jnp.where(lane, pltpu.roll(tiles, 64, 3), 0.0)
        for d in range(7):
            ref[4 * d:4 * d + 2] = first[d]
            ref[4 * d + 2:4 * d + 4] = later[d]

    for copy in got_c2:
        copy.wait_recv()

    unpack_wide(rn2, n2w)
    valid2 = L2.row_valid((1, 16, 128)) * L2.plane_valid_many(0, 28)
    L2.C[...] = (1.0 + (999.0 / 64.0) * n2w[...]) * valid2
    L2.setup_all(1, 26)

    count2 = n2w[2:24, 0:8]
    pairs = jnp.concatenate([count2[2 * i:2 * i + 1] + count2[2 * i + 1:2 * i + 2] for i in range(11)], 0)
    n3s[...] = jnp.dot(
        pairs.reshape(11 * 8, 128).astype(BF16), p1_mat[...], preferred_element_type=F32
    ).reshape(11, 8, 128)
    count3 = n3s[:, pl.ds(0, 4, stride=2), :] + n3s[:, pl.ds(1, 4, stride=2), :]

    def pack(planes, ref):
        for t in range(2):
            for h in range(2):
                total = jnp.zeros((4, 128), F32)
                for q in range(4):
                    p = 8 * t + 4 * h + q
                    if p < len(planes):
                        total = total + (pltpu.roll(planes[p], 32 * q, 1) if q else planes[p])
                ref[t, 4 * h:4 * h + 4] = total
        tiles = ref[...]
        tiles = jnp.where(lax.rem(l, 2) == 1, pltpu.roll(tiles, 4, 1), tiles)
        tiles = jnp.where(lax.rem(lax.div(l, 4), 2) == 1, pltpu.roll(tiles, 32, 2), tiles)
        ref[...] = jnp.where(l >= 8, pltpu.roll(tiles, 64, 2), tiles)

    def unpack_along(slots, count, put):
        half, group = row_ids((8, 128)) // 4, lane_ids((8, 128)) // 32
        cell = [[(half == h) & (group == q) for q in range(4)] for h in range(2)]
        for p in range(count):
            t, h, q = p // 8, (p % 8) // 4, p % 4
            for tile in range(2):
                total = slots[2 * tile, t]
                for owner in range(1, 8):
                    e, o = owner % 2, owner // 2
                    total = jnp.where(cell[(h + e) % 2][(q + o) % 4], slots[4 * o + 2 * tile + e, t], total)
                if h:
                    total = pltpu.roll(total, 4, 0)
                if q:
                    total = pltpu.roll(total, 128 - 32 * q, 1)
                put(p, slice(8 * tile, 8 * tile + 8), total)

    pack([count3[i] for i in range(11)], pc3)
    rc3[l] = pc3[...]
    got_c3 = along_sends(pc3, rc3, sc3, qc3)
    flush(earlier)

    for copy in got_f2:
        copy.wait_recv()

    unpack_wide(rf2, L2.F)
    L2.first_all(1, 26)
    L2.sweep_all(L2.U, L2.V, 2, 25)
    r2 = L2.residual_all(L2.V, 3, 24) * valid2[3:24]
    for i, plane in enumerate(coarser_planes(r2)):
        s2[i, 0:8] = plane[8:16]
        s2[i, 8:24] = plane
    f3 = split_dot(coarser_rows(s2, 8).reshape(10 * 8, 128), r2_mat[...]).reshape(10, 8, 128)
    pack([f3[i, 0:4] for i in range(10)], pf3)
    earlier = sent[:]
    got_f3 = along_sends(pf3, rf3, sf3, qf3)
    rf3[l] = pf3[...]

    flush(earlier)
    got_c3[0].wait()

    def put_c3(p, rows, value):
        L3.C[p, rows] = (1.0 + (999.0 / 512.0) * value) * L3.plane_valid(p)

    unpack_along(rc3, 11, put_c3)
    L3.setup_all(1, 11)

    got_f3[0].wait()

    def put_f3(p, rows, value):
        L3.F[p + 1, rows] = value

    unpack_along(rf3, 10, put_f3)
    L3.first_all(1, 11)
    source, target = L3.U, L3.V
    for sweep in range(COARSE_SWEEPS - 1):
        L3.sweep_all(source, target, 2 + sweep, 10 - sweep)
        source, target = target, source
    last = (8.0 / 12.0) * L3.residual_all(source, 5, 7)
    for i in range(2):
        turned = jnp.transpose(last[i], (1, 0))
        coarse_out[i] = jnp.concatenate([turned[32 * q:32 * q + 32] for q in range(4)], 1)

    store.wait()
    got_c3[1].wait()
    got_f3[1].wait()


def per_device(right_side, phase):
    scratch = []
    for k in range(4):
        shape = (PLANES[k], ROWS[k], LANES[k])
        scratch += [pltpu.VMEM(shape, F32) for _ in range(9)]
    scratch += [
        pltpu.VMEM(s, d)
        for s, d in (
            ((16, 32, 256), jnp.int32),
            ((16, 8, 256), F32), ((16, 8, 256), F32),
            ((22, 8, 256), F32), ((22, 8, 256), F32),
            ((17, 2, 40, 128), F32), ((2, 8, 40, 128), F32),
            ((16, 32, 256), F32),
            ((8, 32, 128), F32), ((8, 16, 128), F32), ((17, 16, 128), F32),
            ((14, 16, 128), F32), ((14, 8, 128), F32), ((14, 16, 128), F32), ((14, 8, 128), F32),
            ((14, 32, 128), F32),
            ((4, 40, 128), F32),
            ((4, 16, 128), F32),
            ((2, 16, 128), F32), ((2, 16, 128), F32),
            ((7, 2, 16, 128), F32), ((7, 2, 16, 128), F32),
            ((28, 16, 128), F32), ((11, 8, 128), F32), ((10, 24, 128), F32),
            ((2, 8, 128), F32), ((2, 8, 128), F32),
            ((16, 2, 8, 128), F32), ((16, 2, 8, 128), F32),
            ((256, 128), BF16), ((128, 128), BF16), ((128, 128), BF16),
            ((256, 128), BF16), ((128, 128), BF16),
        )
    ]
    scratch += [pltpu.SemaphoreType.DMA((3,)), pltpu.SemaphoreType.REGULAR((5,))]
    for n in (16, len(NEAR), len(NEAR), len(WIDE), len(WIDE), 1, 1):
        scratch += [pltpu.SemaphoreType.DMA((n,)), pltpu.SemaphoreType.DMA((n,))]
    vmem = pl.BlockSpec(memory_space=pltpu.VMEM)
    hbm = pl.BlockSpec(memory_space=pl.ANY)
    fine, coarse = pl.pallas_call(
        kernel,
        out_shape=(
            jax.ShapeDtypeStruct((16, 32, 256), F32),
            jax.ShapeDtypeStruct((2, 32, 64), F32),
        ),
        in_specs=[hbm, hbm],
        out_specs=(hbm, vmem),
        scratch_shapes=scratch,
        compiler_params=pltpu.CompilerParams(
            collective_id=0, has_side_effects=True, vmem_limit_bytes=24 * 2**20
        ),
    )(pltpu.with_memory_space_constraint(right_side, pltpu.HBM), pltpu.with_memory_space_constraint(phase, pltpu.HBM))
    return fine, jnp.transpose(coarse, (0, 2, 1))


def solution(mesh):
    in_specs = (P("grp", "loc", None), P("grp", "loc", None))
    out_specs = (P("grp", "loc", None), P("grp", None, None))
    return jax.shard_map(
        per_device, mesh=mesh, in_specs=in_specs, out_specs=out_specs, check_vma=False
    )
```
